32 devices in a mesh: fsdp: 16 (over z, x, core), tp: 2 (over y).
Axes of the slice: x: 2, y: 2, z: 4, core: 2. Of those that a mesh axis runs over, the one named last changes fastest.
Arguments:
- inputs: bfloat16 [16384, 768], P(('fsdp', 'tp')), may hold values from -12 to 12
- token_ids: int32 [16384], P('fsdp'), may hold values from 0 to 50303, as said below
- hash_table: int32 [50304], replicated, may hold values from 0 to 15, as said below
- segment_lengths: int32 [16, 13], P('fsdp'), may hold values from 1 to 256, 1024 in all within a row
- segment_parents: int32 [16, 13], P('fsdp'), may hold values from 0 to 11, as said below
- first_gain: float32 [768], replicated, may hold values from 0.5 to 1.5
- first_bias: float32 [768], replicated, may hold values from -1.25 to 1.25
- input_weight: bfloat16 [3, 768, 768], P(None, 'fsdp', 'tp'), may hold values from -0.21875 to 0.21875
- output_weight: bfloat16 [768, 768], P('tp', 'fsdp'), may hold values from -0.875 to 0.875
- second_gain: float32 [768], replicated, may hold values from 0.5 to 1.5
- second_bias: float32 [768], replicated, may hold values from -1.25 to 1.25
- expert_in: bfloat16 [16, 768, 3072], P('fsdp', None, 'tp'), may hold values from -0.21875 to 0.21875
- expert_out: bfloat16 [16, 3072, 768], P('fsdp', 'tp'), may hold values from -0.109375 to 0.109375
- cotangent: bfloat16 [16384, 768], P(('fsdp', 'tp')), may hold values from -12 to 12
Outputs:
- out_block: bfloat16 [16384, 768], P(('fsdp', 'tp'))
- input_grad: float32 [16384, 768], P(('fsdp', 'tp'))
- first_gain_grad: float32 [768], replicated
- first_bias_grad: float32 [768], replicated
- input_weight_grad: float32 [3, 768, 768], P(None, 'fsdp', 'tp')
- output_weight_grad: float32 [768, 768], P('tp', 'fsdp')
- second_gain_grad: float32 [768], replicated
- second_bias_grad: float32 [768], replicated
- expert_in_grad: float32 [16, 768, 3072], P('fsdp', None, 'tp')
- expert_out_grad: float32 [16, 3072, 768], P('fsdp', 'tp')
The draws below stay inside these ranges and needn't reach their ends.
Inputs may be any that keep to these rules, and one draw needn't show every extreme that they name: `token_ids`: in each aligned block of 512 rows at most 64 tokens hash through hash_table to one expert, and in every block 1 expert take exactly 64. `hash_table`: every expert is the value of exactly 3144 entries. `segment_lengths`: the 13 lengths of a tree sum to 1024. `segment_parents`: segment 0 is its own parent; any other segment's parent is a smaller segment number.
All inputs are finite; a program needn't handle non-finite values.
Results may differ from the reference program's by a relative error of at most 0.011.
Values may be sent and summed in bfloat16 or wider, within the bound.
No kernel may reach another device: no remote copies, remote signals or barrier semaphores. Data moves between devices by JAX's collectives and lax.ppermute only.
A program may use at most 192 MiB of HBM per device.

```python
import math
import jax
import jax.numpy as jnp
import numpy as np
from jax import lax

D = 768
H = 12
HD = 64
FF = 3072
VOCAB = 50304
TREE = 1024
NSEG = 13
TREES = 16
TOKENS = 16384
EXPERTS = 16
HALF = 512
CAP = 64
HOT = 1
N_FSDP = 16
N_TP = 2


def route_tables(key):
    return jax.random.permutation(jax.random.fold_in(key, 101), VOCAB)


def draw_hash_table(key, part):
    return (route_tables(key) % EXPERTS).astype(jnp.int32)


def draw_token_ids(key, part):
    shuffled = route_tables(key)
    inverse = jnp.argsort(shuffled, stable=True).astype(jnp.int32)
    favoured = jax.random.permutation(jax.random.fold_in(key, 102), EXPERTS)[:HOT]
    heat = jnp.zeros((EXPERTS,), jnp.int32).at[favoured].set(1)
    slot_total = EXPERTS * CAP
    slot_expert = jnp.arange(slot_total, dtype=jnp.int32) // CAP

    def one_block(block):
        block_key = jax.random.fold_in(jax.random.fold_in(key, 103), block)
        keys_three = jax.random.split(block_key, 3)
        priority = jax.random.randint(keys_three[0], (slot_total,), 0, 2 ** 14) * slot_total
        priority = priority + jnp.arange(slot_total, dtype=jnp.int32) + jnp.take(heat, slot_expert) * (2 ** 14 * slot_total)
        chosen = lax.top_k(priority, HALF)[1]
        experts = jnp.take(slot_expert, chosen)
        experts = jnp.take(experts, jax.random.permutation(keys_three[1], HALF))
        within = jax.random.randint(keys_three[2], (HALF,), 0, VOCAB // EXPERTS)
        return jnp.take(inverse, experts + EXPERTS * within)
    return jax.vmap(one_block)(jnp.arange(TOKENS // HALF)).reshape(TOKENS).astype(jnp.int32)


def draw_segment_parents(key, part):
    limits = jnp.maximum(jnp.arange(NSEG, dtype=jnp.int32), 1)
    raw = jax.random.randint(jax.random.fold_in(key, 104), (TREES, NSEG), 0, limits)
    return raw.astype(jnp.int32)


def strengthened(drawn, rng, source, target, blocks, factor):
    owner, partner = [(jnp.arange(drawn.shape[axis_at]) // (drawn.shape[axis_at] // blocks)).reshape([-1 if axis == axis_at else 1 for axis in range(drawn.ndim)]) for axis_at in (source, target)]
    chosen = jax.random.permutation(rng, blocks)[partner]
    strong = (owner == chosen) | (owner == (partner + blocks // 2) % blocks)
    return jnp.where(strong, factor * drawn, drawn)


def shard_levels(rng, dims, cuts, smallest, high):
    def one(dim, shards_of):
        draws = jax.random.uniform(jax.random.fold_in(jax.random.fold_in(rng, 6), dim), (shards_of,), jnp.float32, smallest / len(cuts), high / len(cuts))
        return jnp.repeat(jnp.exp(draws), dims[dim] // shards_of).reshape((-1,) + (1,) * (len(dims) - dim - 1))

    level = one(*cuts[0])
    for cut in cuts[1:]:
        level = level * one(*cut)
    return level


def split_up(number_of, total, reach, slope):
    loads = [(1 << 20) // math.isqrt(standing ** slope) + 1 for standing in range(2, number_of + 1)]
    surplus, given = total - reach - (number_of - 1), [1] * (number_of - 1)
    while surplus > 0:
        free = [i for i in range(number_of - 1) if given[i] < reach]
        mass, remaining = sum([loads[i] for i in free]), surplus
        for i in free:
            extra = min(reach - given[i], max(1, remaining * loads[i] // mass), surplus)
            given[i] = given[i] + extra
            surplus = surplus - extra
    return np.array([reach] + given)


def uneven(own_key, number_of, total, most, slope):
    if number_of == 2:
        one = jax.random.randint(own_key, (), max(1, total - most), min(most, total - 1) + 1)
        return jnp.stack([one, total - one])
    tallies = jnp.asarray(split_up(number_of, total, most, slope), jnp.int32)
    twos = (number_of - 1) // 2
    donor, receiver = tallies[1:1 + 2 * twos:2], tallies[2:2 + 2 * twos:2]
    margin = jnp.minimum(donor - 1, most - receiver)
    shifted = jax.random.randint(jax.random.fold_in(own_key, 1), (twos,), 0, 1 << 20) % (margin + 1)
    tallies = tallies.at[1:1 + 2 * twos:2].set(donor - shifted).at[2:2 + 2 * twos:2].set(receiver + shifted)
    return tallies[jax.random.permutation(jax.random.fold_in(own_key, 2), number_of)]


def noise(stream_key, dims, scale, limit, cuts=(), kind=jnp.bfloat16):
    loudness = shard_levels(stream_key, dims, cuts, -0.22, 0.18) if cuts else 1.0
    array = jax.random.normal(stream_key, dims, jnp.float32) * scale * loudness
    return jnp.minimum(jnp.maximum(array, -limit), limit).astype(kind)


def gaussian_with(key, dims, deviation, most, cuts, heavy, kind=jnp.bfloat16):
    entries = deviation * jax.random.normal(key, dims, jnp.float32)
    if cuts:
        entries = entries * shard_levels(key, dims, cuts, -0.22, 0.18)
    return jnp.clip(strengthened(entries, jax.random.fold_in(key, 3), *heavy), -most, most).astype(kind)


def setup_inputs(seed: int = 0) -> dict:
    key_list = jax.random.split(jax.random.key(seed), 15)
    inputs = gaussian_with(key_list[0], (TOKENS, D), 1.0, 12.0, ((0, 32),), (0, 1, 32, 2.75))
    token_ids = draw_token_ids(jax.random.fold_in(key_list[14], 71), 0)
    hash_table = draw_hash_table(jax.random.fold_in(key_list[14], 71), 0)
    segment_lengths = jax.vmap(lambda own: uneven(own, NSEG, TREE, TREE // 4, 2))(jax.random.split(key_list[3], TREES)).reshape((TREES, NSEG)).astype(jnp.int32)
    segment_parents = draw_segment_parents(jax.random.fold_in(key_list[14], 71), 0)
    first_gain = jnp.clip(1.0 + 0.1 * jax.random.normal(key_list[5], (D,), jnp.float32), 0.5, 1.5)
    first_bias = noise(key_list[6], (D,), 0.2, 1.25, (), jnp.float32)
    input_weight = noise(key_list[7], (3, D, D), D ** -0.5, 0.21875, ((1, 16), (2, 2)))
    output_weight = noise(key_list[8], (D, D), (D // 16) ** -0.5, 0.875, ((0, 2), (1, 16)))
    second_gain = jnp.clip(1.0 + 0.1 * jax.random.normal(key_list[9], (D,), jnp.float32), 0.5, 1.5)
    second_bias = noise(key_list[10], (D,), 0.2, 1.25, (), jnp.float32)
    expert_in = noise(key_list[11], (EXPERTS, D, FF), D ** -0.5, 0.21875, ((0, 16), (2, 2)))
    expert_out = noise(key_list[12], (EXPERTS, FF, D), FF ** -0.5, 0.109375, ((0, 16), (1, 2)))
    cotangent = gaussian_with(key_list[13], (TOKENS, D), 1.0, 12.0, ((0, 32),), (0, 1, 32, 2.75))
    return dict(inputs=inputs, token_ids=token_ids, hash_table=hash_table, segment_lengths=segment_lengths, segment_parents=segment_parents, first_gain=first_gain, first_bias=first_bias, input_weight=input_weight, output_weight=output_weight, second_gain=second_gain, second_bias=second_bias, expert_in=expert_in, expert_out=expert_out, cotangent=cotangent)


@jax.custom_vjp
def low(v):
    return lax.optimization_barrier(v.astype(jnp.bfloat16)).astype(jnp.float32)

@jax.custom_vjp
def low_back(v):
    return v

def low_keep(v):
    return (low(v), None)

def low_pass(kept, grad):
    return (grad,)

def back_keep(v):
    return (v, None)

def back_low(kept, grad):
    return (low(grad),)
low.defvjp(low_keep, low_pass)
low_back.defvjp(back_keep, back_low)
highest = lax.Precision.HIGHEST
norm_eps = 1e-05
gelu_root = 0.7978845608028654
gelu_cubic = 0.044715

def gelu_tanh(values):
    return 0.5 * values * (1.0 + jnp.tanh(gelu_root * (values + gelu_cubic * values * values * values)))

def layer_norm(values, gain, shift):
    average = lax.optimization_barrier(jnp.mean(values, axis=-1, keepdims=True))
    centred = values - average
    variance = lax.optimization_barrier(jnp.mean(centred * centred, axis=-1, keepdims=True))
    return centred * lax.rsqrt(variance + norm_eps) * gain + shift

def segment_reach(lengths, parents, tree_size):
    segment_count = lengths.shape[0]
    lengths_int = lengths.astype(jnp.int32)
    segment_end = jnp.cumsum(lengths_int, dtype=jnp.int32).astype(jnp.int32)
    starts = (segment_end - lengths_int).astype(jnp.int32)
    position = jnp.arange(tree_size, dtype=jnp.int32)
    member = ((position[:, None] >= starts[None, :]) & (position[:, None] < segment_end[None, :])).astype(jnp.float32)
    parent_table = (parents.astype(jnp.int32)[:, None] == jnp.arange(segment_count, dtype=jnp.int32)[None, :]).astype(jnp.float32)
    identity = jnp.eye(segment_count, dtype=jnp.float32)
    closure = identity
    for counter in range(segment_count):
        closure = jnp.maximum(identity, jnp.dot(parent_table, closure, precision=highest))
    reachable = jnp.dot(member, closure, precision=highest)
    return (reachable, member)

def visible(lengths, parents):
    reachable, member = segment_reach(lengths, parents, TREE)
    path_seen = jnp.dot(reachable, member.T, precision=highest)
    place = jnp.arange(TREE, dtype=jnp.int32)
    return (path_seen > 0.5) & (place[None, :] <= place[:, None])

def tree_attention(normed, weight, lengths, parents):
    projected = low_back(low(jnp.einsum('td,kde->kte', normed, weight, precision=highest)))
    per_head = projected.reshape(3, TREE, H, HD)
    scores = low_back(jnp.einsum('qhc,khc->hqk', per_head[0], per_head[1], precision=highest) * (1.0 / math.sqrt(HD)))
    scores = jnp.where(visible(lengths, parents)[None], scores, -1e+30)
    row_max = lax.optimization_barrier(jnp.max(scores, axis=-1, keepdims=True))
    weights = jnp.exp(scores - row_max)
    softmax_weights = weights / lax.optimization_barrier(jnp.sum(weights, axis=-1, keepdims=True))
    attended = jnp.einsum('hqk,khc->qhc', low(softmax_weights), per_head[2], precision=highest)
    return low_back(low(attended)).reshape(TREE, D)

def reference(inputs, token_ids, hash_table, segment_lengths, segment_parents, first_gain, first_bias, input_weight, output_weight, second_gain, second_bias, expert_in, expert_out, cotangent):
    expert_of = jnp.take(hash_table, token_ids.astype(jnp.int32)).astype(jnp.int32)
    slot_limit = N_FSDP * N_TP * CAP
    onehot = (expert_of[:, None] == jnp.arange(EXPERTS, dtype=jnp.int32)[None, :]).astype(jnp.int32)
    before = (jnp.cumsum(onehot, axis=0, dtype=jnp.int32) - onehot).astype(jnp.int32)
    rank_within = lax.optimization_barrier(jnp.sum(before * onehot, axis=1, dtype=jnp.int32)).astype(jnp.int32)
    flat_place = (expert_of * slot_limit + rank_within).astype(jnp.int32)
    token_place = jnp.arange(TOKENS, dtype=jnp.int32)
    slot_index = jnp.zeros((EXPERTS * slot_limit,), jnp.int32).at[flat_place].set(token_place).reshape(EXPERTS, slot_limit)
    slot_valid = jnp.zeros((EXPERTS * slot_limit,), jnp.float32).at[flat_place].set(1.0).reshape(EXPERTS, slot_limit)

    def forward(residual, gain_first, bias_first, weight_qkv, weight_final, gain_second, bias_second, weight_up, weight_down):
        normed = low(layer_norm(residual, gain_first, bias_first))

        def one_tree(pieces):
            return tree_attention(pieces[0], weight_qkv, pieces[1], pieces[2])
        attended = lax.map(jax.checkpoint(one_tree), (normed.reshape(TREES, TREE, D), segment_lengths, segment_parents))
        branch = low_back(jnp.dot(attended.reshape(TOKENS, D), weight_final, precision=highest))
        middle = residual + branch
        second = low(layer_norm(middle, gain_second, bias_second))

        def one_expert(pieces):
            positions, validity, weight_in, weight_out = pieces
            picked = jnp.take(second, positions, axis=0) * validity[:, None]
            hidden_pre = low_back(jnp.dot(picked, weight_in, precision=highest))
            active = low(gelu_tanh(hidden_pre))
            return jnp.dot(active, weight_out, precision=highest) * validity[:, None]
        slot_out = lax.map(jax.checkpoint(one_expert), (slot_index, slot_valid, weight_up, weight_down))
        ffn = jnp.zeros((TOKENS, D), jnp.float32).at[slot_index.reshape(-1)].add(slot_out.reshape(-1, D))
        return middle + low_back(ffn)
    result, pullback = jax.vjp(forward, inputs.astype(jnp.float32), first_gain.astype(jnp.float32), first_bias.astype(jnp.float32), input_weight.astype(jnp.float32), output_weight.astype(jnp.float32), second_gain.astype(jnp.float32), second_bias.astype(jnp.float32), expert_in.astype(jnp.float32), expert_out.astype(jnp.float32))
    gradients = pullback(cotangent.astype(jnp.float32))
    return (result.astype(jnp.bfloat16), gradients[0], gradients[1], gradients[2], gradients[3], gradients[4], gradients[5], gradients[6], gradients[7], gradients[8])
```

```python
import math

import jax
import jax.numpy as jnp
from jax import lax
from jax.sharding import PartitionSpec as P

HD = 64


norm_eps = 1e-05
masked_score = -1e30
highest = lax.Precision.HIGHEST
gelu_root = 0.7978845608028654
gelu_cubic = 0.044715
low = jnp.bfloat16
wide = jnp.float32


def gelu_both(values):
    squared = values * values
    tangent = jnp.tanh(gelu_root * values * (1.0 + gelu_cubic * squared))
    half_up = 0.5 * (1.0 + tangent)
    slope = half_up + 0.5 * values * (1.0 - tangent * tangent) * gelu_root * (
        1.0 + 3.0 * gelu_cubic * squared
    )
    return values * half_up, slope


def normalize(values):
    average = jnp.mean(values, axis=-1, keepdims=True)
    centred = values - average
    inverse = lax.rsqrt(jnp.mean(centred * centred, axis=-1, keepdims=True) + norm_eps)
    return (centred * inverse, inverse)


def norm_back(upstream, normed, inverse, gain):
    scaled = upstream * gain
    centred_grad = (
        scaled
        - jnp.mean(scaled, axis=-1, keepdims=True)
        - normed * jnp.mean(scaled * normed, axis=-1, keepdims=True)
    )
    return inverse * centred_grad


def segment_reach(lengths, parents, tree_size):
    segment_count = lengths.shape[0]
    number = jnp.arange(segment_count, dtype=jnp.int32)
    segment_end = jnp.sum(jnp.where(number[None, :] <= number[:, None], lengths[None, :], 0), axis=1)
    starts = segment_end - lengths
    position = jnp.arange(tree_size, dtype=jnp.int32)
    member = (
        (position[:, None] >= starts[None, :]) & (position[:, None] < segment_end[None, :])
    ).astype(jnp.float32)
    parent_table = (parents[:, None] == number[None, :]).astype(jnp.float32)
    identity = jnp.eye(segment_count, dtype=jnp.float32)
    closure = jnp.maximum(identity, parent_table)
    steps = 1
    while steps < segment_count:
        closure = jnp.minimum(jnp.dot(closure, closure), 1.0)
        steps *= 2
    reachable = jnp.dot(member, closure)
    return (reachable, member)


def block_mask(reachable, member, first_row, block_rows):
    path_seen = jnp.dot(reachable[first_row : first_row + block_rows], member.T)
    query_place = first_row + jnp.arange(block_rows, dtype=jnp.int32)
    key_place = jnp.arange(member.shape[0], dtype=jnp.int32)
    return (path_seen > 0.5) & (key_place[None, :] <= query_place[:, None])


def block_scores(query_block, key_heads, reachable, member, first_row):
    score_scale = 1.0 / math.sqrt(query_block.shape[-1])
    scores = (
        jnp.einsum("hqc,hkc->hqk", query_block, key_heads, preferred_element_type=jnp.float32)
        * score_scale
    )
    allowed = block_mask(reachable, member, first_row, query_block.shape[1])
    return jnp.where(allowed[None], scores, masked_score)


def attend_tree(query_heads, key_heads, value_heads, reachable, member):
    tree_size = query_heads.shape[1]
    block_rows = min(512, tree_size)
    outputs = []
    totals = []
    for first_row in range(0, tree_size, block_rows):
        query_block = query_heads[:, first_row : first_row + block_rows]
        scores = block_scores(query_block, key_heads, reachable, member, first_row)
        row_max = jnp.max(scores, axis=-1, keepdims=True)
        weights = jnp.exp(scores - row_max)
        row_total = jnp.sum(weights, axis=-1, keepdims=True)
        softmax_low = (weights / row_total).astype(jnp.bfloat16)
        attended = jnp.einsum(
            "hqk,hkc->hqc", softmax_low, value_heads, preferred_element_type=jnp.float32
        )
        outputs.append(attended.astype(jnp.bfloat16))
        totals.append((row_max + jnp.log(row_total))[..., 0])
    return (jnp.concatenate(outputs, axis=1), jnp.concatenate(totals, axis=1))


def attend_back(query_heads, key_heads, value_heads, reachable, member, log_totals, grad_attended):
    tree_size = query_heads.shape[1]
    block_rows = min(512, tree_size)
    score_scale = 1.0 / math.sqrt(query_heads.shape[-1])
    query_grads = []
    key_grad = jnp.zeros(key_heads.shape, jnp.float32)
    value_grad = jnp.zeros(value_heads.shape, jnp.float32)
    for first_row in range(0, tree_size, block_rows):
        query_block = query_heads[:, first_row : first_row + block_rows]
        scores = block_scores(query_block, key_heads, reachable, member, first_row)
        softmax_weights = jnp.exp(scores - log_totals[:, first_row : first_row + block_rows, None])
        grad_block = grad_attended[:, first_row : first_row + block_rows]
        grad_weights = jnp.einsum(
            "hqc,hkc->hqk", grad_block, value_heads, preferred_element_type=jnp.float32
        )
        centre = jnp.sum(softmax_weights * grad_weights, axis=-1, keepdims=True)
        grad_scores = (softmax_weights * (grad_weights - centre)).astype(jnp.bfloat16)
        query_grads.append(
            jnp.einsum("hqk,hkc->hqc", grad_scores, key_heads, preferred_element_type=jnp.float32)
            * score_scale
        )
        key_grad = (
            key_grad
            + jnp.einsum(
                "hqk,hqc->hkc", grad_scores, query_block, preferred_element_type=jnp.float32
            )
            * score_scale
        )
        value_grad = value_grad + jnp.einsum(
            "hqk,hqc->hkc",
            softmax_weights.astype(jnp.bfloat16),
            grad_block,
            preferred_element_type=jnp.float32,
        )
    query_grad = jnp.concatenate(query_grads, axis=1)
    return (
        query_grad.astype(jnp.bfloat16),
        key_grad.astype(jnp.bfloat16),
        value_grad.astype(jnp.bfloat16),
    )


def across(values):
    return lax.ppermute(values, "tp", [(0, 1), (1, 0)])


def swapped(values, offset):
    if offset == 0:
        return values
    count = lax.axis_size("fsdp")
    return lax.ppermute(values, "fsdp", [(i, i ^ offset) for i in range(count)])


def in_order(bit, first, second, axis=0):
    return jnp.stack(
        [jnp.where(bit == 0, first, second), jnp.where(bit == 0, second, first)], axis=axis
    )


def gather_blocks(own, index, bits):
    gathered = own[None]
    for bit in bits:
        other = swapped(gathered, 1 << bit)
        pair = in_order((index >> bit) & 1, gathered, other)
        gathered = pair.reshape(-1, *own.shape)
    return gathered


def reduce_blocks(blocks, index, count):
    bit = 0
    part = blocks
    while count > 1:
        mine = (index >> bit) & 1
        split = part.reshape(count // 2, 2, *blocks.shape[1:])
        keep = lax.dynamic_index_in_dim(split, mine, 1, keepdims=False)
        give = lax.dynamic_index_in_dim(split, 1 - mine, 1, keepdims=False)
        got = swapped(give.astype(low), 1 << bit)
        part = keep.astype(wide) + got.astype(wide)
        if count > 2:
            part = part.astype(low)
        count //= 2
        bit += 1
    return part[0]


def shards(
    inputs,
    token_ids,
    hash_table,
    segment_lengths,
    segment_parents,
    first_gain,
    first_bias,
    input_weight,
    output_weight,
    second_gain,
    second_bias,
    expert_in,
    expert_out,
    cotangent,
):
    own_count, model_width = inputs.shape
    expert_count = lax.axis_size("fsdp")
    tree_size = token_ids.shape[0]
    capacity = 2 * own_count // expert_count
    local_width = input_weight.shape[2]
    head_count = local_width // HD
    place = lax.axis_index("fsdp")
    side = lax.axis_index("tp")
    chips = expert_count // 2
    bit_count = expert_count.bit_length() - 1

    def both_rows(mine, theirs):
        return in_order(side, mine, theirs).reshape(2 * own_count, *mine.shape[1:])

    def own_rows(values):
        return lax.dynamic_slice_in_dim(values, side * own_count, own_count, 0)

    def other_rows(values):
        return lax.dynamic_slice_in_dim(values, (1 - side) * own_count, own_count, 0)

    def split_heads(flat):
        return flat.reshape(tree_size, head_count, HD).transpose(1, 0, 2)

    def join_heads(split):
        return split.transpose(1, 0, 2).reshape(tree_size, local_width)

    group_inputs = both_rows(inputs, across(inputs))
    shard_in = jnp.transpose(input_weight, (1, 0, 2)).reshape(-1, 3 * local_width)
    full_in = gather_blocks(shard_in, place, list(range(1, bit_count)) + [0])
    half = expert_count // 2
    full_in = (
        full_in.reshape(2, half, *shard_in.shape).swapaxes(0, 1).reshape(model_width, 3 * local_width)
    )
    shard_out = output_weight.T
    full_out = gather_blocks(shard_out, place, list(range(1, bit_count)) + [0])
    full_out = (
        full_out.reshape(2, half, *shard_out.shape).swapaxes(0, 1).reshape(model_width, local_width)
    )
    other_out = across(full_out)

    own_ids = own_rows(token_ids)
    table = hash_table.reshape(-1, 128).astype(low)
    row_hot = (own_ids[:, None] // 128 == jnp.arange(table.shape[0])[None, :]).astype(low)
    rows = jnp.dot(row_hot, table, preferred_element_type=wide)
    lane_hot = own_ids[:, None] % 128 == jnp.arange(128)[None, :]
    experts = jnp.sum(jnp.where(lane_hot, rows, 0.0), axis=1).astype(jnp.int32)
    hot = (experts[:, None] == jnp.arange(expert_count)[None, :]).astype(low)
    earlier = (jnp.arange(own_count)[:, None] > jnp.arange(own_count)[None, :]).astype(low)
    before = jnp.dot(earlier, hot, preferred_element_type=wide)
    rank = jnp.sum(before * hot.astype(wide), axis=1).astype(jnp.int32)
    offset = experts ^ place
    slot = ((offset & 1) * chips + (offset >> 1)) * capacity + rank
    slot_count = expert_count * capacity
    chooser = (slot[None, :] == jnp.arange(slot_count)[:, None]).astype(low)

    def pack(values):
        return jnp.dot(chooser, values, preferred_element_type=wide).astype(low)

    def unpack(values):
        return lax.dot_general(
            chooser, values, (((0,), (0,)), ((), ())), preferred_element_type=wide
        )

    group_chips = max(1, chips // 4)

    def dispatch(values):
        packed = pack(values).reshape(2, chips, capacity, model_width)
        sibling = swapped(packed[1], 1)
        groups = []
        for first in range(0, chips, group_chips):
            arrived = [
                swapped(jnp.stack([packed[0, k], sibling[k]]), 2 * k)
                for k in range(first, first + group_chips)
            ]
            arrived = jnp.stack(arrived).reshape(-1, model_width)
            groups.append(jnp.concatenate([arrived, across(arrived)]))
        return groups

    def give_back(groups):
        returned = []
        for g, values in enumerate(groups):
            count = values.shape[0] // 2
            mine = values[:count] + across(values[count:].astype(low)).astype(wide)
            mine = mine.astype(low).reshape(group_chips, 2, capacity, model_width)
            returned += [swapped(mine[k], 2 * (g * group_chips + k)) for k in range(group_chips)]
        returned = jnp.stack(returned)
        ours = returned[:, 0]
        theirs = swapped(returned[:, 1], 1)
        return unpack(jnp.concatenate([ours, theirs]).reshape(slot_count, model_width))

    grad_groups = dispatch(cotangent)

    residual = inputs.astype(wide)
    group_hat, group_inverse = normalize(group_inputs.astype(wide))
    group_normed = (group_hat * first_gain + first_bias).astype(low)
    first_hat = own_rows(group_hat)
    first_inverse = own_rows(group_inverse)
    projected = jnp.dot(group_normed, full_in, preferred_element_type=wide).astype(low)
    query_heads = split_heads(projected[:, :local_width])
    key_heads = split_heads(projected[:, local_width : 2 * local_width])
    value_heads = split_heads(projected[:, 2 * local_width :])
    reachable, member = segment_reach(segment_lengths[0], segment_parents[0], tree_size)
    attended, log_totals = attend_tree(query_heads, key_heads, value_heads, reachable, member)
    attended = join_heads(attended)
    attended_mine = own_rows(attended)
    attended_more = across(other_rows(attended))

    def wide_nt(left, right):
        return lax.dot_general(left, right, (((1,), (1,)), ((), ())), preferred_element_type=wide)

    def wide_tn(left, right):
        return lax.dot_general(left, right, (((0,), (0,)), ((), ())), preferred_element_type=wide)

    branch = wide_nt(attended_mine, full_out) + wide_nt(attended_more, other_out)
    middle = residual + branch
    second_hat, second_inverse = normalize(middle)
    second_normed = (second_hat * second_gain + second_bias).astype(low)

    weight_in = expert_in[0]
    weight_out = expert_out[0]
    slot_groups = dispatch(second_normed)
    grad_rows = []
    ffn_rows = []
    actives = []
    grad_pres = []
    for slot_rows, slot_grads in zip(slot_groups, grad_groups):
        grad_active = wide_nt(slot_grads, weight_out).astype(low)
        hidden_pre = jnp.dot(slot_rows, weight_in, preferred_element_type=wide)
        active, slope = gelu_both(hidden_pre)
        grad_pre = (grad_active * slope).astype(low)
        grad_rows.append(wide_nt(grad_pre, weight_in))
        actives.append(active.astype(low))
        grad_pres.append(grad_pre)
    grad_second = give_back(grad_rows)
    for active in actives:
        ffn_rows.append(jnp.dot(active, weight_out, preferred_element_type=wide))
    expert_out_grad = wide_tn(jnp.concatenate(actives), jnp.concatenate(grad_groups))
    expert_in_grad = wide_tn(jnp.concatenate(slot_groups), jnp.concatenate(grad_pres))

    second_gain_grad = jnp.sum(grad_second * second_hat, axis=0)
    second_bias_grad = jnp.sum(grad_second, axis=0)
    grad_middle = cotangent.astype(wide) + norm_back(
        grad_second, second_hat, second_inverse, second_gain
    )
    grad_branch = grad_middle.astype(low)
    grad_attended_mine = jnp.dot(grad_branch, full_out, preferred_element_type=wide).astype(low)
    grad_attended_more = across(
        jnp.dot(grad_branch, other_out, preferred_element_type=wide).astype(low)
    )
    grad_attended = both_rows(grad_attended_mine, grad_attended_more)
    ffn = give_back(ffn_rows)
    out_block = (middle + ffn).astype(low)

    query_grad, key_grad, value_grad = attend_back(
        query_heads, key_heads, value_heads, reachable, member, log_totals, split_heads(grad_attended)
    )
    grad_projected = jnp.concatenate(
        [join_heads(query_grad), join_heads(key_grad), join_heads(value_grad)], axis=1
    )
    output_part = wide_tn(grad_branch, attended_mine) + across(
        wide_tn(grad_branch, attended_more).astype(low)
    ).astype(wide)
    output_weight_grad = reduce_blocks(
        output_part.astype(low).reshape(expert_count, -1, local_width), place, expert_count
    ).T

    grad_first_part = wide_nt(grad_projected, full_in)
    grad_first = own_rows(grad_first_part) + across(other_rows(grad_first_part).astype(low)).astype(
        wide
    )
    input_grad = grad_middle + norm_back(grad_first, first_hat, first_inverse, first_gain)
    input_part = wide_tn(group_normed, grad_projected).astype(low)
    input_weight_grad = reduce_blocks(
        input_part.reshape(expert_count, -1, 3 * local_width), place, expert_count
    )
    input_weight_grad = input_weight_grad.reshape(-1, 3, local_width).transpose(1, 0, 2)
    norm_sums = jnp.stack(
        [
            jnp.sum(grad_first_part * group_hat, axis=0),
            jnp.sum(grad_first_part, axis=0),
            second_gain_grad,
            second_bias_grad,
        ]
    )
    for bit in range(bit_count):
        norm_sums = norm_sums + swapped(norm_sums, 1 << bit)
    norm_sums = norm_sums + across(norm_sums)
    return (
        out_block,
        input_grad,
        norm_sums[0],
        norm_sums[1],
        input_weight_grad,
        output_weight_grad,
        norm_sums[2],
        norm_sums[3],
        expert_in_grad[None],
        expert_out_grad[None],
    )


def solution(mesh):
    return jax.shard_map(
        shards,
        mesh=mesh,
        in_specs=(
            P(("fsdp", "tp"), None),
            P("fsdp"),
            P(),
            P("fsdp", None),
            P("fsdp", None),
            P(),
            P(),
            P(None, "fsdp", "tp"),
            P("tp", "fsdp"),
            P(),
            P(),
            P("fsdp", None, "tp"),
            P("fsdp", "tp", None),
            P(("fsdp", "tp"), None),
        ),
        out_specs=(
            P(("fsdp", "tp"), None),
            P(("fsdp", "tp"), None),
            P(),
            P(),
            P(None, "fsdp", "tp"),
            P("tp", "fsdp"),
            P(),
            P(),
            P("fsdp", None, "tp"),
            P("fsdp", "tp", None),
        ),
        check_vma=False,
    )
```

```python
import functools

import jax
import jax.numpy as jnp
from jax import lax
from jax.experimental import pallas as pl
from jax.experimental.pallas import tpu as pltpu
from jax.sharding import PartitionSpec as P

HD = 64
LANES = 128

norm_eps = 1e-05
masked_score = -1e30
gelu_root = 0.7978845608028654
gelu_cubic = 0.044715
low = jnp.bfloat16
wide = jnp.float32

NN = (((1,), (0,)), ((), ()))
NT = (((1,), (1,)), ((), ()))
TN = (((0,), (0,)), ((), ()))


def dot(left, right, dims=NN):
    return lax.dot_general(left, right, dims, preferred_element_type=wide)


def gelu_both(values):
    squared = values * values
    tangent = jnp.tanh(gelu_root * values * (1.0 + gelu_cubic * squared))
    half_up = 0.5 * (1.0 + tangent)
    slope = half_up + 0.5 * values * (1.0 - tangent * tangent) * gelu_root * (
        1.0 + 3.0 * gelu_cubic * squared
    )
    return values * half_up, slope


def normalize(values):
    average = jnp.mean(values, axis=-1, keepdims=True)
    centred = values - average
    inverse = lax.rsqrt(jnp.mean(centred * centred, axis=-1, keepdims=True) + norm_eps)
    return (centred * inverse, inverse)


def norm_back(upstream, normed, inverse, gain):
    scaled = upstream * gain
    centred_grad = (
        scaled
        - jnp.mean(scaled, axis=-1, keepdims=True)
        - normed * jnp.mean(scaled * normed, axis=-1, keepdims=True)
    )
    return inverse * centred_grad


def array(shape, kind):
    return jax.ShapeDtypeStruct(shape, kind)


def run(kernel, operands, outs, flops=0, limit=32, **more):
    if "in_specs" not in more:
        more["in_specs"] = [spec_of(x) for x in operands]
    moved = sum(x.size * x.dtype.itemsize for x in operands) + sum(
        x.size * x.dtype.itemsize for x in jax.tree.leaves(outs)
    )
    return pl.pallas_call(
        kernel,
        out_shape=outs,
        compiler_params=pltpu.CompilerParams(vmem_limit_bytes=limit << 20),
        cost_estimate=pl.CostEstimate(flops=int(flops), bytes_accessed=int(moved), transcendentals=0),
        **more,
    )(*operands)


def spec_of(x):
    scalar = x.ndim == 1 and x.dtype == jnp.int32
    return pl.BlockSpec(memory_space=pltpu.SMEM if scalar else pltpu.VMEM)


def project_kernel(chips, place_ref, own_ref, other_ref, gain_ref, bias_ref, mine_ref, sibling_ref, full_ref, out_ref):
    place, side = place_ref[0], place_ref[1]
    if chips:
        rows = mine_ref.shape[2]
        for k in range(chips):
            source = place ^ (2 * k)
            full_ref[:, pl.ds(pl.multiple_of(source * rows, rows), rows), :] = mine_ref[k]
            source = source ^ 1
            full_ref[:, pl.ds(pl.multiple_of(source * rows, rows), rows), :] = sibling_ref[k]
    else:
        full_ref[...] = mine_ref[...]
    count, width = own_ref.shape[0], mine_ref.shape[-1]
    for ref, first in ((own_ref, side * count), (other_ref, (1 - side) * count)):
        hat, _ = normalize(ref[...].astype(wide))
        normed = (hat * gain_ref[...] + bias_ref[...]).astype(low)
        for n in range(3):
            out_ref[pl.ds(pl.multiple_of(first, count), count), n * width : (n + 1) * width] = dot(
                normed, full_ref[n]
            ).astype(low)


def attend_kernel(block, place_ref, q_ref, k_ref, v_ref, unreached_ref, member_ref, out_ref, total_ref, keep_ref, give_ref):
    side = place_ref[1]
    rows = q_ref.shape[0]
    lane = lax.broadcasted_iota(jnp.int32, (1, LANES), 1)
    first_head = lane < HD
    ones = jnp.ones((rows, LANES), low)
    keys = jnp.concatenate([k_ref[...], member_ref[...]], axis=1)
    values = jnp.concatenate([v_ref[...], ones], axis=1)
    causal = lax.broadcasted_iota(jnp.int32, (block, block), 1) <= lax.broadcasted_iota(
        jnp.int32, (block, block), 0
    )
    for start in range(0, rows, block):
        stop = start + block
        query = q_ref[start:stop] * HD**-0.5
        unreached = unreached_ref[start:stop]
        halves = []
        for own in (first_head, ~first_head):
            left = jnp.concatenate([jnp.where(own, query, 0).astype(low), unreached], axis=1)
            scores = dot(left, keys[:stop], NT)
            near = jnp.where(causal, scores[:, start:], masked_score)
            top = jnp.max(near, axis=1, keepdims=True)
            if start:
                far = scores[:, :start]
                top = jnp.maximum(top, jnp.max(far, axis=1, keepdims=True))
                weights = jnp.concatenate(
                    [jnp.exp(far - top).astype(low), jnp.exp(near - top).astype(low)], axis=1
                )
            else:
                weights = jnp.exp(near - top).astype(low)
            sums = dot(weights, values[:stop], NN)
            total = sums[:, LANES:]
            halves.append((sums[:, :LANES] / total, top + jnp.log(total)))
        out_ref[start:stop] = jnp.where(first_head, halves[0][0], halves[1][0]).astype(low)
        total_ref[start:stop] = jnp.where(first_head, halves[0][1], halves[1][1])
    half = rows // 2
    keep_ref[...] = out_ref[pl.ds(pl.multiple_of(side * half, half), half)]
    give_ref[...] = out_ref[pl.ds(pl.multiple_of((1 - side) * half, half), half)]


def attend(place, projected, unreached, member, block=256):
    rows, width = projected.shape
    pairs = width // (3 * LANES)

    def part(n, height=rows):
        return pl.BlockSpec((height, LANES), lambda p: (0, n * pairs + p))

    fixed = pl.BlockSpec((rows, LANES), lambda p: (0, 0))
    return run(
        functools.partial(attend_kernel, block),
        (place, projected, projected, projected, unreached, member),
        [
            array((rows, width // 3), low),
            array((rows, width // 3), wide),
            array((rows // 2, width // 3), low),
            array((rows // 2, width // 3), low),
        ],
        flops=12e9,
        grid=(pairs,),
        in_specs=[spec_of(place), part(0), part(1), part(2), fixed, fixed],
        out_specs=[part(0), part(0), part(0, rows // 2), part(0, rows // 2)],
    )


def attend_back_kernel(
    block, place_ref, q_ref, k_ref, v_ref, unreached_ref, member_ref, out_ref, total_ref, mine_ref, more_ref, res_ref, dk, dv, grads
):
    side = place_ref[1]
    rows = q_ref.shape[0]
    half = rows // 2
    grads[pl.ds(pl.multiple_of(side * half, half), half)] = mine_ref[...]
    grads[pl.ds(pl.multiple_of((1 - side) * half, half), half)] = more_ref[...]
    lane = lax.broadcasted_iota(jnp.int32, (1, LANES), 1)
    first_head = lane < HD
    keys = jnp.concatenate([k_ref[...], member_ref[...]], axis=1)
    causal = lax.broadcasted_iota(jnp.int32, (block, block), 1) <= lax.broadcasted_iota(
        jnp.int32, (block, block), 0
    )
    for start in range(rows - block, -1, -block):
        stop = start + block
        query = q_ref[start:stop] * HD**-0.5
        unreached = unreached_ref[start:stop]
        grad = grads[start:stop]
        both = grad.astype(wide) * out_ref[start:stop].astype(wide)
        query_halves = []
        key_terms = []
        value_terms = []
        for head, own in enumerate((first_head, ~first_head)):
            q_own = jnp.where(own, query, 0).astype(low)
            g_own = jnp.where(own, grad, 0).astype(low)
            scores = dot(jnp.concatenate([q_own, unreached], axis=1), keys[:stop], NT)
            total = total_ref[start:stop, HD * head : HD * head + 1]
            centre = jnp.sum(jnp.where(own, both, 0.0), axis=1, keepdims=True)
            near = jnp.exp(jnp.where(causal, scores[:, start:], masked_score) - total)
            if start:
                weights = jnp.concatenate([jnp.exp(scores[:, :start] - total), near], axis=1)
            else:
                weights = near
            gains = dot(g_own, v_ref[:stop], NT)
            slopes = (weights * (gains - centre)).astype(low)
            query_halves.append(dot(slopes, k_ref[:stop], NN))
            key_terms.append(dot(slopes, q_own, TN))
            value_terms.append(dot(weights.astype(low), g_own, TN))
        res_ref[0, start:stop] = (
            jnp.where(first_head, query_halves[0], query_halves[1]) * HD**-0.5
        ).astype(low)
        if stop == rows:
            dk[...] = key_terms[0] + key_terms[1]
            dv[...] = value_terms[0] + value_terms[1]
        else:
            dk[:stop] += key_terms[0] + key_terms[1]
            dv[:stop] += value_terms[0] + value_terms[1]
    res_ref[1] = dk[...].astype(low)
    res_ref[2] = dv[...].astype(low)


def attend_back(place, projected, unreached, member, out, total, mine, more, block=256):
    rows, width = projected.shape
    pairs = width // (3 * LANES)

    def part(n, height=rows):
        return pl.BlockSpec((height, LANES), lambda p: (0, n * pairs + p))

    fixed = pl.BlockSpec((rows, LANES), lambda p: (0, 0))
    return run(
        functools.partial(attend_back_kernel, block),
        (place, projected, projected, projected, unreached, member, out, total, mine, more),
        array((3, rows, width // 3), low),
        flops=24e9,
        grid=(pairs,),
        in_specs=[spec_of(place), part(0), part(1), part(2), fixed, fixed, part(0), part(0)]
        + [part(0, rows // 2)] * 2,
        out_specs=pl.BlockSpec((3, rows, LANES), lambda p: (0, 0, p)),
        scratch_shapes=[pltpu.VMEM((rows, LANES), wide)] * 2 + [pltpu.VMEM((rows, LANES), low)],
    )


def branch_kernel(keep_ref, more_ref, weight_ref, other_ref, residual_ref, gain_ref, bias_ref, middle_ref, normed_ref):
    branch = dot(keep_ref[...], weight_ref[...], NT) + dot(more_ref[...], other_ref[...], NT)
    middle = residual_ref[...].astype(wide) + branch
    middle_ref[...] = middle
    hat, _ = normalize(middle)
    normed_ref[...] = (hat * gain_ref[...] + bias_ref[...]).astype(low)


def pack_kernel(own_ref, sibling_ref, own_slot_ref, sibling_slot_ref, *out_refs):
    capacity = out_refs[0].shape[1]
    slots = len(out_refs) * capacity
    for source, (ref, slot_ref) in enumerate(
        ((own_ref, own_slot_ref), (sibling_ref, sibling_slot_ref))
    ):
        place = lax.broadcasted_iota(jnp.int32, (slots, ref.shape[0]), 0)
        chooser = (place == slot_ref[...]).astype(wide).astype(low)
        packed = dot(chooser, ref[...]).astype(low)
        for k, out_ref in enumerate(out_refs):
            out_ref[source] = packed[k * capacity : (k + 1) * capacity]


def expert_kernel(first, count, chunk, place_ref, in_ref, out_ref, grads_ref, more_grads_ref, *refs):
    pieces, more_pieces = refs[:count], refs[count : 2 * count]
    x_ref, ct_ref, active_ref, slope_ref, keep_ref, give_ref = refs[-6:]
    step = pl.program_id(0)
    place = place_ref[0]
    capacity = pieces[0].shape[1]
    rows = 2 * capacity
    for k in range(count):

        @pl.when(step == k)
        def _(k=k):
            for c in range(2):
                x_ref[0, c * capacity : (c + 1) * capacity] = pieces[k][c]
                x_ref[0, rows + c * capacity : rows + (c + 1) * capacity] = more_pieces[k][c]

    source = place ^ (2 * (first + step))
    for c in range(2):
        ct_ref[0, c * capacity : (c + 1) * capacity] = grads_ref[source ^ c]
        ct_ref[0, rows + c * capacity : rows + (c + 1) * capacity] = more_grads_ref[source ^ c]
    x = x_ref[0]
    ct = ct_ref[0]
    total = None
    for start in range(0, in_ref.shape[1], chunk):
        stop = start + chunk
        pre = dot(x, in_ref[:, start:stop])
        gains = dot(ct, out_ref[start:stop], NT)
        active, slope = gelu_both(pre)
        active_ref[0, :, start:stop] = active.astype(low)
        grad_pre = (gains * slope).astype(low)
        slope_ref[0, :, start:stop] = grad_pre
        term = dot(grad_pre, in_ref[:, start:stop], NT)
        total = term if total is None else total + term
    keep_ref[0] = total[:rows]
    give_ref[0] = total[rows:].astype(low)


def expert_group(place, weight_in, weight_out, grads, more_grads, pieces, more_pieces, buffers, span, chips):
    first, stop = span
    count = stop - first
    capacity, width = pieces[0].shape[1:]
    hidden = weight_in.shape[1]
    rows = 4 * capacity
    operands = [place, weight_in, weight_out, grads, more_grads, *pieces, *more_pieces]
    specs = [spec_of(place)] + [
        pl.BlockSpec(x.shape, lambda i, n=x.ndim: (0,) * n) for x in operands[1:]
    ]
    aliases = {}
    if buffers is not None:
        aliases = {len(operands) + n: n for n in range(4)}
        operands += buffers
        specs += [pl.BlockSpec(memory_space=pl.ANY)] * 4

    def block(height, size, offset):
        return pl.BlockSpec((1, height, size), lambda i: (offset + i, 0, 0))

    res = run(
        functools.partial(expert_kernel, first, count, min(512, hidden)),
        operands,
        [
            array((chips, rows, width), low),
            array((chips, rows, width), low),
            array((chips, rows, hidden), low),
            array((chips, rows, hidden), low),
            array((count, rows // 2, width), wide),
            array((count, rows // 2, width), low),
        ],
        flops=6 * count * rows * width * hidden,
        grid=(count,),
        in_specs=specs,
        out_specs=[
            block(rows, width, first),
            block(rows, width, first),
            block(rows, hidden, first),
            block(rows, hidden, first),
            block(rows // 2, width, 0),
            block(rows // 2, width, 0),
        ],
        input_output_aliases=aliases,
    )
    return res[:4], res[4], res[5]


def pieces_kernel(keep_ref, more_ref, *out_refs):
    capacity = out_refs[0].shape[1]
    for k, out_ref in enumerate(out_refs):
        total = (keep_ref[k] + more_ref[k].astype(wide)).astype(low)
        for c in range(2):
            out_ref[c] = total[c * capacity : (c + 1) * capacity]


def unpack_kernel(own_slot_ref, sibling_slot_ref, *refs):
    pieces, (own_ref, sibling_ref) = refs[:-2], refs[-2:]
    capacity = pieces[0].shape[1]
    slots = len(pieces) * capacity
    for source, (slot_ref, out_ref) in enumerate(
        ((own_slot_ref, own_ref), (sibling_slot_ref, sibling_ref))
    ):
        place = lax.broadcasted_iota(jnp.int32, (slot_ref.shape[0], slots), 1)
        chooser = (place == slot_ref[...]).astype(wide).astype(low)
        values = jnp.concatenate([piece[source] for piece in pieces], axis=0)
        out_ref[...] = dot(chooser, values).astype(low)


def ffn_kernel(active_ref, weight_ref, keep_ref, give_ref):
    values = dot(active_ref[0], weight_ref[...])
    rows = keep_ref.shape[1]
    keep_ref[0] = values[:rows]
    give_ref[0] = values[rows:].astype(low)


def ffn_sum_kernel(place_ref, keep_ref, more_ref, out_ref):
    place = place_ref[0]
    capacity = out_ref.shape[1]
    for k in range(keep_ref.shape[0]):
        total = (keep_ref[k] + more_ref[k].astype(wide)).astype(low)
        for c in range(2):
            out_ref[place ^ (2 * k + c)] = total[c * capacity : (c + 1) * capacity]


def out_kernel(slot_ref, values_ref, middle_ref, out_ref):
    place = lax.broadcasted_iota(jnp.int32, (slot_ref.shape[0], values_ref.shape[0]), 1)
    chooser = (place == slot_ref[...]).astype(wide).astype(low)
    out_ref[...] = (middle_ref[...] + dot(chooser, values_ref[...])).astype(low)


def middle_back_kernel(
    own_ref, more_ref, middle_ref, ct_ref, gain_ref, weight_ref, other_ref,
    grad_ref, branch_ref, mine_ref, give_ref, sums_ref,
):
    grad_second = own_ref[...].astype(wide) + more_ref[...].astype(wide)
    hat, inverse = normalize(middle_ref[...])
    sums_ref[0:1] = jnp.sum(grad_second * hat, axis=0, keepdims=True)
    sums_ref[1:2] = jnp.sum(grad_second, axis=0, keepdims=True)
    grad_middle = ct_ref[...].astype(wide) + norm_back(grad_second, hat, inverse, gain_ref[...])
    grad_ref[...] = grad_middle
    branch = grad_middle.astype(low)
    branch_ref[...] = branch
    give_ref[...] = dot(branch, other_ref[...]).astype(low)
    mine_ref[...] = dot(branch, weight_ref[...]).astype(low)


def output_part_kernel(branch_ref, keep_ref, more_ref, own_ref, give_ref):
    give_ref[...] = dot(branch_ref[...], more_ref[...], TN).astype(low)
    own_ref[...] = dot(branch_ref[...], keep_ref[...], TN)


def first_give_kernel(place_ref, grads_ref, full_ref, give_ref):
    half = give_ref.shape[0]
    first = pl.multiple_of((1 - place_ref[1]) * half, half)
    total = None
    for n in range(3):
        term = dot(grads_ref[n, pl.ds(first, half)], full_ref[n], NT)
        total = term if total is None else total + term
    give_ref[...] = total.astype(low)


def weight_part_kernel(
    chips, place_ref, own_ref, other_ref, gain_ref, bias_ref, grads_ref, part_ref, more_ref, keep_ref, give_ref, normed, parts
):
    place, side = place_ref[0], place_ref[1]
    count = own_ref.shape[0]
    for ref, first in ((own_ref, side * count), (other_ref, (1 - side) * count)):
        hat, _ = normalize(ref[...].astype(wide))
        normed[pl.ds(pl.multiple_of(first, count), count)] = (
            hat * gain_ref[...] + bias_ref[...]
        ).astype(low)
    for n in range(3):
        parts[n] = dot(normed[...], grads_ref[n], TN).astype(low)
    parts[3] = (part_ref[...] + more_ref[...].astype(wide)).astype(low)
    if chips:
        rows = keep_ref.shape[3]
        for k in range(chips):
            target = place ^ (2 * k)
            keep_ref[k % 2, k // 2] = parts[:, pl.ds(pl.multiple_of(target * rows, rows), rows)]
            target = target ^ 1
            give_ref[k % 2, k // 2] = parts[:, pl.ds(pl.multiple_of(target * rows, rows), rows)]
    else:
        keep_ref[...] = parts[...]
        give_ref[...] = jnp.zeros(give_ref.shape, low)


def first_own_kernel(place_ref, grads_ref, full_ref, give_ref, own_in_ref, other_in_ref, own_ref, sums_ref):
    half = own_ref.shape[0]
    first = pl.multiple_of(place_ref[1] * half, half)
    total = None
    for n in range(3):
        term = dot(grads_ref[n, pl.ds(first, half)], full_ref[n], NT)
        total = term if total is None else total + term
    own_ref[...] = total
    hat, _ = normalize(own_in_ref[...].astype(wide))
    more_hat, _ = normalize(other_in_ref[...].astype(wide))
    more = give_ref[...].astype(wide)
    sums_ref[0:1] = jnp.sum(total * hat + more * more_hat, axis=0, keepdims=True)
    sums_ref[1:2] = jnp.sum(total + more, axis=0, keepdims=True)


def halves_kernel(keep_ref, more_ref, near_ref, far_ref):
    near_ref[...] = (keep_ref[0].astype(wide) + more_ref[0].astype(wide)).astype(low)
    far_ref[...] = (keep_ref[1].astype(wide) + more_ref[1].astype(wide)).astype(low)


def quarters_kernel(keep_ref, more_ref, own_ref, *out_refs):
    own_ref[...] = keep_ref[0].astype(wide) + more_ref[0].astype(wide)
    for n, out_ref in enumerate(out_refs):
        out_ref[...] = (keep_ref[n + 1].astype(wide) + more_ref[n + 1].astype(wide)).astype(low)


def total_kernel(own_ref, *refs):
    total = own_ref[...]
    for ref in refs[:-2]:
        total = total + ref[...].astype(wide)
    refs[-2][...] = total[:3]
    refs[-1][...] = total[3]


def input_grad_kernel(grad_ref, own_ref, more_ref, input_ref, gain_ref, out_ref):
    hat, inverse = normalize(input_ref[...].astype(wide))
    upstream = own_ref[...] + more_ref[...].astype(wide)
    out_ref[...] = grad_ref[...] + norm_back(upstream, hat, inverse, gain_ref[...])


def across(values):
    return lax.ppermute(values, "tp", [(0, 1), (1, 0)])


def swapped(values, offset):
    if offset == 0:
        return values
    count = lax.axis_size("fsdp")
    return lax.ppermute(values, "fsdp", [(i, i ^ offset) for i in range(count)])


def after(values, *earlier):
    return lax.optimization_barrier((values, earlier))[0]


def reduce_blocks(blocks, index, count):
    bit = 0
    part = blocks
    while count > 1:
        mine = (index >> bit) & 1
        split = part.reshape(count // 2, 2, *blocks.shape[1:])
        keep = lax.dynamic_index_in_dim(split, mine, 1, keepdims=False)
        give = lax.dynamic_index_in_dim(split, 1 - mine, 1, keepdims=False)
        got = swapped(give.astype(low), 1 << bit)
        part = keep.astype(wide) + got.astype(wide)
        if count > 2:
            part = part.astype(low)
        count //= 2
        bit += 1
    return part[0]


def tree_masks(lengths, parents, tree_size):
    segment_count = lengths.shape[0]
    number = jnp.arange(segment_count, dtype=jnp.int32)
    segment_end = jnp.sum(jnp.where(number[None, :] <= number[:, None], lengths[None, :], 0), axis=1)
    starts = segment_end - lengths
    position = jnp.arange(tree_size, dtype=jnp.int32)
    member = (
        (position[:, None] >= starts[None, :]) & (position[:, None] < segment_end[None, :])
    ).astype(wide)
    closure = jnp.maximum(
        jnp.eye(segment_count, dtype=wide), (parents[:, None] == number[None, :]).astype(wide)
    )
    steps = 1
    while steps < segment_count:
        closure = jnp.minimum(jnp.dot(closure, closure), 1.0)
        steps *= 2
    unreached = (1.0 - jnp.dot(member, closure)) * masked_score
    padding = ((0, 0), (0, LANES - segment_count))
    return jnp.pad(unreached, padding).astype(low), jnp.pad(member, padding).astype(low)


def shards(
    inputs,
    token_ids,
    hash_table,
    segment_lengths,
    segment_parents,
    first_gain,
    first_bias,
    input_weight,
    output_weight,
    second_gain,
    second_bias,
    expert_in,
    expert_out,
    cotangent,
):
    own_count, width = inputs.shape
    experts_in_all = lax.axis_size("fsdp")
    tree_size = token_ids.shape[0]
    capacity = 2 * own_count // experts_in_all
    local_width = input_weight.shape[2]
    chips = experts_in_all // 2
    shard_rows = input_weight.shape[1]
    hidden = expert_in.shape[2]
    index = lax.axis_index("fsdp")
    side = lax.axis_index("tp")
    place = jnp.stack([index, side]).astype(jnp.int32)
    in_kernel = shard_rows % 16 == 0
    first_gain, first_bias = first_gain[None], first_bias[None]
    second_gain, second_bias = second_gain[None], second_bias[None]

    other_inputs = across(inputs)
    shard = jnp.concatenate([input_weight, output_weight.T[None]])
    pieces = {0: shard}
    for k in range(2, chips, 2):
        pieces[k] = swapped(shard, 2 * k)
    for k in range(1, chips, 2):
        pieces[k] = swapped(pieces[k - 1], 2)
    mine = jnp.stack([pieces[k] for k in range(chips)])
    sibling = swapped(mine, 1)

    own_ids = lax.dynamic_slice_in_dim(token_ids, side * own_count, own_count, 0)
    table = hash_table.reshape(-1, LANES).astype(low)
    row_hot = (own_ids[:, None] // LANES == jnp.arange(table.shape[0])[None, :]).astype(low)
    lane_hot = own_ids[:, None] % LANES == jnp.arange(LANES)[None, :]
    experts = jnp.sum(jnp.where(lane_hot, dot(row_hot, table), 0.0), axis=1).astype(jnp.int32)
    hot = (experts[:, None] == jnp.arange(experts_in_all)[None, :]).astype(low)
    earlier = (jnp.arange(own_count)[:, None] > jnp.arange(own_count)[None, :]).astype(low)
    rank = jnp.sum(dot(earlier, hot) * hot.astype(wide), axis=1).astype(jnp.int32)
    own_slot = experts * capacity + rank
    sibling_slot = swapped(own_slot, 1)

    def chip_slot(slot):
        offset = (slot // capacity) ^ index
        return jnp.where(offset & 1 == 0, (offset >> 1) * capacity + slot % capacity, -1)

    own_place, sibling_place = chip_slot(own_slot), chip_slot(sibling_slot)

    slot_count = experts_in_all * capacity
    straight = (own_slot[None, :] == jnp.arange(slot_count)[:, None]).astype(low)
    packed_grads = after(dot(straight, cotangent).astype(low), mine)
    slot_grads = lax.all_to_all(
        packed_grads.reshape(experts_in_all, capacity, width), "fsdp", 0, 0, tiled=True
    )
    more_slot_grads = across(slot_grads)

    if in_kernel:
        weights = (mine, sibling)
    else:
        both = jnp.stack([mine, sibling], 1)
        both = both.reshape(experts_in_all, 4, shard_rows, local_width)
        full = jnp.concatenate(
            [lax.dynamic_index_in_dim(both, index ^ n, 0, False) for n in range(experts_in_all)], axis=1
        )
        weights = (full, full[:1, :16])
    full_weight, projected = run(
        functools.partial(project_kernel, chips if in_kernel else 0),
        (place, inputs, other_inputs, first_gain, first_bias, *weights),
        [array((4, width, local_width), low), array((tree_size, 3 * local_width), low)],
        flops=2 * tree_size * width * 3 * local_width,
    )
    out_weight = full_weight[3]
    other_out_weight = across(out_weight)
    unreached, member = tree_masks(segment_lengths[0], segment_parents[0], tree_size)
    attended, totals, attended_keep, attended_give = attend(place, projected, unreached, member)
    attended_more = across(attended_give)
    middle, second_normed = run(
        branch_kernel,
        (attended_keep, attended_more, out_weight, other_out_weight, inputs, second_gain, second_bias),
        [array((own_count, width), wide), array((own_count, width), low)],
        flops=2 * own_count * width * width,
    )

    sibling_normed = swapped(second_normed, 1)
    piece = array((2, capacity, width), low)
    packed = run(
        pack_kernel,
        (second_normed, sibling_normed, own_place[None], sibling_place[None]),
        [piece] * chips,
        flops=4 * own_count * own_count * width,
    )
    packed = after(packed, slot_grads)
    spans = [(0, chips // 2), (chips // 2, 3 * chips // 4), (3 * chips // 4, chips)]
    arrived = {}
    for k in range(*spans[1]):
        arrived[k] = swapped(packed[k], 2 * k)
    for k in range(*spans[0]):
        arrived[k] = swapped(packed[k], 2 * k)
    for k in range(*spans[2]):
        arrived[k] = swapped(after(packed[k], *[arrived[n] for n in range(*spans[0])]), 2 * k)
    more_arrived = {k: across(arrived[k]) for k in range(chips)}

    weight_in, weight_out = expert_in[0], expert_out[0]
    buffers = None
    returned = []
    for span in spans:
        buffers, keep, give = expert_group(
            place, weight_in, weight_out, slot_grads, more_slot_grads,
            [arrived[k] for k in range(*span)], [more_arrived[k] for k in range(*span)],
            buffers, span, chips,
        )
        sums = run(pieces_kernel, (keep, across(give)), [piece] * (span[1] - span[0]))
        returned += [swapped(sums[k - span[0]], 2 * k) for k in range(*span)]
    own_part, sibling_part = run(
        unpack_kernel,
        (own_place[:, None], sibling_place[:, None], *returned),
        [array((own_count, width), low)] * 2,
        flops=4 * own_count * own_count * width,
    )
    sibling_part = swapped(sibling_part, 1)
    slot_rows, grad_rows, actives, grad_pres = after(buffers, *sums)
    rows = 4 * capacity
    ffn_keep, ffn_give = run(
        ffn_kernel,
        (actives, weight_out),
        [array((chips, rows // 2, width), wide), array((chips, rows // 2, width), low)],
        flops=2 * chips * rows * width * hidden,
        grid=(chips,),
        in_specs=[
            pl.BlockSpec((1, rows, hidden), lambda i: (i, 0, 0)),
            pl.BlockSpec((hidden, width), lambda i: (0, 0)),
        ],
        out_specs=[pl.BlockSpec((1, rows // 2, width), lambda i: (i, 0, 0))] * 2,
    )
    ffn_sums = run(
        ffn_sum_kernel, (place, ffn_keep, across(ffn_give)), array((experts_in_all, capacity, width), low)
    )
    ffn_back = lax.all_to_all(ffn_sums, "fsdp", 0, 0, tiled=True)
    grad_rows, slot_rows = grad_rows.reshape(-1, width), slot_rows.reshape(-1, width)
    expert_out_grad = dot(actives.reshape(-1, hidden), grad_rows, TN)
    expert_in_grad = dot(slot_rows, grad_pres.reshape(-1, hidden), TN)

    grad_middle, grad_branch, grad_mine, grad_give, second_sums = run(
        middle_back_kernel,
        (own_part, sibling_part, middle, cotangent, second_gain, out_weight, other_out_weight),
        [
            array((own_count, width), wide),
            array((own_count, width), low),
            array((own_count, local_width), low),
            array((own_count, local_width), low),
            array((2, width), wide),
        ],
        flops=2 * own_count * width * width,
    )
    grad_more = across(grad_give)
    output_own, output_give = run(
        output_part_kernel,
        (grad_branch, attended_keep, attended_more),
        [array((width, local_width), wide), array((width, local_width), low)],
        flops=2 * own_count * width * width,
    )
    output_more = across(output_give)
    grad_projected = attend_back(
        place, projected, unreached, member, attended, totals, grad_mine, grad_more
    )

    first_give = run(
        first_give_kernel,
        (place, grad_projected, full_weight),
        array((own_count, width), low),
        flops=2 * own_count * width * 3 * local_width,
    )
    first_more = across(first_give)
    if in_kernel:
        block = array((2, chips // 2, 4, shard_rows, local_width), low)
        part_outs = [block, block]
    else:
        part_outs = [array((4, width, local_width), low), array((8, LANES), low)]
    part_keep, part_give = run(
        functools.partial(weight_part_kernel, chips if in_kernel else 0),
        (place, inputs, other_inputs, first_gain, first_bias, grad_projected, output_own, output_more),
        part_outs,
        flops=2 * tree_size * width * 3 * local_width,
        scratch_shapes=[
            pltpu.VMEM((tree_size, width), low),
            pltpu.VMEM((4, width, local_width), low),
        ],
    )
    if in_kernel:
        part_more = swapped(part_give, 1)
        quarter = array((chips // 2, 4, shard_rows, local_width), low)
        near, far = run(halves_kernel, (part_keep, part_more), [quarter, quarter])
        shape = (4, shard_rows, local_width)
        own_sum, *away = run(
            quarters_kernel,
            (near, swapped(far, 2)),
            [array(shape, wide)] + [array(shape, low)] * (chips // 2 - 1),
        )
        away = [swapped(away[k - 1], 4 * k) for k in range(1, chips // 2)]
        input_weight_grad, output_weight_grad = run(
            total_kernel, (own_sum, *away), [array((3, *shape[1:]), wide), array(shape[1:], wide)]
        )
    else:
        blocks = part_keep.reshape(4, experts_in_all, shard_rows, local_width).transpose(1, 0, 2, 3)
        summed = reduce_blocks(blocks, index, experts_in_all)
        input_weight_grad, output_weight_grad = summed[:3], summed[3]
    output_weight_grad = output_weight_grad.T
    first_own, first_sums = run(
        first_own_kernel,
        (place, grad_projected, full_weight, first_give, inputs, other_inputs),
        [array((own_count, width), wide), array((2, width), wide)],
        flops=2 * own_count * width * 3 * local_width,
    )
    norm_sums = jnp.concatenate([first_sums, second_sums])
    bit = 1
    while bit < experts_in_all:
        norm_sums = norm_sums + swapped(norm_sums, bit)
        bit *= 2
    norm_sums = norm_sums + across(norm_sums)
    input_grad = run(
        input_grad_kernel,
        (grad_middle, first_own, first_more, inputs, first_gain),
        array((own_count, width), wide),
    )
    out_block = run(
        out_kernel,
        (own_slot[:, None], ffn_back.reshape(slot_count, width), middle),
        array((own_count, width), low),
        flops=2 * own_count * slot_count * width,
    )
    return (
        out_block,
        input_grad,
        norm_sums[0],
        norm_sums[1],
        input_weight_grad,
        output_weight_grad,
        norm_sums[2],
        norm_sums[3],
        expert_in_grad[None],
        expert_out_grad[None],
    )


def solution(mesh):
    return jax.shard_map(
        shards,
        mesh=mesh,
        in_specs=(
            P(("fsdp", "tp"), None),
            P("fsdp"),
            P(),
            P("fsdp", None),
            P("fsdp", None),
            P(),
            P(),
            P(None, "fsdp", "tp"),
            P("tp", "fsdp"),
            P(),
            P(),
            P("fsdp", None, "tp"),
            P("fsdp", "tp", None),
            P(("fsdp", "tp"), None),
        ),
        out_specs=(
            P(("fsdp", "tp"), None),
            P(("fsdp", "tp"), None),
            P(),
            P(),
            P(None, "fsdp", "tp"),
            P("tp", "fsdp"),
            P(),
            P(),
            P("fsdp", None, "tp"),
            P("fsdp", "tp", None),
        ),
        check_vma=False,
    )
```

```python
import functools
import math

import jax
import jax.numpy as jnp
from jax import lax
from jax.experimental import pallas as pl
from jax.experimental.pallas import tpu as pltpu
from jax.sharding import PartitionSpec as P

HD = 64
LANES = 128

norm_eps = 1e-05
masked_score = -1e30
gelu_root = 0.7978845608028654
gelu_cubic = 0.044715
low = jnp.bfloat16
wide = jnp.float32

NN = (((1,), (0,)), ((), ()))
NT = (((1,), (1,)), ((), ()))
TN = (((0,), (0,)), ((), ()))


def dot(left, right, dims=NN):
    return lax.dot_general(left, right, dims, preferred_element_type=wide)


def gelu_both(values):
    squared = values * values
    tangent = jnp.tanh(values * (gelu_root + gelu_root * gelu_cubic * squared))
    half_up = 0.5 + 0.5 * tangent
    active = values * half_up
    slope = half_up + active * (1.0 - half_up) * (
        2.0 * gelu_root + 6.0 * gelu_root * gelu_cubic * squared
    )
    return active, slope


def normalize(values):
    average = jnp.mean(values, axis=-1, keepdims=True)
    centred = values - average
    inverse = lax.rsqrt(jnp.mean(centred * centred, axis=-1, keepdims=True) + norm_eps)
    return (centred * inverse, inverse)


def norm_back(upstream, normed, inverse, gain):
    scaled = upstream * gain
    centred_grad = (
        scaled
        - jnp.mean(scaled, axis=-1, keepdims=True)
        - normed * jnp.mean(scaled * normed, axis=-1, keepdims=True)
    )
    return inverse * centred_grad


def array(shape, kind):
    return jax.ShapeDtypeStruct(shape, kind)


def kept(shape, kind):
    return pltpu.HBM(shape, kind)


def size_of(x):
    return math.prod(x.shape) * jnp.dtype(x.dtype).itemsize


def run(kernel, operands, outs, flops=0, limit=32, first=(), mark=False, **more):
    if "in_specs" not in more:
        more["in_specs"] = [spec_of(x) for x in operands]
    operands = [in_hbm(x.values) if isinstance(x, Far) else x for x in operands]
    alone = not isinstance(outs, list)
    outs = [outs] if alone else list(outs)
    count, results = len(operands), len(outs)
    moved = sum(map(size_of, operands)) + sum(map(size_of, outs))
    first = tuple(first)
    more["in_specs"] = list(more["in_specs"]) + [pl.BlockSpec(memory_space=pl.ANY)] * len(first)
    if mark:
        outs.append(array((8, LANES), wide))
    if "out_specs" in more:
        more["out_specs"] = list(more["out_specs"])
        if mark:
            more["out_specs"].append(pl.BlockSpec((8, LANES), lambda *i: (0, 0)))

    def whole(*refs):
        end = count + len(first) + results
        if mark:
            refs[end][...] = jnp.zeros((8, LANES), wide)
        kernel(*refs[:count], *refs[count + len(first) : end], *refs[end + mark :])

    res = pl.pallas_call(
        whole,
        out_shape=outs,
        compiler_params=pltpu.CompilerParams(vmem_limit_bytes=limit << 20),
        cost_estimate=pl.CostEstimate(flops=int(flops), bytes_accessed=int(moved), transcendentals=0),
        **more,
    )(*operands, *first)
    return res[0] if alone and not mark else res


def in_hbm(x):
    return pltpu.with_memory_space_constraint(x, pltpu.HBM)


class Far:
    def __init__(self, values):
        self.values = values


def spec_of(x):
    if isinstance(x, Far):
        shape = x.values.shape
        return pl.BlockSpec(shape, lambda *i: (0,) * len(shape))
    scalar = x.ndim == 1 and x.dtype == jnp.int32
    return pl.BlockSpec(memory_space=pltpu.SMEM if scalar else pltpu.VMEM)


def project_kernel(
    chips, place_ref, own_ref, other_ref, gain_ref, bias_ref, gain2_ref, bias2_ref, mine_ref, sibling_ref,
    full_ref, last_ref, out_ref, scale_ref
):
    place, side = place_ref[0], place_ref[1]
    for n, ref in enumerate((gain_ref, bias_ref, gain2_ref, bias2_ref)):
        scale_ref[n : n + 1] = ref[...].reshape(1, ref.shape[0])
    if chips:
        rows = mine_ref.shape[2]
        for k in range(chips):
            for ref, source in ((mine_ref, place ^ (2 * k)), (sibling_ref, place ^ (2 * k + 1))):
                block = pl.ds(pl.multiple_of(source * rows, rows), rows)
                full_ref[:, block, :] = ref[k, :3]
                last_ref[block, :] = ref[k, 3]
    else:
        full_ref[...] = mine_ref[:3]
        last_ref[...] = mine_ref[3]
    count, width = own_ref.shape[0], mine_ref.shape[-1]
    for ref, first in ((own_ref, side * count), (other_ref, (1 - side) * count)):
        hat, _ = normalize(ref[...].astype(wide))
        normed = (hat * scale_ref[0:1] + scale_ref[1:2]).astype(low)
        for n in range(3):
            out_ref[pl.ds(pl.multiple_of(first, count), count), n * width : (n + 1) * width] = dot(
                normed, full_ref[n]
            ).astype(low)


def turned_kernel(place_ref, own_ref, other_ref, scale_ref, out_ref):
    side = place_ref[1]
    count = own_ref.shape[0]
    for ref, first in ((own_ref, side * count), (other_ref, (1 - side) * count)):
        hat, _ = normalize(ref[...].astype(wide))
        normed = (hat * scale_ref[0:1] + scale_ref[1:2]).T
        out_ref[:, pl.ds(pl.multiple_of(first, count), count)] = normed.astype(low)


def attend_kernel(block, place_ref, q_ref, k_ref, v_ref, unreached_ref, member_ref, out_ref, total_ref, keep_ref, give_ref):
    side = place_ref[1]
    rows = q_ref.shape[0]
    lane = lax.broadcasted_iota(jnp.int32, (1, LANES), 1)
    first_head = lane < HD
    ones = jnp.ones((rows, LANES), low)
    keys = jnp.concatenate([k_ref[...], member_ref[...]], axis=1)
    values = jnp.concatenate([v_ref[...], ones], axis=1)
    causal = lax.broadcasted_iota(jnp.int32, (block, block), 1) <= lax.broadcasted_iota(
        jnp.int32, (block, block), 0
    )
    for start in range(0, rows, block):
        stop = start + block
        query = q_ref[start:stop] * HD**-0.5
        unreached = unreached_ref[start:stop]
        halves = []
        for own in (first_head, ~first_head):
            left = jnp.concatenate([jnp.where(own, query, 0).astype(low), unreached], axis=1)
            scores = dot(left, keys[:stop], NT)
            near = jnp.where(causal, scores[:, start:], masked_score)
            top = jnp.max(near, axis=1, keepdims=True)
            if start:
                far = scores[:, :start]
                top = jnp.maximum(top, jnp.max(far, axis=1, keepdims=True))
                weights = jnp.concatenate(
                    [jnp.exp(far - top).astype(low), jnp.exp(near - top).astype(low)], axis=1
                )
            else:
                weights = jnp.exp(near - top).astype(low)
            sums = dot(weights, values[:stop], NN)
            total = sums[:, LANES:]
            halves.append((sums[:, :LANES] / total, top + jnp.log(total)))
        out_ref[start:stop] = jnp.where(first_head, halves[0][0], halves[1][0]).astype(low)
        total_ref[start:stop] = jnp.where(first_head, halves[0][1], halves[1][1])
    half = rows // 2
    keep_ref[...] = out_ref[pl.ds(pl.multiple_of(side * half, half), half)]
    give_ref[...] = out_ref[pl.ds(pl.multiple_of((1 - side) * half, half), half)]


def attend(place, projected, unreached, member, block=256):
    rows, width = projected.shape
    pairs = width // (3 * LANES)

    def part(n, height=rows):
        return pl.BlockSpec((height, LANES), lambda p: (0, n * pairs + p))

    fixed = pl.BlockSpec((rows, LANES), lambda p: (0, 0))
    return run(
        functools.partial(attend_kernel, block),
        (place, in_hbm(projected), in_hbm(projected), in_hbm(projected), unreached, member),
        [
            kept((rows, width // 3), low),
            kept((rows, width // 3), wide),
            array((rows // 2, width // 3), low),
            array((rows // 2, width // 3), low),
        ],
        flops=12e9,
        grid=(pairs,),
        in_specs=[spec_of(place), part(0), part(1), part(2), fixed, fixed],
        out_specs=[part(0), part(0), part(0, rows // 2), part(0, rows // 2)],
    )


def attend_back_kernel(
    block, place_ref, q_ref, k_ref, v_ref, unreached_ref, member_ref, out_ref, total_ref, mine_ref, more_ref, res_ref, dk, dv, grads
):
    side = place_ref[1]
    rows = q_ref.shape[0]
    half = rows // 2
    grads[pl.ds(pl.multiple_of(side * half, half), half)] = mine_ref[...]
    grads[pl.ds(pl.multiple_of((1 - side) * half, half), half)] = more_ref[...]
    lane = lax.broadcasted_iota(jnp.int32, (1, LANES), 1)
    first_head = lane < HD
    keys = jnp.concatenate([k_ref[...], member_ref[...]], axis=1)
    causal = lax.broadcasted_iota(jnp.int32, (block, block), 1) <= lax.broadcasted_iota(
        jnp.int32, (block, block), 0
    )
    for start in range(rows - block, -1, -block):
        stop = start + block
        query = q_ref[start:stop] * HD**-0.5
        unreached = unreached_ref[start:stop]
        grad = grads[start:stop]
        both = grad.astype(wide) * out_ref[start:stop].astype(wide)
        query_halves = []
        key_terms = []
        value_terms = []
        for head, own in enumerate((first_head, ~first_head)):
            q_own = jnp.where(own, query, 0).astype(low)
            g_own = jnp.where(own, grad, 0).astype(low)
            scores = dot(jnp.concatenate([q_own, unreached], axis=1), keys[:stop], NT)
            total = total_ref[start:stop, HD * head : HD * head + 1]
            centre = jnp.sum(jnp.where(own, both, 0.0), axis=1, keepdims=True)
            near = jnp.exp(jnp.where(causal, scores[:, start:], masked_score) - total)
            if start:
                weights = jnp.concatenate([jnp.exp(scores[:, :start] - total), near], axis=1)
            else:
                weights = near
            gains = dot(g_own, v_ref[:stop], NT)
            slopes = (weights * (gains - centre)).astype(low)
            query_halves.append(dot(slopes, k_ref[:stop], NN))
            key_terms.append(dot(slopes, q_own, TN))
            value_terms.append(dot(weights.astype(low), g_own, TN))
        res_ref[0, start:stop] = (
            jnp.where(first_head, query_halves[0], query_halves[1]) * HD**-0.5
        ).astype(low)
        if stop == rows:
            dk[...] = key_terms[0] + key_terms[1]
            dv[...] = value_terms[0] + value_terms[1]
        else:
            dk[:stop] += key_terms[0] + key_terms[1]
            dv[:stop] += value_terms[0] + value_terms[1]
    res_ref[1] = dk[...].astype(low)
    res_ref[2] = dv[...].astype(low)


def attend_back(place, projected, unreached, member, out, total, mine, more, block=256, first=()):
    rows, width = projected.shape
    pairs = width // (3 * LANES)

    def part(n, height=rows):
        return pl.BlockSpec((height, LANES), lambda p: (0, n * pairs + p))

    fixed = pl.BlockSpec((rows, LANES), lambda p: (0, 0))
    return run(
        functools.partial(attend_back_kernel, block),
        (
            place, in_hbm(projected), in_hbm(projected), in_hbm(projected), unreached, member,
            in_hbm(out), in_hbm(total), mine, more,
        ),
        [kept((3, rows, width // 3), low)],
        flops=24e9,
        first=first,
        grid=(pairs,),
        in_specs=[spec_of(place), part(0), part(1), part(2), fixed, fixed, part(0), part(0)]
        + [part(0, rows // 2)] * 2,
        out_specs=[pl.BlockSpec((3, rows, LANES), lambda p: (0, 0, p))],
        scratch_shapes=[pltpu.VMEM((rows, LANES), wide)] * 2 + [pltpu.VMEM((rows, LANES), low)],
    )


def branch_kernel(keep_ref, more_ref, weight_ref, other_ref, residual_ref, scale_ref, middle_ref, normed_ref):
    branch = dot(keep_ref[...], weight_ref[...], NT) + dot(more_ref[...], other_ref[...], NT)
    middle = residual_ref[...].astype(wide) + branch
    middle_ref[...] = middle
    hat, _ = normalize(middle)
    normed_ref[...] = (hat * scale_ref[2:3] + scale_ref[3:4]).astype(low)


def pack_kernel(own_ref, sibling_ref, own_slot_ref, sibling_slot_ref, *out_refs):
    capacity = out_refs[0].shape[1]
    slots = len(out_refs) * capacity
    for source, (ref, slot_ref) in enumerate(
        ((own_ref, own_slot_ref), (sibling_ref, sibling_slot_ref))
    ):
        place = lax.broadcasted_iota(jnp.int32, (slots, ref.shape[0]), 0)
        chooser = (place == slot_ref[...]).astype(wide).astype(low)
        packed = dot(chooser, ref[...]).astype(low)
        for k, out_ref in enumerate(out_refs):
            out_ref[source] = packed[k * capacity : (k + 1) * capacity]


def straight_pack_kernel(values_ref, slot_ref, out_ref):
    place = lax.broadcasted_iota(jnp.int32, (out_ref.shape[0], values_ref.shape[0]), 0)
    chooser = (place == slot_ref[...]).astype(wide).astype(low)
    out_ref[...] = dot(chooser, values_ref[...]).astype(low)


def expert_kernel(first, count, chunk, place_ref, in_ref, out_ref, grads_ref, more_grads_ref, *refs):
    pieces, more_pieces = refs[:count], refs[count : 2 * count]
    x_ref, ct_ref, active_ref, slope_ref, keep_ref, give_ref = refs[-6:]
    step = pl.program_id(0)
    place = place_ref[0]
    capacity = pieces[0].shape[1]
    rows = 2 * capacity
    for k in range(count):

        @pl.when(step == k)
        def _(k=k):
            for c in range(2):
                x_ref[0, c * capacity : (c + 1) * capacity] = pieces[k][c]
                x_ref[0, rows + c * capacity : rows + (c + 1) * capacity] = more_pieces[k][c]

    source = place ^ (2 * (first + step))
    for c in range(2):
        ct_ref[0, c * capacity : (c + 1) * capacity] = grads_ref[source ^ c]
        ct_ref[0, rows + c * capacity : rows + (c + 1) * capacity] = more_grads_ref[source ^ c]
    x = x_ref[0]
    ct = ct_ref[0]
    total = None
    for start in range(0, in_ref.shape[1], chunk):
        stop = start + chunk
        pre = dot(x, in_ref[:, start:stop])
        gains = dot(ct, out_ref[start:stop], NT)
        active, slope = gelu_both(pre)
        active_ref[0, :, start:stop] = active.astype(low)
        grad_pre = (gains * slope).astype(low)
        slope_ref[0, :, start:stop] = grad_pre
        term = dot(grad_pre, in_ref[:, start:stop], NT)
        total = term if total is None else total + term
    keep_ref[0] = total[:rows]
    give_ref[0] = total[rows:].astype(low)


def expert_group(
    place, weight_in, weight_out, grads, more_grads, pieces, more_pieces, buffers, span, chips, earlier
):
    first, stop = span
    count = stop - first
    capacity, width = pieces[0].shape[1:]
    hidden = weight_in.shape[1]
    rows = 4 * capacity
    operands = [place, weight_in, weight_out, grads, more_grads, *pieces, *more_pieces]
    specs = [spec_of(place)] + [
        pl.BlockSpec(x.shape, lambda i, n=x.ndim: (0,) * n) for x in operands[1:]
    ]
    aliases = {}
    if buffers is not None:
        aliases = {len(operands) + n: n for n in range(4)}
        operands += buffers
        specs += [pl.BlockSpec(memory_space=pl.ANY)] * 4

    def block(height, size, offset):
        return pl.BlockSpec((1, height, size), lambda i: (offset + i, 0, 0))

    res = run(
        functools.partial(expert_kernel, first, count, min(512, hidden)),
        operands,
        [
            kept((chips, rows, width), low),
            kept((chips, rows, width), low),
            kept((chips, rows, hidden), low),
            kept((chips, rows, hidden), low),
            array((count, rows // 2, width), wide),
            array((count, rows // 2, width), low),
        ],
        flops=6 * count * rows * width * hidden,
        grid=(count,),
        in_specs=specs,
        out_specs=[
            block(rows, width, first),
            block(rows, width, first),
            block(rows, hidden, first),
            block(rows, hidden, first),
            block(rows // 2, width, 0),
            block(rows // 2, width, 0),
        ],
        input_output_aliases=aliases,
        first=earlier,
    )
    return res[:4], res[4], res[5]


def pieces_kernel(keep_ref, more_ref, *out_refs):
    capacity = out_refs[0].shape[1]
    for k, out_ref in enumerate(out_refs):
        total = (keep_ref[k] + more_ref[k].astype(wide)).astype(low)
        for c in range(2):
            out_ref[c] = total[c * capacity : (c + 1) * capacity]


def unpack_kernel(own_slot_ref, sibling_slot_ref, *refs):
    pieces, (own_ref, sibling_ref) = refs[:-2], refs[-2:]
    capacity = pieces[0].shape[1]
    slots = len(pieces) * capacity
    for source, (slot_ref, out_ref) in enumerate(
        ((own_slot_ref, own_ref), (sibling_slot_ref, sibling_ref))
    ):
        place = lax.broadcasted_iota(jnp.int32, (slots, out_ref.shape[0]), 0)
        chooser = (place == slot_ref[...]).astype(wide).astype(low)
        values = jnp.concatenate([piece[source] for piece in pieces], axis=0)
        out_ref[...] = dot(chooser, values, TN).astype(low)


def ffn_kernel(active_ref, weight_ref, keep_ref, give_ref):
    values = dot(active_ref[0], weight_ref[...])
    rows = keep_ref.shape[1]
    keep_ref[0] = values[:rows]
    give_ref[0] = values[rows:].astype(low)


def product_kernel(left_ref, right_ref, out_ref):
    left, right = left_ref[...], right_ref[...]
    out_ref[...] = dot(
        left.reshape(-1, left.shape[-1]), right.reshape(-1, right.shape[-1]), TN
    )


def ffn_sum_kernel(place_ref, keep_ref, more_ref, out_ref):
    place = place_ref[0]
    capacity = out_ref.shape[1]
    for k in range(keep_ref.shape[0]):
        total = (keep_ref[k] + more_ref[k].astype(wide)).astype(low)
        for c in range(2):
            out_ref[place ^ (2 * k + c)] = total[c * capacity : (c + 1) * capacity]


def out_kernel(slot_ref, values_ref, middle_ref, out_ref):
    place = lax.broadcasted_iota(jnp.int32, (values_ref.shape[0], out_ref.shape[0]), 0)
    chooser = (place == slot_ref[...]).astype(wide).astype(low)
    out_ref[...] = (middle_ref[...] + dot(chooser, values_ref[...], TN)).astype(low)


def middle_back_kernel(
    own_ref, more_ref, middle_ref, ct_ref, scale_ref, weight_ref, other_ref,
    grad_ref, branch_ref, mine_ref, give_ref, sums_ref,
):
    grad_second = own_ref[...].astype(wide) + more_ref[...].astype(wide)
    hat, inverse = normalize(middle_ref[...])
    sums_ref[0:1] = jnp.sum(grad_second * hat, axis=0, keepdims=True)
    sums_ref[1:2] = jnp.sum(grad_second, axis=0, keepdims=True)
    grad_middle = ct_ref[...].astype(wide) + norm_back(grad_second, hat, inverse, scale_ref[2:3])
    grad_ref[...] = grad_middle
    branch = grad_middle.astype(low)
    branch_ref[...] = branch
    give_ref[...] = dot(branch, other_ref[...]).astype(low)
    mine_ref[...] = dot(branch, weight_ref[...]).astype(low)


def output_part_kernel(branch_ref, keep_ref, more_ref, own_ref, give_ref):
    give_ref[...] = dot(branch_ref[...], more_ref[...], TN).astype(low)
    own_ref[...] = dot(branch_ref[...], keep_ref[...], TN)


def first_kernel(
    place_ref, grads_ref, full_ref, own_in_ref, other_in_ref, second_ref, give_ref, own_ref, sums_ref
):
    half = own_ref.shape[0]
    side = place_ref[1]
    sums = None
    for ref, out_ref, first in ((other_in_ref, give_ref, 1 - side), (own_in_ref, own_ref, side)):
        rows = pl.ds(pl.multiple_of(first * half, half), half)
        total = None
        for n in range(3):
            term = dot(grads_ref[n, rows], full_ref[n], NT)
            total = term if total is None else total + term
        out_ref[...] = total.astype(out_ref.dtype)
        hat, _ = normalize(ref[...].astype(wide))
        more = [jnp.sum(total * hat, axis=0, keepdims=True), jnp.sum(total, axis=0, keepdims=True)]
        sums = more if sums is None else [x + y for x, y in zip(sums, more)]
    sums_ref[0:1] = sums[0]
    sums_ref[1:2] = sums[1]
    sums_ref[2:4] = second_ref[...]


def weight_part_kernel(chips, place_ref, turned_ref, grads_ref, part_ref, more_ref, keep_ref, give_ref, parts):
    place = place_ref[0]
    for n in range(3):
        parts[n] = dot(turned_ref[...], grads_ref[n]).astype(low)
    parts[3] = (part_ref[...] + more_ref[...].astype(wide)).astype(low)
    if chips:
        rows = keep_ref.shape[3]
        for k in range(chips):
            target = place ^ (2 * k)
            keep_ref[k % 2, k // 2] = parts[:, pl.ds(pl.multiple_of(target * rows, rows), rows)]
            target = target ^ 1
            give_ref[k % 2, k // 2] = parts[:, pl.ds(pl.multiple_of(target * rows, rows), rows)]
    else:
        keep_ref[...] = parts[...]
        give_ref[...] = jnp.zeros(give_ref.shape, low)


def spread(sums):
    half = sums.shape[1] // 2
    rows = []
    rest = sums
    for _ in range(3):
        term = rest.astype(low).astype(wide)
        rest = rest - term
        rows += [term[:, :half], term[:, half:]]
    rows.append(jnp.zeros((8, half), wide))
    return jnp.concatenate(rows, axis=0).astype(low)


def gathered(rows):
    rows = rows.astype(wide)
    terms = [
        jnp.concatenate([rows[8 * n : 8 * n + 4], rows[8 * n + 4 : 8 * n + 8]], axis=1)
        for n in range(3)
    ]
    return (terms[0] + terms[1]) + terms[2]


def halves_kernel(keep_ref, more_ref, sums_ref, more_sums_ref, near_ref, far_ref, out_sums_ref):
    count = near_ref.shape[0]
    sums = sums_ref[...] + more_sums_ref[...]
    out_sums_ref[...] = sums
    far_ref[count:] = spread(sums)
    for side, ref in ((0, near_ref), (1, far_ref)):
        total = keep_ref[side].astype(wide) + more_ref[side].astype(wide)
        ref[:count] = total.reshape(count, total.shape[-1]).astype(low)


def quarters_kernel(near_ref, more_ref, sums_ref, own_ref, out_sums_ref, *out_refs):
    rows = own_ref.shape[0]
    sums = sums_ref[...] + gathered(more_ref[near_ref.shape[0] :])
    out_sums_ref[...] = sums
    packed = spread(sums)
    for n, ref in enumerate((own_ref, *out_refs)):
        block = slice(n * rows, (n + 1) * rows)
        total = near_ref[block].astype(wide) + more_ref[block].astype(wide)
        ref[:rows] = total.astype(ref.dtype)
        if n:
            ref[rows:] = packed


def total_kernel(own_ref, sums_ref, *refs):
    aways, (in_ref, out_ref, out_sums_ref) = refs[:-3], refs[-3:]
    rows = out_ref.shape[0]
    sums = [sums_ref[...]]
    total = own_ref[...]
    for ref in aways:
        total = total + ref[: own_ref.shape[0]].astype(wide)
        sums.append(gathered(ref[own_ref.shape[0] :]))
    while len(sums) > 1:
        sums = [x + y for x, y in zip(sums[0::2], sums[1::2])]
    out_sums_ref[...] = sums[0]
    for n in range(3):
        in_ref[n] = total[n * rows : (n + 1) * rows]
    out_ref[...] = total[3 * rows :]


def input_grad_kernel(grad_ref, own_ref, more_ref, input_ref, scale_ref, out_ref):
    hat, inverse = normalize(input_ref[...].astype(wide))
    upstream = own_ref[...] + more_ref[...].astype(wide)
    out_ref[...] = grad_ref[...] + norm_back(upstream, hat, inverse, scale_ref[0:1])


def across(values):
    return lax.ppermute(values, "tp", [(0, 1), (1, 0)])


def swapped(values, offset):
    if offset == 0:
        return values
    count = lax.axis_size("fsdp")
    return lax.ppermute(values, "fsdp", [(i, i ^ offset) for i in range(count)])


def reduce_blocks(blocks, index, count):
    bit = 0
    part = blocks
    while count > 1:
        mine = (index >> bit) & 1
        split = part.reshape(count // 2, 2, *blocks.shape[1:])
        keep = lax.dynamic_index_in_dim(split, mine, 1, keepdims=False)
        give = lax.dynamic_index_in_dim(split, 1 - mine, 1, keepdims=False)
        got = swapped(give.astype(low), 1 << bit)
        part = keep.astype(wide) + got.astype(wide)
        if count > 2:
            part = part.astype(low)
        count //= 2
        bit += 1
    return part[0]


def tree_masks(lengths, parents, tree_size):
    segment_count = lengths.shape[0]
    number = jnp.arange(segment_count, dtype=jnp.int32)
    segment_end = jnp.sum(jnp.where(number[None, :] <= number[:, None], lengths[None, :], 0), axis=1)
    starts = segment_end - lengths
    position = jnp.arange(tree_size, dtype=jnp.int32)
    member = (
        (position[:, None] >= starts[None, :]) & (position[:, None] < segment_end[None, :])
    ).astype(wide)
    closure = jnp.maximum(
        jnp.eye(segment_count, dtype=wide), (parents[:, None] == number[None, :]).astype(wide)
    )
    steps = 1
    while steps < segment_count:
        closure = jnp.minimum(jnp.dot(closure, closure), 1.0)
        steps *= 2
    unreached = (1.0 - jnp.dot(member, closure)) * masked_score
    padding = ((0, 0), (0, LANES - segment_count))
    return jnp.pad(unreached, padding).astype(low), jnp.pad(member, padding).astype(low)


def shards(
    inputs,
    token_ids,
    hash_table,
    segment_lengths,
    segment_parents,
    first_gain,
    first_bias,
    input_weight,
    output_weight,
    second_gain,
    second_bias,
    expert_in,
    expert_out,
    cotangent,
):
    own_count, width = inputs.shape
    experts_in_all = lax.axis_size("fsdp")
    tree_size = token_ids.shape[0]
    capacity = 2 * own_count // experts_in_all
    local_width = input_weight.shape[2]
    chips = experts_in_all // 2
    shard_rows = input_weight.shape[1]
    hidden = expert_in.shape[2]
    index = lax.axis_index("fsdp")
    side = lax.axis_index("tp")
    place = jnp.stack([index, side]).astype(jnp.int32)
    in_kernel = shard_rows % 16 == 0
    scales = [first_gain, first_bias, second_gain, second_bias]

    other_inputs = across(inputs)
    shard = jnp.concatenate([input_weight, output_weight.T[None]])
    pieces = {0: shard}
    for k in range(2, chips, 2):
        pieces[k] = swapped(shard, 2 * k)
    for k in range(1, chips, 2):
        pieces[k] = swapped(pieces[k - 1], 2)
    mine = jnp.stack([pieces[k] for k in range(chips)])
    sibling = swapped(mine, 1)

    own_ids = lax.dynamic_slice_in_dim(token_ids, side * own_count, own_count, 0)
    table = hash_table.reshape(-1, LANES).astype(low)
    row_hot = (own_ids[:, None] // LANES == jnp.arange(table.shape[0])[None, :]).astype(low)
    lane_hot = own_ids[:, None] % LANES == jnp.arange(LANES)[None, :]
    experts = jnp.sum(jnp.where(lane_hot, dot(row_hot, table), 0.0), axis=1).astype(jnp.int32)
    hot = (experts[:, None] == jnp.arange(experts_in_all)[None, :]).astype(low)
    earlier = (jnp.arange(own_count)[:, None] > jnp.arange(own_count)[None, :]).astype(low)
    rank = jnp.sum(dot(earlier, hot) * hot.astype(wide), axis=1).astype(jnp.int32)
    own_slot = experts * capacity + rank
    sibling_slot = swapped(own_slot, 1)

    def chip_slot(slot):
        offset = (slot // capacity) ^ index
        return jnp.where(offset & 1 == 0, (offset >> 1) * capacity + slot % capacity, -1)

    own_place, sibling_place = chip_slot(own_slot), chip_slot(sibling_slot)

    slot_count = experts_in_all * capacity
    packed_grads = run(
        straight_pack_kernel,
        (cotangent, own_slot[None]),
        kept((slot_count, width), low),
        flops=2 * slot_count * own_count * width,
        first=(mine, other_inputs),
    )
    slot_grads = lax.all_to_all(
        packed_grads.reshape(experts_in_all, capacity, width), "fsdp", 0, 0, tiled=True
    )
    more_slot_grads = across(slot_grads)

    if in_kernel:
        weights = (mine, sibling)
    else:
        both = jnp.stack([mine, sibling], 1)
        both = both.reshape(experts_in_all, 4, shard_rows, local_width)
        full = jnp.concatenate(
            [lax.dynamic_index_in_dim(both, index ^ n, 0, False) for n in range(experts_in_all)], axis=1
        )
        weights = (full, full[:1, :16])
    full_weight, out_weight, projected, scales = run(
        functools.partial(project_kernel, chips if in_kernel else 0),
        (place, inputs, other_inputs, *scales, *weights),
        [
            kept((3, width, local_width), low),
            array((width, local_width), low),
            kept((tree_size, 3 * local_width), low),
            array((4, width), wide),
        ],
        flops=2 * tree_size * width * 3 * local_width,
    )
    other_out_weight = across(out_weight)
    unreached, member = tree_masks(segment_lengths[0], segment_parents[0], tree_size)
    attended, totals, attended_keep, attended_give = attend(place, projected, unreached, member)
    attended_more = across(attended_give)
    middle, second_normed = run(
        branch_kernel,
        (attended_keep, attended_more, out_weight, other_out_weight, inputs, scales),
        [kept((own_count, width), wide), array((own_count, width), low)],
        flops=2 * own_count * width * width,
    )

    sibling_normed = swapped(second_normed, 1)
    piece = array((2, capacity, width), low)
    packed = run(
        pack_kernel,
        (second_normed, sibling_normed, own_place[None], sibling_place[None]),
        [piece] * chips,
        first=(slot_grads,),
        flops=4 * own_count * own_count * width,
    )
    quarter = chips // 4
    near, next_near, far, next_far = [(n * quarter, (n + 1) * quarter) for n in range(4)]
    arrived = {}
    for span in (far, near, next_near):
        for k in range(*span):
            arrived[k] = swapped(packed[k], 2 * k)
    for k in range(*next_far):
        arrived[k] = swapped(packed[k], 2 * k)
    spans = (near, far, next_far, next_near)
    more_arrived = {k: across(arrived[k]) for span in spans for k in range(*span)}

    weight_in, weight_out = expert_in[0], expert_out[0]
    buffers = None
    returned = {}
    done = []
    back = []
    for turn, span in enumerate(spans):
        own_pieces = [arrived[k] for k in range(*span)]
        buffers, keep, give = expert_group(
            place, weight_in, weight_out, slot_grads, more_slot_grads,
            own_pieces, [more_arrived[k] for k in range(*span)], buffers, span, chips,
            [more_arrived[k] for later in spans[turn + 1 : turn + 2] for k in range(*later)]
            + ([arrived[k] for k in range(1, chips)] if turn == 0 else []),
        )
        *sums, token = run(pieces_kernel, (keep, across(give)), [piece] * quarter, mark=True)
        done.append(token)
        for k in range(*span):
            returned[k] = swapped(sums[k - span[0]], 2 * k)
        back.append([returned[k] for k in range(*span)])
    slot_rows, grad_rows, actives, grad_pres = buffers
    rows = 4 * capacity
    ffn_keep, ffn_give, ffn_done = run(
        ffn_kernel,
        (in_hbm(actives), weight_out),
        [array((chips, rows // 2, width), wide), array((chips, rows // 2, width), low)],
        flops=2 * chips * rows * width * hidden,
        first=done[2:3],
        mark=True,
        grid=(chips,),
        in_specs=[
            pl.BlockSpec((1, rows, hidden), lambda i: (i, 0, 0)),
            pl.BlockSpec((hidden, width), lambda i: (0, 0)),
        ],
        out_specs=[pl.BlockSpec((1, rows // 2, width), lambda i: (i, 0, 0))] * 2,
    )
    ffn_more = across(ffn_give)
    tile = min(512, hidden)
    stripe = pl.BlockSpec((chips, rows, tile), lambda i: (0, 0, i))
    fixed = pl.BlockSpec((chips, rows, width), lambda i: (0, 0, 0))
    expert_out_grad, out_done = run(
        product_kernel,
        (in_hbm(actives), in_hbm(grad_rows)),
        array((hidden, width), wide),
        flops=2 * chips * rows * width * hidden,
        first=(ffn_done, done[3], *back[0], *back[1]),
        mark=True,
        grid=(hidden // tile,),
        in_specs=[stripe, fixed],
        out_specs=[pl.BlockSpec((tile, width), lambda i: (i, 0))],
    )
    expert_in_grad, in_done = run(
        product_kernel,
        (in_hbm(slot_rows), in_hbm(grad_pres)),
        array((width, hidden), wide),
        flops=2 * chips * rows * width * hidden,
        first=(out_done, *back[2]),
        mark=True,
        grid=(hidden // tile,),
        in_specs=[fixed, stripe],
        out_specs=[pl.BlockSpec((width, tile), lambda i: (0, i))],
    )
    own_part, sibling_part = run(
        unpack_kernel,
        (own_place[None], sibling_place[None], *[returned[k] for k in range(chips)]),
        [array((own_count, width), low)] * 2,
        first=(in_done,),
        flops=4 * own_count * own_count * width,
    )
    sibling_part = swapped(sibling_part, 1)
    ffn_sums, sums_done = run(
        ffn_sum_kernel,
        (place, ffn_keep, ffn_more),
        kept((experts_in_all, capacity, width), low),
        mark=True,
    )
    ffn_back = lax.all_to_all(ffn_sums, "fsdp", 0, 0, tiled=True)

    grad_middle, grad_branch, grad_mine, grad_give, second_sums = run(
        middle_back_kernel,
        (
            own_part, sibling_part, Far(middle), Far(cotangent), scales,
            Far(out_weight), Far(other_out_weight),
        ),
        [
            kept((own_count, width), wide),
            array((own_count, width), low),
            array((own_count, local_width), low),
            array((own_count, local_width), low),
            array((2, width), wide),
        ],
        first=(sums_done,),
        flops=2 * own_count * width * width,
    )
    grad_more = across(grad_give)
    output_own, output_give, output_done = run(
        output_part_kernel,
        (grad_branch, Far(attended_keep), Far(attended_more)),
        [kept((width, local_width), wide), array((width, local_width), low)],
        mark=True,
        flops=2 * own_count * width * width,
    )
    output_more = across(output_give)
    turned, turned_done = run(
        turned_kernel,
        (place, Far(inputs), Far(other_inputs), scales),
        kept((width, tree_size), low),
        mark=True,
    )
    (grad_projected,) = attend_back(
        place, projected, unreached, member, attended, totals, grad_mine, grad_more,
        first=(turned_done, output_done),
    )

    first_give, first_own, norm_sums, give_done = run(
        first_kernel,
        (
            place, Far(grad_projected), Far(full_weight), Far(inputs), Far(other_inputs), second_sums,
        ),
        [array((own_count, width), low), array((own_count, width), wide), array((4, width), wide)],
        mark=True,
        first=(ffn_back,),
        flops=2 * tree_size * width * 3 * local_width,
    )
    norm_more = across(norm_sums)
    norm_sums = norm_sums + norm_more
    first_more = across(first_give)
    if in_kernel:
        block = array((2, chips // 2, 4, shard_rows, local_width), low)
        part_outs = [block, block]
    else:
        part_outs = [array((4, width, local_width), low), array((8, LANES), low)]
    part_keep, part_give, part_done = run(
        functools.partial(weight_part_kernel, chips if in_kernel else 0),
        (place, Far(turned), Far(grad_projected), Far(output_own), output_more),
        part_outs,
        mark=True,
        first=(give_done, norm_more),
        flops=2 * tree_size * width * 3 * local_width,
        scratch_shapes=[pltpu.VMEM((4, width, local_width), low)],
    )
    if in_kernel:
        part_more = swapped(part_give, 1)
        rows = 4 * shard_rows
        near_sum, far_sum, norm_sums = run(
            halves_kernel,
            (part_keep, part_more, norm_sums, swapped(norm_sums, 1)),
            [
                array((chips // 2 * rows, local_width), low),
                array((chips // 2 * rows + 32, local_width), low),
                array((4, width), wide),
            ],
        )
        own_sum, norm_sums, *away = run(
            quarters_kernel,
            (near_sum, swapped(far_sum, 2), norm_sums),
            [array((rows, local_width), wide), array((4, width), wide)]
            + [array((rows + 32, local_width), low)] * (chips // 2 - 1),
            first=(first_more,),
        )
        away = [swapped(away[k - 1], 4 * k) for k in range(1, chips // 2)]
    else:
        blocks = part_keep.reshape(4, experts_in_all, shard_rows, local_width).transpose(1, 0, 2, 3)
        summed = reduce_blocks(blocks, index, experts_in_all)
        bit = 1
        while bit < experts_in_all:
            norm_sums = norm_sums + swapped(norm_sums, bit)
            bit *= 2
    input_grad, input_done = run(
        input_grad_kernel,
        (Far(grad_middle), first_own, first_more, Far(inputs), scales),
        array((own_count, width), wide),
        mark=True,
    )
    out_block, out_done = run(
        out_kernel,
        (own_slot[None], ffn_back.reshape(slot_count, width), Far(middle)),
        array((own_count, width), low),
        mark=True,
        flops=2 * own_count * slot_count * width,
    )
    if in_kernel:
        input_weight_grad, output_weight_grad, norm_sums = run(
            total_kernel,
            (own_sum, norm_sums, *away),
            [
                array((3, shard_rows, local_width), wide),
                array((shard_rows, local_width), wide),
                array((4, width), wide),
            ],
            first=(input_done, out_done),
        )
    else:
        input_weight_grad, output_weight_grad = summed[:3], summed[3]
    output_weight_grad = output_weight_grad.T
    return (
        out_block,
        input_grad,
        norm_sums[0],
        norm_sums[1],
        input_weight_grad,
        output_weight_grad,
        norm_sums[2],
        norm_sums[3],
        expert_in_grad[None],
        expert_out_grad[None],
    )


def solution(mesh):
    return jax.shard_map(
        shards,
        mesh=mesh,
        in_specs=(
            P(("fsdp", "tp"), None),
            P("fsdp"),
            P(),
            P("fsdp", None),
            P("fsdp", None),
            P(),
            P(),
            P(None, "fsdp", "tp"),
            P("tp", "fsdp"),
            P(),
            P(),
            P("fsdp", None, "tp"),
            P("fsdp", "tp", None),
            P(("fsdp", "tp"), None),
        ),
        out_specs=(
            P(("fsdp", "tp"), None),
            P(("fsdp", "tp"), None),
            P(),
            P(),
            P(None, "fsdp", "tp"),
            P("tp", "fsdp"),
            P(),
            P(),
            P("fsdp", None, "tp"),
            P("fsdp", "tp", None),
        ),
        check_vma=False,
    )
```

```python
import functools
import math

import jax
import jax.numpy as jnp
from jax import lax
from jax.experimental import pallas as pl
from jax.experimental.pallas import tpu as pltpu
from jax.sharding import PartitionSpec as P

HD = 64
LANES = 128

norm_eps = 1e-05
masked_score = -1e30
gelu_root = 0.7978845608028654
gelu_cubic = 0.044715
low = jnp.bfloat16
wide = jnp.float32

NN = (((1,), (0,)), ((), ()))
NT = (((1,), (1,)), ((), ()))
TN = (((0,), (0,)), ((), ()))


def dot(left, right, dims=NN):
    return lax.dot_general(left, right, dims, preferred_element_type=wide)


def gelu_both(values):
    squared = values * values
    tangent = jnp.tanh(values * (gelu_root + gelu_root * gelu_cubic * squared))
    half_up = 0.5 + 0.5 * tangent
    active = values * half_up
    slope = half_up + active * (1.0 - half_up) * (
        2.0 * gelu_root + 6.0 * gelu_root * gelu_cubic * squared
    )
    return active, slope


def normalize(values):
    average = jnp.mean(values, axis=-1, keepdims=True)
    centred = values - average
    inverse = lax.rsqrt(jnp.mean(centred * centred, axis=-1, keepdims=True) + norm_eps)
    return (centred * inverse, inverse)


def norm_back(upstream, normed, inverse, gain):
    scaled = upstream * gain
    centred_grad = (
        scaled
        - jnp.mean(scaled, axis=-1, keepdims=True)
        - normed * jnp.mean(scaled * normed, axis=-1, keepdims=True)
    )
    return inverse * centred_grad


def array(shape, kind):
    return jax.ShapeDtypeStruct(shape, kind)


def kept(shape, kind):
    return pltpu.HBM(shape, kind)


def size_of(x):
    return math.prod(x.shape) * jnp.dtype(x.dtype).itemsize


def run(kernel, operands, outs, flops=0, limit=32, first=(), mark=False, light=False, **more):
    if "in_specs" not in more:
        more["in_specs"] = [spec_of(x) for x in operands]
    operands = [in_hbm(x.values) if isinstance(x, Far) else x for x in operands]
    alone = not isinstance(outs, list)
    outs = [outs] if alone else list(outs)
    count, results = len(operands), len(outs)
    moved = sum(map(size_of, operands)) + sum(map(size_of, outs))
    if light:
        flops = moved = 0
    first = tuple(first)
    more["in_specs"] = list(more["in_specs"]) + [pl.BlockSpec(memory_space=pl.ANY)] * len(first)
    if mark:
        outs.append(array((8, LANES), wide))
    if "out_specs" in more:
        more["out_specs"] = list(more["out_specs"])
        if mark:
            more["out_specs"].append(pl.BlockSpec((8, LANES), lambda *i: (0, 0)))

    def whole(*refs):
        end = count + len(first) + results
        if mark:
            refs[end][...] = jnp.zeros((8, LANES), wide)
        kernel(*refs[:count], *refs[count + len(first) : end], *refs[end + mark :])

    res = pl.pallas_call(
        whole,
        out_shape=outs,
        compiler_params=pltpu.CompilerParams(vmem_limit_bytes=limit << 20),
        cost_estimate=pl.CostEstimate(flops=int(flops), bytes_accessed=int(moved), transcendentals=0),
        **more,
    )(*operands, *first)
    return res[0] if alone and not mark else res


def in_hbm(x):
    return pltpu.with_memory_space_constraint(x, pltpu.HBM)


class Far:
    def __init__(self, values):
        self.values = values


def spec_of(x):
    if isinstance(x, Far):
        shape = x.values.shape
        return pl.BlockSpec(shape, lambda *i: (0,) * len(shape))
    scalar = x.ndim == 1 and x.dtype == jnp.int32
    return pl.BlockSpec(memory_space=pltpu.SMEM if scalar else pltpu.VMEM)


def project_kernel(
    chips, place_ref, own_ref, other_ref, gain_ref, bias_ref, gain2_ref, bias2_ref, mine_ref, sibling_ref,
    full_ref, last_ref, out_ref, scale_ref
):
    place, side = place_ref[0], place_ref[1]
    for n, ref in enumerate((gain_ref, bias_ref, gain2_ref, bias2_ref)):
        scale_ref[n : n + 1] = ref[...].reshape(1, ref.shape[0])
    if chips:
        rows = mine_ref.shape[2]
        for k in range(chips):
            for ref, source in ((mine_ref, place ^ (2 * k)), (sibling_ref, place ^ (2 * k + 1))):
                block = pl.ds(pl.multiple_of(source * rows, rows), rows)
                full_ref[:, block, :] = ref[k, :3]
                last_ref[block, :] = ref[k, 3]
    else:
        full_ref[...] = mine_ref[:3]
        last_ref[...] = mine_ref[3]
    count, width = own_ref.shape[0], mine_ref.shape[-1]
    for ref, first in ((own_ref, side * count), (other_ref, (1 - side) * count)):
        hat, _ = normalize(ref[...].astype(wide))
        normed = (hat * scale_ref[0:1] + scale_ref[1:2]).astype(low)
        for n in range(3):
            out_ref[pl.ds(pl.multiple_of(first, count), count), n * width : (n + 1) * width] = dot(
                normed, full_ref[n]
            ).astype(low)


def turned_kernel(place_ref, own_ref, other_ref, scale_ref, out_ref):
    side = place_ref[1]
    count = own_ref.shape[0]
    for ref, first in ((own_ref, side * count), (other_ref, (1 - side) * count)):
        hat, _ = normalize(ref[...].astype(wide))
        normed = (hat * scale_ref[0:1] + scale_ref[1:2]).T
        out_ref[:, pl.ds(pl.multiple_of(first, count), count)] = normed.astype(low)


def attend_kernel(block, place_ref, q_ref, k_ref, v_ref, unreached_ref, member_ref, out_ref, total_ref, keep_ref, give_ref):
    side = place_ref[1]
    rows = q_ref.shape[0]
    lane = lax.broadcasted_iota(jnp.int32, (1, LANES), 1)
    first_head = lane < HD
    ones = jnp.ones((rows, LANES), low)
    keys = jnp.concatenate([k_ref[...], member_ref[...]], axis=1)
    values = jnp.concatenate([v_ref[...], ones], axis=1)
    causal = lax.broadcasted_iota(jnp.int32, (block, block), 1) <= lax.broadcasted_iota(
        jnp.int32, (block, block), 0
    )
    for start in range(0, rows, block):
        stop = start + block
        query = q_ref[start:stop] * HD**-0.5
        unreached = unreached_ref[start:stop]
        halves = []
        for own in (first_head, ~first_head):
            left = jnp.concatenate([jnp.where(own, query, 0).astype(low), unreached], axis=1)
            scores = dot(left, keys[:stop], NT)
            near = jnp.where(causal, scores[:, start:], masked_score)
            top = jnp.max(near, axis=1, keepdims=True)
            if start:
                far = scores[:, :start]
                top = jnp.maximum(top, jnp.max(far, axis=1, keepdims=True))
                weights = jnp.concatenate(
                    [jnp.exp(far - top).astype(low), jnp.exp(near - top).astype(low)], axis=1
                )
            else:
                weights = jnp.exp(near - top).astype(low)
            sums = dot(weights, values[:stop], NN)
            total = sums[:, LANES:]
            halves.append((sums[:, :LANES] / total, top + jnp.log(total)))
        out_ref[start:stop] = jnp.where(first_head, halves[0][0], halves[1][0]).astype(low)
        total_ref[start:stop] = jnp.where(first_head, halves[0][1], halves[1][1])
    half = rows // 2
    keep_ref[...] = out_ref[pl.ds(pl.multiple_of(side * half, half), half)]
    give_ref[...] = out_ref[pl.ds(pl.multiple_of((1 - side) * half, half), half)]


def attend(place, projected, unreached, member, block=256):
    rows, width = projected.shape
    pairs = width // (3 * LANES)

    def part(n, height=rows):
        return pl.BlockSpec((height, LANES), lambda p: (0, n * pairs + p))

    fixed = pl.BlockSpec((rows, LANES), lambda p: (0, 0))
    return run(
        functools.partial(attend_kernel, block),
        (place, in_hbm(projected), in_hbm(projected), in_hbm(projected), unreached, member),
        [
            kept((rows, width // 3), low),
            kept((rows, width // 3), wide),
            array((rows // 2, width // 3), low),
            array((rows // 2, width // 3), low),
        ],
        flops=12e9,
        grid=(pairs,),
        in_specs=[spec_of(place), part(0), part(1), part(2), fixed, fixed],
        out_specs=[part(0), part(0), part(0, rows // 2), part(0, rows // 2)],
    )


def attend_back_kernel(
    chips, block, place_ref, q_ref, k_ref, v_ref, unreached_ref, member_ref, out_ref, total_ref, mine_ref, more_ref,
    turned_ref, weight_ref, scale_ref, second_ref,
    res_ref, keep_ref, give_ref, sums_ref, dk, dv, grads, parts, products, columns,
):
    place, side = place_ref[0], place_ref[1]
    step = pl.program_id(0)
    rows = q_ref.shape[0]
    half = rows // 2
    grads[pl.ds(pl.multiple_of(side * half, half), half)] = mine_ref[...]
    grads[pl.ds(pl.multiple_of((1 - side) * half, half), half)] = more_ref[...]
    lane = lax.broadcasted_iota(jnp.int32, (1, LANES), 1)
    first_head = lane < HD
    keys = jnp.concatenate([k_ref[...], member_ref[...]], axis=1)
    causal = lax.broadcasted_iota(jnp.int32, (block, block), 1) <= lax.broadcasted_iota(
        jnp.int32, (block, block), 0
    )
    for start in range(rows - block, -1, -block):
        stop = start + block
        query = q_ref[start:stop] * HD**-0.5
        unreached = unreached_ref[start:stop]
        grad = grads[start:stop]
        both = grad.astype(wide) * out_ref[start:stop].astype(wide)
        query_halves = []
        key_terms = []
        value_terms = []
        for head, own in enumerate((first_head, ~first_head)):
            q_own = jnp.where(own, query, 0).astype(low)
            g_own = jnp.where(own, grad, 0).astype(low)
            scores = dot(jnp.concatenate([q_own, unreached], axis=1), keys[:stop], NT)
            total = total_ref[start:stop, HD * head : HD * head + 1]
            centre = jnp.sum(jnp.where(own, both, 0.0), axis=1, keepdims=True)
            near = jnp.exp(jnp.where(causal, scores[:, start:], masked_score) - total)
            if start:
                weights = jnp.concatenate([jnp.exp(scores[:, :start] - total), near], axis=1)
            else:
                weights = near
            gains = dot(g_own, v_ref[:stop], NT)
            slopes = (weights * (gains - centre)).astype(low)
            query_halves.append(dot(slopes, k_ref[:stop], NN))
            key_terms.append(dot(slopes, q_own, TN))
            value_terms.append(dot(weights.astype(low), g_own, TN))
        res_ref[0, start:stop] = (
            jnp.where(first_head, query_halves[0], query_halves[1]) * HD**-0.5
        ).astype(low)
        if stop == rows:
            dk[...] = key_terms[0] + key_terms[1]
            dv[...] = value_terms[0] + value_terms[1]
        else:
            dk[:stop] += key_terms[0] + key_terms[1]
            dv[:stop] += value_terms[0] + value_terms[1]
    res_ref[1] = dk[...].astype(low)
    res_ref[2] = dv[...].astype(low)

    pair = dot(turned_ref[...], jnp.concatenate([res_ref[0], res_ref[1]], axis=1))
    grads_in = (pair[:, :LANES], pair[:, LANES:], dot(turned_ref[...], res_ref[2]))
    product = column = None
    for n, grad_in in enumerate(grads_in):
        weight = weight_ref[n].astype(wide)
        total = jnp.sum(res_ref[n].astype(wide), axis=0, keepdims=True)
        terms = weight * grad_in, weight * total
        product = terms[0] if n == 0 else product + terms[0]
        column = terms[1] if n == 0 else column + terms[1]
        parts[n] = grad_in.astype(low)

    @pl.when(step == 0)
    def _():
        products[...] = product
        columns[...] = column

    @pl.when(step > 0)
    def _():
        products[...] += product
        columns[...] += column

    lanes = pl.ds(pl.multiple_of(step * LANES, LANES), LANES)
    if chips:
        height = keep_ref.shape[3]
        for k in range(chips):
            for ref, target in ((keep_ref, place ^ (2 * k)), (give_ref, place ^ (2 * k + 1))):
                ref[k % 2, k // 2, :, :, lanes] = parts[
                    :, pl.ds(pl.multiple_of(target * height, height), height)
                ]
    else:
        keep_ref[:, :, lanes] = parts[...]
        give_ref[...] = jnp.zeros(give_ref.shape, low)

    @pl.when(step == pl.num_programs(0) - 1)
    def _():
        bias_grad = jnp.sum(columns[...].T, axis=0, keepdims=True)
        whole = jnp.sum(products[...].T, axis=0, keepdims=True)
        sums_ref[0:1] = (whole - scale_ref[1:2] * bias_grad) / scale_ref[0:1]
        sums_ref[1:2] = bias_grad
        sums_ref[2:4] = second_ref[...]


def attend_back(
    place, projected, unreached, member, out, total, mine, more, turned, weight, scales, second,
    chips, block=256, first=(),
):
    rows, width = projected.shape
    pairs = width // (3 * LANES)
    features = turned.shape[0]

    def part(n, height=rows):
        return pl.BlockSpec((height, LANES), lambda p: (0, n * pairs + p))

    def fixed(shape):
        return pl.BlockSpec(shape, lambda p: (0,) * len(shape))

    if chips:
        shape = (2, chips // 2, 3, features // (2 * chips), width // 3)
        shapes = [shape, shape]
    else:
        shapes = [(3, features, width // 3), (8, LANES)]
    triple = pl.BlockSpec((3, rows, LANES), lambda p: (0, 0, p))
    return run(
        functools.partial(attend_back_kernel, chips, block),
        (
            place, in_hbm(projected), in_hbm(projected), in_hbm(projected), unreached, member,
            in_hbm(out), in_hbm(total), mine, more, in_hbm(turned), in_hbm(weight), scales, second,
        ),
        [kept((3, rows, width // 3), low), *[array(x, low) for x in shapes], array((4, features), wide)],
        flops=30e9,
        limit=44,
        first=first,
        grid=(pairs,),
        in_specs=[spec_of(place), part(0), part(1), part(2), fixed(unreached.shape), fixed(member.shape)]
        + [part(0), part(0), part(0, rows // 2), part(0, rows // 2), fixed(turned.shape)]
        + [pl.BlockSpec((3, features, LANES), lambda p: (0, 0, p)), fixed(scales.shape)]
        + [fixed(second.shape)],
        out_specs=[triple, fixed(shapes[0]), fixed(shapes[1]), fixed((4, features))],
        scratch_shapes=[pltpu.VMEM((rows, LANES), wide)] * 2
        + [pltpu.VMEM((rows, LANES), low), pltpu.VMEM((3, features, LANES), low)]
        + [pltpu.VMEM((features, LANES), wide)] * 2,
    )


def branch_kernel(keep_ref, more_ref, weight_ref, other_ref, residual_ref, scale_ref, middle_ref, normed_ref):
    branch = dot(keep_ref[...], weight_ref[...], NT) + dot(more_ref[...], other_ref[...], NT)
    middle = residual_ref[...].astype(wide) + branch
    middle_ref[...] = middle
    hat, _ = normalize(middle)
    normed_ref[...] = (hat * scale_ref[2:3] + scale_ref[3:4]).astype(low)


def pack_kernel(own_ref, sibling_ref, own_slot_ref, sibling_slot_ref, *out_refs):
    capacity = out_refs[0].shape[1]
    slots = len(out_refs) * capacity
    for source, (ref, slot_ref) in enumerate(
        ((own_ref, own_slot_ref), (sibling_ref, sibling_slot_ref))
    ):
        place = lax.broadcasted_iota(jnp.int32, (slots, ref.shape[0]), 0)
        chooser = (place == slot_ref[...]).astype(wide).astype(low)
        packed = dot(chooser, ref[...]).astype(low)
        for k, out_ref in enumerate(out_refs):
            out_ref[source] = packed[k * capacity : (k + 1) * capacity]


def straight_pack_kernel(values_ref, slot_ref, out_ref):
    place = lax.broadcasted_iota(jnp.int32, (out_ref.shape[0], values_ref.shape[0]), 0)
    chooser = (place == slot_ref[...]).astype(wide).astype(low)
    out_ref[...] = dot(chooser, values_ref[...]).astype(low)


def expert_kernel(first, count, chunk, place_ref, in_ref, out_ref, grads_ref, more_grads_ref, *refs):
    pieces, more_pieces = refs[:count], refs[count : 2 * count]
    x_ref, ct_ref, active_ref, slope_ref, keep_ref, give_ref = refs[-6:]
    step = pl.program_id(0)
    place = place_ref[0]
    capacity = pieces[0].shape[1]
    rows = 2 * capacity
    for k in range(count):

        @pl.when(step == k)
        def _(k=k):
            for c in range(2):
                x_ref[0, c * capacity : (c + 1) * capacity] = pieces[k][c]
                x_ref[0, rows + c * capacity : rows + (c + 1) * capacity] = more_pieces[k][c]

    source = place ^ (2 * (first + step))
    for c in range(2):
        ct_ref[0, c * capacity : (c + 1) * capacity] = grads_ref[source ^ c]
        ct_ref[0, rows + c * capacity : rows + (c + 1) * capacity] = more_grads_ref[source ^ c]
    x = x_ref[0]
    ct = ct_ref[0]
    total = None
    for start in range(0, in_ref.shape[1], chunk):
        stop = start + chunk
        pre = dot(x, in_ref[:, start:stop])
        gains = dot(ct, out_ref[start:stop], NT)
        active, slope = gelu_both(pre)
        active_ref[0, :, start:stop] = active.astype(low)
        grad_pre = (gains * slope).astype(low)
        slope_ref[0, :, start:stop] = grad_pre
        term = dot(grad_pre, in_ref[:, start:stop], NT)
        total = term if total is None else total + term
    keep_ref[0] = total[:rows]
    give_ref[0] = total[rows:].astype(low)


def expert_group(
    place, weight_in, weight_out, grads, more_grads, pieces, more_pieces, buffers, span, chips, earlier
):
    first, stop = span
    count = stop - first
    capacity, width = pieces[0].shape[1:]
    hidden = weight_in.shape[1]
    rows = 4 * capacity
    operands = [place, weight_in, weight_out, grads, more_grads, *pieces, *more_pieces]
    specs = [spec_of(place)] + [
        pl.BlockSpec(x.shape, lambda i, n=x.ndim: (0,) * n) for x in operands[1:]
    ]
    aliases = {}
    if buffers is not None:
        aliases = {len(operands) + n: n for n in range(4)}
        operands += buffers
        specs += [pl.BlockSpec(memory_space=pl.ANY)] * 4

    def block(height, size, offset):
        return pl.BlockSpec((1, height, size), lambda i: (offset + i, 0, 0))

    res = run(
        functools.partial(expert_kernel, first, count, min(512, hidden)),
        operands,
        [
            kept((chips, rows, width), low),
            kept((chips, rows, width), low),
            kept((chips, rows, hidden), low),
            kept((chips, rows, hidden), low),
            array((count, rows // 2, width), wide),
            array((count, rows // 2, width), low),
        ],
        flops=6 * count * rows * width * hidden,
        grid=(count,),
        in_specs=specs,
        out_specs=[
            block(rows, width, first),
            block(rows, width, first),
            block(rows, hidden, first),
            block(rows, hidden, first),
            block(rows // 2, width, 0),
            block(rows // 2, width, 0),
        ],
        input_output_aliases=aliases,
        first=earlier,
    )
    return res[:4], res[4], res[5]


def pieces_kernel(keep_ref, more_ref, *out_refs):
    capacity = out_refs[0].shape[1]
    for k, out_ref in enumerate(out_refs):
        total = (keep_ref[k] + more_ref[k].astype(wide)).astype(low)
        for c in range(2):
            out_ref[c] = total[c * capacity : (c + 1) * capacity]


def unpack_kernel(own_slot_ref, sibling_slot_ref, *refs):
    pieces, (own_ref, sibling_ref) = refs[:-2], refs[-2:]
    capacity = pieces[0].shape[1]
    slots = len(pieces) * capacity
    for source, (slot_ref, out_ref) in enumerate(
        ((own_slot_ref, own_ref), (sibling_slot_ref, sibling_ref))
    ):
        place = lax.broadcasted_iota(jnp.int32, (slots, out_ref.shape[0]), 0)
        chooser = (place == slot_ref[...]).astype(wide).astype(low)
        values = jnp.concatenate([piece[source] for piece in pieces], axis=0)
        out_ref[...] = dot(chooser, values, TN).astype(low)


def ffn_kernel(active_ref, weight_ref, keep_ref, give_ref):
    values = dot(active_ref[0], weight_ref[...])
    rows = keep_ref.shape[1]
    keep_ref[0] = values[:rows]
    give_ref[0] = values[rows:].astype(low)


def product_kernel(left_ref, right_ref, out_ref):
    left, right = left_ref[...], right_ref[...]
    out_ref[...] = dot(
        left.reshape(-1, left.shape[-1]), right.reshape(-1, right.shape[-1]), TN
    )


def ffn_sum_kernel(place_ref, keep_ref, more_ref, out_ref):
    place = place_ref[0]
    capacity = out_ref.shape[1]
    for k in range(keep_ref.shape[0]):
        total = (keep_ref[k] + more_ref[k].astype(wide)).astype(low)
        for c in range(2):
            out_ref[place ^ (2 * k + c)] = total[c * capacity : (c + 1) * capacity]


def out_kernel(slot_ref, values_ref, middle_ref, out_ref):
    place = lax.broadcasted_iota(jnp.int32, (values_ref.shape[0], out_ref.shape[0]), 0)
    chooser = (place == slot_ref[...]).astype(wide).astype(low)
    out_ref[...] = (middle_ref[...] + dot(chooser, values_ref[...], TN)).astype(low)


def middle_back_kernel(
    own_ref, more_ref, middle_ref, ct_ref, scale_ref, weight_ref, other_ref,
    grad_ref, branch_ref, mine_ref, give_ref, sums_ref,
):
    grad_second = own_ref[...].astype(wide) + more_ref[...].astype(wide)
    hat, inverse = normalize(middle_ref[...])
    sums_ref[0:1] = jnp.sum(grad_second * hat, axis=0, keepdims=True)
    sums_ref[1:2] = jnp.sum(grad_second, axis=0, keepdims=True)
    grad_middle = ct_ref[...].astype(wide) + norm_back(grad_second, hat, inverse, scale_ref[2:3])
    grad_ref[...] = grad_middle
    branch = grad_middle.astype(low)
    branch_ref[...] = branch
    give_ref[...] = dot(branch, other_ref[...]).astype(low)
    mine_ref[...] = dot(branch, weight_ref[...]).astype(low)


def output_part_kernel(chips, place_ref, branch_ref, keep_ref, more_ref, own_ref, give_ref, parts):
    place = place_ref[0]
    parts[0] = dot(branch_ref[...], keep_ref[...], TN)
    parts[1] = dot(branch_ref[...], more_ref[...], TN)
    if chips:
        rows = own_ref.shape[2]
        for k in range(chips):
            block = pl.ds(pl.multiple_of((place ^ (2 * k)) * rows, rows), rows)
            own_ref[:, k] = parts[:, block]
            block = pl.ds(pl.multiple_of((place ^ (2 * k + 1)) * rows, rows), rows)
            give_ref[:, k] = parts[:, block].astype(low)
    else:
        own_ref[...] = parts[0]
        give_ref[...] = parts[1].astype(low)


def output_sum_kernel(own_ref, more_ref, keep_ref, give_ref):
    keep_ref[...] = own_ref[0] + more_ref[0].astype(wide)
    give_ref[...] = (own_ref[1] + more_ref[1].astype(wide)).astype(low)


def first_kernel(place_ref, grads_ref, full_ref, give_ref, own_ref):
    half = own_ref.shape[0]
    side = place_ref[1]
    for out_ref, first in ((give_ref, 1 - side), (own_ref, side)):
        rows = pl.ds(pl.multiple_of(first * half, half), half)
        total = None
        for n in range(3):
            term = dot(grads_ref[n, rows], full_ref[n], NT)
            total = term if total is None else total + term
        out_ref[...] = total.astype(out_ref.dtype)


def spread(sums):
    half = sums.shape[1] // 2
    rows = []
    rest = sums
    for _ in range(3):
        term = rest.astype(low).astype(wide)
        rest = rest - term
        rows += [term[:, :half], term[:, half:]]
    rows.append(jnp.zeros((8, half), wide))
    return jnp.concatenate(rows, axis=0).astype(low)


def gathered(rows):
    rows = rows.astype(wide)
    terms = [
        jnp.concatenate([rows[8 * n : 8 * n + 4], rows[8 * n + 4 : 8 * n + 8]], axis=1)
        for n in range(3)
    ]
    return (terms[0] + terms[1]) + terms[2]


def halves_kernel(
    keep_ref, more_ref, output_ref, more_output_ref, sums_ref, core_ref, across_ref, both_ref,
    near_ref, far_ref, out_sums_ref,
):
    count, size = near_ref.shape
    pieces = keep_ref.shape[1]
    height = count // pieces
    sums = (sums_ref[...] + core_ref[...]) + (across_ref[...] + both_ref[...])
    out_sums_ref[...] = sums
    far_ref[count:] = spread(sums)
    for side, ref in ((0, near_ref), (1, far_ref)):
        for k in range(pieces):
            total = keep_ref[side, k].astype(wide) + more_ref[side, k].astype(wide)
            total = total.reshape(-1, size).astype(low)
            ref[k * height : k * height + total.shape[0]] = total
            rest = output_ref[2 * k + side] + more_output_ref[2 * k + side].astype(wide)
            ref[k * height + total.shape[0] : (k + 1) * height] = rest.astype(low)


def quarters_kernel(near_ref, more_ref, sums_ref, own_ref, out_sums_ref, *out_refs):
    rows = own_ref.shape[0]
    sums = sums_ref[...] + gathered(more_ref[near_ref.shape[0] :])
    out_sums_ref[...] = sums
    packed = spread(sums)
    for n, ref in enumerate((own_ref, *out_refs)):
        block = slice(n * rows, (n + 1) * rows)
        total = near_ref[block].astype(wide) + more_ref[block].astype(wide)
        ref[:rows] = total.astype(ref.dtype)
        if n:
            ref[rows:] = packed


def total_kernel(own_ref, sums_ref, *refs):
    aways, (in_ref, out_ref, out_sums_ref) = refs[:-3], refs[-3:]
    rows = out_ref.shape[0]
    sums = [sums_ref[...]]
    total = own_ref[...]
    for ref in aways:
        total = total + ref[: own_ref.shape[0]].astype(wide)
        sums.append(gathered(ref[own_ref.shape[0] :]))
    while len(sums) > 1:
        sums = [x + y for x, y in zip(sums[0::2], sums[1::2])]
    out_sums_ref[...] = sums[0]
    for n in range(3):
        in_ref[n] = total[n * rows : (n + 1) * rows]
    out_ref[...] = total[3 * rows :]


def input_grad_kernel(grad_ref, own_ref, more_ref, input_ref, scale_ref, out_ref):
    hat, inverse = normalize(input_ref[...].astype(wide))
    upstream = own_ref[...] + more_ref[...].astype(wide)
    out_ref[...] = grad_ref[...] + norm_back(upstream, hat, inverse, scale_ref[0:1])


def across(values):
    return lax.ppermute(values, "tp", [(0, 1), (1, 0)])


def swapped(values, offset):
    if offset == 0:
        return values
    count = lax.axis_size("fsdp")
    return lax.ppermute(values, "fsdp", [(i, i ^ offset) for i in range(count)])


def reduce_blocks(blocks, index, count):
    bit = 0
    part = blocks
    while count > 1:
        mine = (index >> bit) & 1
        split = part.reshape(count // 2, 2, *blocks.shape[1:])
        keep = lax.dynamic_index_in_dim(split, mine, 1, keepdims=False)
        give = lax.dynamic_index_in_dim(split, 1 - mine, 1, keepdims=False)
        got = swapped(give.astype(low), 1 << bit)
        part = keep.astype(wide) + got.astype(wide)
        if count > 2:
            part = part.astype(low)
        count //= 2
        bit += 1
    return part[0]


def tree_masks(lengths, parents, tree_size):
    segment_count = lengths.shape[0]
    number = jnp.arange(segment_count, dtype=jnp.int32)
    segment_end = jnp.sum(jnp.where(number[None, :] <= number[:, None], lengths[None, :], 0), axis=1)
    starts = segment_end - lengths
    position = jnp.arange(tree_size, dtype=jnp.int32)
    member = (
        (position[:, None] >= starts[None, :]) & (position[:, None] < segment_end[None, :])
    ).astype(wide)
    closure = jnp.maximum(
        jnp.eye(segment_count, dtype=wide), (parents[:, None] == number[None, :]).astype(wide)
    )
    steps = 1
    while steps < segment_count:
        closure = jnp.minimum(jnp.dot(closure, closure), 1.0)
        steps *= 2
    unreached = (1.0 - jnp.dot(member, closure)) * masked_score
    padding = ((0, 0), (0, LANES - segment_count))
    return jnp.pad(unreached, padding).astype(low), jnp.pad(member, padding).astype(low)


def shards(
    inputs,
    token_ids,
    hash_table,
    segment_lengths,
    segment_parents,
    first_gain,
    first_bias,
    input_weight,
    output_weight,
    second_gain,
    second_bias,
    expert_in,
    expert_out,
    cotangent,
):
    own_count, width = inputs.shape
    experts_in_all = lax.axis_size("fsdp")
    tree_size = token_ids.shape[0]
    capacity = 2 * own_count // experts_in_all
    local_width = input_weight.shape[2]
    chips = experts_in_all // 2
    shard_rows = input_weight.shape[1]
    hidden = expert_in.shape[2]
    index = lax.axis_index("fsdp")
    side = lax.axis_index("tp")
    place = jnp.stack([index, side]).astype(jnp.int32)
    in_kernel = shard_rows % 16 == 0
    scales = [first_gain, first_bias, second_gain, second_bias]

    other_inputs = across(inputs)
    shard = jnp.concatenate([input_weight, output_weight.T[None]])
    pieces = {0: shard}
    for k in range(2, chips, 2):
        pieces[k] = swapped(shard, 2 * k)
    for k in range(1, chips, 2):
        pieces[k] = swapped(pieces[k - 1], 2)
    mine = jnp.stack([pieces[k] for k in range(chips)])
    sibling = swapped(mine, 1)

    own_ids = lax.dynamic_slice_in_dim(token_ids, side * own_count, own_count, 0)
    table = hash_table.reshape(-1, LANES).astype(low)
    row_hot = (own_ids[:, None] // LANES == jnp.arange(table.shape[0])[None, :]).astype(low)
    lane_hot = own_ids[:, None] % LANES == jnp.arange(LANES)[None, :]
    experts = jnp.sum(jnp.where(lane_hot, dot(row_hot, table), 0.0), axis=1).astype(jnp.int32)
    hot = (experts[:, None] == jnp.arange(experts_in_all)[None, :]).astype(low)
    earlier = (jnp.arange(own_count)[:, None] > jnp.arange(own_count)[None, :]).astype(low)
    rank = jnp.sum(dot(earlier, hot) * hot.astype(wide), axis=1).astype(jnp.int32)
    own_slot = experts * capacity + rank
    sibling_slot = swapped(own_slot, 1)

    def chip_slot(slot):
        offset = (slot // capacity) ^ index
        return jnp.where(offset & 1 == 0, (offset >> 1) * capacity + slot % capacity, -1)

    own_place, sibling_place = chip_slot(own_slot), chip_slot(sibling_slot)

    slot_count = experts_in_all * capacity
    packed_grads = run(
        straight_pack_kernel,
        (cotangent, own_slot[None]),
        kept((slot_count, width), low),
        flops=2 * slot_count * own_count * width,
        first=(mine, other_inputs),
    )
    slot_grads = lax.all_to_all(
        packed_grads.reshape(experts_in_all, capacity, width), "fsdp", 0, 0, tiled=True
    )
    more_slot_grads = across(slot_grads)

    if in_kernel:
        weights = (mine, sibling)
    else:
        both = jnp.stack([mine, sibling], 1)
        both = both.reshape(experts_in_all, 4, shard_rows, local_width)
        full = jnp.concatenate(
            [lax.dynamic_index_in_dim(both, index ^ n, 0, False) for n in range(experts_in_all)], axis=1
        )
        weights = (full, full[:1, :16])
    full_weight, out_weight, projected, scales = run(
        functools.partial(project_kernel, chips if in_kernel else 0),
        (place, inputs, other_inputs, *scales, *weights),
        [
            kept((3, width, local_width), low),
            array((width, local_width), low),
            kept((tree_size, 3 * local_width), low),
            array((4, width), wide),
        ],
        flops=2 * tree_size * width * 3 * local_width,
    )
    other_out_weight = across(out_weight)
    unreached, member = tree_masks(segment_lengths[0], segment_parents[0], tree_size)
    attended, totals, attended_keep, attended_give = attend(place, projected, unreached, member)
    attended_more = across(attended_give)
    middle, second_normed = run(
        branch_kernel,
        (attended_keep, attended_more, out_weight, other_out_weight, inputs, scales),
        [kept((own_count, width), wide), array((own_count, width), low)],
        flops=2 * own_count * width * width,
    )

    sibling_normed = swapped(second_normed, 1)
    piece = array((2, capacity, width), low)
    packed = run(
        pack_kernel,
        (second_normed, sibling_normed, own_place[None], sibling_place[None]),
        [piece] * chips,
        first=(slot_grads,),
        flops=4 * own_count * own_count * width,
    )
    quarter = chips // 4
    near, next_near, far, next_far = [(n * quarter, (n + 1) * quarter) for n in range(4)]
    arrived = {}
    for span in (far, near, next_near):
        for k in range(*span):
            arrived[k] = swapped(packed[k], 2 * k)
    for k in range(*next_far):
        arrived[k] = swapped(packed[k], 2 * k)
    spans = (near, far, next_far, next_near)
    more_arrived = {k: across(arrived[k]) for span in spans for k in range(*span)}

    turned, turned_done = run(
        turned_kernel,
        (place, Far(inputs), Far(other_inputs), scales),
        kept((width, tree_size), low),
        mark=True,
        first=(packed[0],),
    )

    weight_in, weight_out = expert_in[0], expert_out[0]
    buffers = None
    returned = {}
    done = []
    back = []
    for turn, span in enumerate(spans):
        own_pieces = [arrived[k] for k in range(*span)]
        buffers, keep, give = expert_group(
            place, weight_in, weight_out, slot_grads, more_slot_grads,
            own_pieces, [more_arrived[k] for k in range(*span)], buffers, span, chips,
            [turned_done] + [arrived[k] for k in range(1, chips)] if turn == 0 else [],
        )
        *sums, token = run(pieces_kernel, (keep, across(give)), [piece] * quarter, mark=True)
        done.append(token)
        for k in range(*span):
            returned[k] = swapped(sums[k - span[0]], 2 * k)
        back.append([returned[k] for k in range(*span)])
    slot_rows, grad_rows, actives, grad_pres = buffers
    rows = 4 * capacity
    ffn_keep, ffn_give, ffn_done = run(
        ffn_kernel,
        (in_hbm(actives), weight_out),
        [array((chips, rows // 2, width), wide), array((chips, rows // 2, width), low)],
        flops=2 * chips * rows * width * hidden,
        first=done[2:3],
        mark=True,
        light=True,
        grid=(chips,),
        in_specs=[
            pl.BlockSpec((1, rows, hidden), lambda i: (i, 0, 0)),
            pl.BlockSpec((hidden, width), lambda i: (0, 0)),
        ],
        out_specs=[pl.BlockSpec((1, rows // 2, width), lambda i: (i, 0, 0))] * 2,
    )
    ffn_more = across(ffn_give)
    tile = min(512, hidden)
    stripe = pl.BlockSpec((chips, rows, tile), lambda i: (0, 0, i))
    fixed = pl.BlockSpec((chips, rows, width), lambda i: (0, 0, 0))
    expert_out_grad, out_done = run(
        product_kernel,
        (in_hbm(actives), in_hbm(grad_rows)),
        array((hidden, width), wide),
        flops=2 * chips * rows * width * hidden,
        first=(ffn_done, done[3], *back[0], *back[1]),
        mark=True,
        grid=(hidden // tile,),
        in_specs=[stripe, fixed],
        out_specs=[pl.BlockSpec((tile, width), lambda i: (i, 0))],
    )
    own_part, sibling_part = run(
        unpack_kernel,
        (own_place[None], sibling_place[None], *[returned[k] for k in range(chips)]),
        [array((own_count, width), low)] * 2,
        first=(out_done, *back[2]),
        flops=4 * own_count * own_count * width,
    )
    sibling_part = swapped(sibling_part, 1)
    grad_middle, grad_branch, grad_mine, grad_give, second_sums, middle_done = run(
        middle_back_kernel,
        (
            own_part, sibling_part, Far(middle), Far(cotangent), scales,
            Far(out_weight), Far(other_out_weight),
        ),
        [
            kept((own_count, width), wide),
            array((own_count, width), low),
            array((own_count, local_width), low),
            array((own_count, local_width), low),
            array((2, width), wide),
        ],
        first=(ffn_more,),
        mark=True,
        flops=2 * own_count * width * width,
    )
    grad_more = across(grad_give)
    ffn_sums, sums_done = run(
        ffn_sum_kernel,
        (place, ffn_keep, ffn_more),
        kept((experts_in_all, capacity, width), low),
        mark=True,
        first=(middle_done,),
    )
    ffn_back = lax.all_to_all(ffn_sums, "fsdp", 0, 0, tiled=True)

    if in_kernel:
        blocks = (2, chips, shard_rows, local_width)
        outs = [array(blocks, wide), array(blocks, low)]
    else:
        outs = [array((width, local_width), wide), array((width, local_width), low)]
    output_own, output_give = run(
        functools.partial(output_part_kernel, chips if in_kernel else 0),
        (place, grad_branch, Far(attended_keep), Far(attended_more)),
        outs,
        scratch_shapes=[pltpu.VMEM((2, width, local_width), wide)],
        flops=2 * own_count * width * width,
    )
    if in_kernel:
        output_own, output_give, output_done = run(
            output_sum_kernel,
            (output_own, swapped(output_give, 1)),
            [array(blocks[1:], wide), array(blocks[1:], low)],
            mark=True,
        )
    else:
        output_done = middle_done
    output_more = across(output_give)
    grad_projected, part_keep, part_give, norm_sums = attend_back(
        place, projected, unreached, member, attended, totals, grad_mine, grad_more,
        turned, full_weight, scales, second_sums,
        chips if in_kernel else 0, first=(sums_done, output_done),
    )

    if in_kernel:
        part_more = swapped(part_give, 1)
        rows = 4 * shard_rows
        near_sum, far_sum, norm_sums, half_done = run(
            halves_kernel,
            (
                part_keep, part_more, output_own, output_more,
                norm_sums, swapped(norm_sums, 1), across(norm_sums),
                lax.ppermute(norm_sums, ("fsdp", "tp"), [(i, i ^ 3) for i in range(2 * experts_in_all)]),
            ),
            [
                kept((chips // 2 * rows, local_width), low),
                kept((chips // 2 * rows + 32, local_width), low),
                array((4, width), wide),
            ],
            mark=True,
        )
    else:
        half_done = norm_sums
    first_give, first_own, give_done = run(
        first_kernel,
        (place, Far(grad_projected), Far(full_weight)),
        [array((own_count, width), low), array((own_count, width), wide)],
        mark=True,
        first=(half_done,),
        light=True,
        flops=2 * tree_size * width * 3 * local_width,
    )
    first_more = across(first_give)
    expert_in_grad, in_done = run(
        product_kernel,
        (in_hbm(slot_rows), in_hbm(grad_pres)),
        array((width, hidden), wide),
        flops=2 * chips * capacity * 4 * width * hidden,
        first=(give_done,),
        mark=True,
        light=True,
        grid=(hidden // tile,),
        in_specs=[fixed, stripe],
        out_specs=[pl.BlockSpec((width, tile), lambda i: (0, i))],
    )
    if in_kernel:
        own_sum, norm_sums, *away = run(
            quarters_kernel,
            (Far(near_sum), Far(swapped(far_sum, 2)), norm_sums),
            [array((rows, local_width), wide), array((4, width), wide)]
            + [array((rows + 32, local_width), low)] * (chips // 2 - 1),
            first=(in_done, ffn_back),
        )
        away = [swapped(away[k - 1], 4 * k) for k in range(1, chips // 2)]
    else:
        output_part = (output_own + output_more.astype(wide)).astype(low)
        blocks = jnp.concatenate([part_keep, output_part[None]])
        blocks = blocks.reshape(4, experts_in_all, shard_rows, local_width).transpose(1, 0, 2, 3)
        summed = reduce_blocks(blocks, index, experts_in_all)
        bit = 1
        while bit < experts_in_all:
            norm_sums = norm_sums + swapped(norm_sums, bit)
            bit *= 2
        norm_sums = norm_sums + across(norm_sums)
    input_grad, input_done = run(
        input_grad_kernel,
        (Far(grad_middle), first_own, first_more, Far(inputs), scales),
        array((own_count, width), wide),
        mark=True,
        light=True,
    )
    out_block, out_done = run(
        out_kernel,
        (own_slot[None], ffn_back.reshape(slot_count, width), Far(middle)),
        array((own_count, width), low),
        mark=True,
        light=True,
        flops=2 * own_count * slot_count * width,
    )
    if in_kernel:
        input_weight_grad, output_weight_grad, norm_sums = run(
            total_kernel,
            (own_sum, norm_sums, *away),
            [
                array((3, shard_rows, local_width), wide),
                array((shard_rows, local_width), wide),
                array((4, width), wide),
            ],
            first=(input_done, out_done),
        )
    else:
        input_weight_grad, output_weight_grad = summed[:3], summed[3]
    output_weight_grad = output_weight_grad.T
    return (
        out_block,
        input_grad,
        norm_sums[0],
        norm_sums[1],
        input_weight_grad,
        output_weight_grad,
        norm_sums[2],
        norm_sums[3],
        expert_in_grad[None],
        expert_out_grad[None],
    )


def solution(mesh):
    return jax.shard_map(
        shards,
        mesh=mesh,
        in_specs=(
            P(("fsdp", "tp"), None),
            P("fsdp"),
            P(),
            P("fsdp", None),
            P("fsdp", None),
            P(),
            P(),
            P(None, "fsdp", "tp"),
            P("tp", "fsdp"),
            P(),
            P(),
            P("fsdp", None, "tp"),
            P("fsdp", "tp", None),
            P(("fsdp", "tp"), None),
        ),
        out_specs=(
            P(("fsdp", "tp"), None),
            P(("fsdp", "tp"), None),
            P(),
            P(),
            P(None, "fsdp", "tp"),
            P("tp", "fsdp"),
            P(),
            P(),
            P("fsdp", None, "tp"),
            P("fsdp", "tp", None),
        ),
        check_vma=False,
    )
```

```python
import functools
import math

import jax
import jax.numpy as jnp
from jax import lax
from jax.experimental import pallas as pl
from jax.experimental.pallas import tpu as pltpu
from jax.sharding import PartitionSpec as P

HD = 64
LANES = 128

norm_eps = 1e-05
masked_score = -1e30
gelu_root = 0.7978845608028654
gelu_cubic = 0.044715
low = jnp.bfloat16
wide = jnp.float32

NN = (((1,), (0,)), ((), ()))
NT = (((1,), (1,)), ((), ()))
TN = (((0,), (0,)), ((), ()))


def dot(left, right, dims=NN):
    return lax.dot_general(left, right, dims, preferred_element_type=wide)


def gelu_both(values):
    squared = values * values
    tangent = jnp.tanh(values * (gelu_root + gelu_root * gelu_cubic * squared))
    half_up = 0.5 + 0.5 * tangent
    active = values * half_up
    slope = half_up + active * (1.0 - half_up) * (
        2.0 * gelu_root + 6.0 * gelu_root * gelu_cubic * squared
    )
    return active, slope


def normalize(values):
    average = jnp.mean(values, axis=-1, keepdims=True)
    centred = values - average
    inverse = lax.rsqrt(jnp.mean(centred * centred, axis=-1, keepdims=True) + norm_eps)
    return (centred * inverse, inverse)


def norm_back(upstream, normed, inverse, gain):
    scaled = upstream * gain
    centred_grad = (
        scaled
        - jnp.mean(scaled, axis=-1, keepdims=True)
        - normed * jnp.mean(scaled * normed, axis=-1, keepdims=True)
    )
    return inverse * centred_grad


def array(shape, kind):
    return jax.ShapeDtypeStruct(shape, kind)


def kept(shape, kind):
    return pltpu.HBM(shape, kind)


def size_of(x):
    return math.prod(x.shape) * jnp.dtype(x.dtype).itemsize


def run(kernel, operands, outs, flops=0, limit=32, first=(), mark=False, light=False, **more):
    if "in_specs" not in more:
        more["in_specs"] = [spec_of(x) for x in operands]
    operands = [in_hbm(x.values) if isinstance(x, Far) else x for x in operands]
    alone = not isinstance(outs, list)
    outs = [outs] if alone else list(outs)
    count, results = len(operands), len(outs)
    moved = sum(map(size_of, operands)) + sum(map(size_of, outs))
    if light:
        flops = moved = 0
    first = tuple(first)
    more["in_specs"] = list(more["in_specs"]) + [pl.BlockSpec(memory_space=pl.ANY)] * len(first)
    if mark:
        outs.append(array((8, LANES), wide))
    if "out_specs" in more:
        more["out_specs"] = list(more["out_specs"])
        if mark:
            more["out_specs"].append(pl.BlockSpec((8, LANES), lambda *i: (0, 0)))

    def whole(*refs):
        end = count + len(first) + results
        if mark:
            refs[end][...] = jnp.zeros((8, LANES), wide)
        kernel(*refs[:count], *refs[count + len(first) : end], *refs[end + mark :])

    res = pl.pallas_call(
        whole,
        out_shape=outs,
        compiler_params=pltpu.CompilerParams(vmem_limit_bytes=limit << 20),
        cost_estimate=pl.CostEstimate(flops=int(flops), bytes_accessed=int(moved), transcendentals=0),
        **more,
    )(*operands, *first)
    return res[0] if alone and not mark else res


def in_hbm(x):
    return pltpu.with_memory_space_constraint(x, pltpu.HBM)


class Far:
    def __init__(self, values):
        self.values = values


def spec_of(x):
    if isinstance(x, Far):
        shape = x.values.shape
        return pl.BlockSpec(shape, lambda *i: (0,) * len(shape))
    scalar = x.ndim == 1 and x.dtype == jnp.int32
    return pl.BlockSpec(memory_space=pltpu.SMEM if scalar else pltpu.VMEM)


def project_kernel(
    chips, place_ref, own_ref, other_ref, gain_ref, bias_ref, gain2_ref, bias2_ref, mine_ref, sibling_ref,
    full_ref, last_ref, out_ref, scale_ref
):
    place, side = place_ref[0], place_ref[1]
    for n, ref in enumerate((gain_ref, bias_ref, gain2_ref, bias2_ref)):
        scale_ref[n : n + 1] = ref[...].reshape(1, ref.shape[0])
    if chips:
        rows = mine_ref.shape[2]
        for k in range(chips):
            for ref, source in ((mine_ref, place ^ (2 * k)), (sibling_ref, place ^ (2 * k + 1))):
                block = pl.ds(pl.multiple_of(source * rows, rows), rows)
                full_ref[:, block, :] = ref[k, :3]
                last_ref[block, :] = ref[k, 3]
    else:
        full_ref[...] = mine_ref[:3]
        last_ref[...] = mine_ref[3]
    count, width = own_ref.shape[0], mine_ref.shape[-1]
    for ref, first in ((own_ref, side * count), (other_ref, (1 - side) * count)):
        hat, _ = normalize(ref[...].astype(wide))
        normed = (hat * scale_ref[0:1] + scale_ref[1:2]).astype(low)
        for n in range(3):
            out_ref[pl.ds(pl.multiple_of(first, count), count), n * width : (n + 1) * width] = dot(
                normed, full_ref[n]
            ).astype(low)


def turned_kernel(place_ref, own_ref, other_ref, scale_ref, out_ref):
    side = place_ref[1]
    count = own_ref.shape[0]
    for ref, first in ((own_ref, side * count), (other_ref, (1 - side) * count)):
        hat, _ = normalize(ref[...].astype(wide))
        normed = (hat * scale_ref[0:1] + scale_ref[1:2]).T
        out_ref[:, pl.ds(pl.multiple_of(first, count), count)] = normed.astype(low)


def attend_kernel(block, place_ref, q_ref, k_ref, v_ref, unreached_ref, member_ref, out_ref, total_ref, keep_ref, give_ref):
    side = place_ref[1]
    rows = q_ref.shape[0]
    lane = lax.broadcasted_iota(jnp.int32, (1, LANES), 1)
    first_head = lane < HD
    ones = jnp.ones((rows, LANES), low)
    keys = jnp.concatenate([k_ref[...], member_ref[...]], axis=1)
    values = jnp.concatenate([v_ref[...], ones], axis=1)
    row = lax.rem(lax.broadcasted_iota(jnp.int32, (2 * block, block), 0), block)
    causal = lax.broadcasted_iota(jnp.int32, (2 * block, block), 1) <= row
    for start in range(0, rows, block):
        stop = start + block
        query = q_ref[start:stop] * HD**-0.5
        zero = jnp.zeros_like(query)
        unreached = unreached_ref[start:stop]
        left = jnp.concatenate(
            [
                jnp.concatenate([jnp.where(first_head, query, zero), unreached], axis=1),
                jnp.concatenate([jnp.where(first_head, zero, query), unreached], axis=1),
            ]
        ).astype(low)
        scores = dot(left, keys[:stop], NT)
        near = jnp.where(causal, scores[:, start:], masked_score)
        top = jnp.max(near, axis=1, keepdims=True)
        if start:
            far = scores[:, :start]
            top = jnp.maximum(top, jnp.max(far, axis=1, keepdims=True))
            weights = jnp.concatenate(
                [jnp.exp(far - top).astype(low), jnp.exp(near - top).astype(low)], axis=1
            )
        else:
            weights = jnp.exp(near - top).astype(low)
        sums = dot(weights, values[:stop], NN)
        total = sums[:, LANES:]
        attended = sums[:, :LANES] / total
        total = top + jnp.log(total)
        out_ref[start:stop] = jnp.where(first_head, attended[:block], attended[block:]).astype(low)
        total_ref[start:stop] = jnp.where(first_head, total[:block], total[block:])
    half = rows // 2
    keep_ref[...] = out_ref[pl.ds(pl.multiple_of(side * half, half), half)]
    give_ref[...] = out_ref[pl.ds(pl.multiple_of((1 - side) * half, half), half)]


def attend(place, projected, unreached, member, block=256):
    rows, width = projected.shape
    pairs = width // (3 * LANES)

    def part(n, height=rows):
        return pl.BlockSpec((height, LANES), lambda p: (0, n * pairs + p))

    fixed = pl.BlockSpec((rows, LANES), lambda p: (0, 0))
    return run(
        functools.partial(attend_kernel, block),
        (place, in_hbm(projected), in_hbm(projected), in_hbm(projected), unreached, member),
        [
            kept((rows, width // 3), low),
            kept((rows, width // 3), wide),
            array((rows // 2, width // 3), low),
            array((rows // 2, width // 3), low),
        ],
        flops=12e9,
        grid=(pairs,),
        in_specs=[spec_of(place), part(0), part(1), part(2), fixed, fixed],
        out_specs=[part(0), part(0), part(0, rows // 2), part(0, rows // 2)],
    )


def attend_back_kernel(
    chips, block, place_ref, q_ref, k_ref, v_ref, unreached_ref, member_ref, out_ref, total_ref, mine_ref, more_ref,
    turned_ref, weight_ref, scale_ref, second_ref,
    res_ref, keep_ref, give_ref, sums_ref, dk, dv, grads, parts, products, columns,
):
    place, side = place_ref[0], place_ref[1]
    step = pl.program_id(0)
    rows = q_ref.shape[0]
    half = rows // 2
    grads[pl.ds(pl.multiple_of(side * half, half), half)] = mine_ref[...]
    grads[pl.ds(pl.multiple_of((1 - side) * half, half), half)] = more_ref[...]
    lane = lax.broadcasted_iota(jnp.int32, (1, LANES), 1)
    first_head = lane < HD
    keys = jnp.concatenate([k_ref[...], member_ref[...]], axis=1)
    causal = lax.broadcasted_iota(jnp.int32, (block, block), 1) <= lax.broadcasted_iota(
        jnp.int32, (block, block), 0
    )
    for start in range(rows - block, -1, -block):
        stop = start + block
        query = q_ref[start:stop] * HD**-0.5
        unreached = unreached_ref[start:stop]
        grad = grads[start:stop]
        both = grad.astype(wide) * out_ref[start:stop].astype(wide)
        query_halves = []
        key_terms = []
        value_terms = []
        for head, own in enumerate((first_head, ~first_head)):
            q_own = jnp.where(own, query, 0).astype(low)
            g_own = jnp.where(own, grad, 0).astype(low)
            scores = dot(jnp.concatenate([q_own, unreached], axis=1), keys[:stop], NT)
            total = total_ref[start:stop, HD * head : HD * head + 1]
            centre = jnp.sum(jnp.where(own, both, 0.0), axis=1, keepdims=True)
            near = jnp.exp(jnp.where(causal, scores[:, start:], masked_score) - total)
            if start:
                weights = jnp.concatenate([jnp.exp(scores[:, :start] - total), near], axis=1)
            else:
                weights = near
            gains = dot(g_own, v_ref[:stop], NT)
            slopes = (weights * (gains - centre)).astype(low)
            query_halves.append(dot(slopes, k_ref[:stop], NN))
            key_terms.append(dot(slopes, q_own, TN))
            value_terms.append(dot(weights.astype(low), g_own, TN))
        res_ref[0, start:stop] = (
            jnp.where(first_head, query_halves[0], query_halves[1]) * HD**-0.5
        ).astype(low)
        if stop == rows:
            dk[...] = key_terms[0] + key_terms[1]
            dv[...] = value_terms[0] + value_terms[1]
        else:
            dk[:stop] += key_terms[0] + key_terms[1]
            dv[:stop] += value_terms[0] + value_terms[1]
    res_ref[1] = dk[...].astype(low)
    res_ref[2] = dv[...].astype(low)

    pair = dot(turned_ref[...], jnp.concatenate([res_ref[0], res_ref[1]], axis=1))
    grads_in = (pair[:, :LANES], pair[:, LANES:], dot(turned_ref[...], res_ref[2]))
    product = column = None
    for n, grad_in in enumerate(grads_in):
        weight = weight_ref[n].astype(wide)
        total = jnp.sum(res_ref[n].astype(wide), axis=0, keepdims=True)
        terms = weight * grad_in, weight * total
        product = terms[0] if n == 0 else product + terms[0]
        column = terms[1] if n == 0 else column + terms[1]
        parts[n] = grad_in.astype(low)

    @pl.when(step == 0)
    def _():
        products[...] = product
        columns[...] = column

    @pl.when(step > 0)
    def _():
        products[...] += product
        columns[...] += column

    lanes = pl.ds(pl.multiple_of(step * LANES, LANES), LANES)
    if chips:
        height = keep_ref.shape[3]
        for k in range(chips):
            for ref, target in ((keep_ref, place ^ (2 * k)), (give_ref, place ^ (2 * k + 1))):
                ref[k % 2, k // 2, :, :, lanes] = parts[
                    :, pl.ds(pl.multiple_of(target * height, height), height)
                ]
    else:
        keep_ref[:, :, lanes] = parts[...]
        give_ref[...] = jnp.zeros(give_ref.shape, low)

    @pl.when(step == pl.num_programs(0) - 1)
    def _():
        bias_grad = jnp.sum(columns[...].T, axis=0, keepdims=True)
        whole = jnp.sum(products[...].T, axis=0, keepdims=True)
        sums_ref[0:1] = (whole - scale_ref[1:2] * bias_grad) / scale_ref[0:1]
        sums_ref[1:2] = bias_grad
        sums_ref[2:4] = second_ref[...]


def attend_back(
    place, projected, unreached, member, out, total, mine, more, turned, weight, scales, second,
    chips, block=256, first=(),
):
    rows, width = projected.shape
    pairs = width // (3 * LANES)
    features = turned.shape[0]

    def part(n, height=rows):
        return pl.BlockSpec((height, LANES), lambda p: (0, n * pairs + p))

    def fixed(shape):
        return pl.BlockSpec(shape, lambda p: (0,) * len(shape))

    if chips:
        shape = (2, chips // 2, 3, features // (2 * chips), width // 3)
        shapes = [shape, shape]
    else:
        shapes = [(3, features, width // 3), (8, LANES)]
    triple = pl.BlockSpec((3, rows, LANES), lambda p: (0, 0, p))
    return run(
        functools.partial(attend_back_kernel, chips, block),
        (
            place, in_hbm(projected), in_hbm(projected), in_hbm(projected), unreached, member,
            in_hbm(out), in_hbm(total), mine, more, in_hbm(turned), in_hbm(weight), scales, second,
        ),
        [kept((3, rows, width // 3), low), *[array(x, low) for x in shapes], array((4, features), wide)],
        flops=30e9,
        limit=44,
        first=first,
        grid=(pairs,),
        in_specs=[spec_of(place), part(0), part(1), part(2), fixed(unreached.shape), fixed(member.shape)]
        + [part(0), part(0), part(0, rows // 2), part(0, rows // 2), fixed(turned.shape)]
        + [pl.BlockSpec((3, features, LANES), lambda p: (0, 0, p)), fixed(scales.shape)]
        + [fixed(second.shape)],
        out_specs=[triple, fixed(shapes[0]), fixed(shapes[1]), fixed((4, features))],
        scratch_shapes=[pltpu.VMEM((rows, LANES), wide)] * 2
        + [pltpu.VMEM((rows, LANES), low), pltpu.VMEM((3, features, LANES), low)]
        + [pltpu.VMEM((features, LANES), wide)] * 2,
    )


def branch_kernel(keep_ref, more_ref, weight_ref, other_ref, residual_ref, scale_ref, middle_ref, normed_ref):
    branch = dot(keep_ref[...], weight_ref[...], NT) + dot(more_ref[...], other_ref[...], NT)
    middle = residual_ref[...].astype(wide) + branch
    middle_ref[...] = middle
    hat, _ = normalize(middle)
    normed_ref[...] = (hat * scale_ref[2:3] + scale_ref[3:4]).astype(low)


def pack_kernel(own_ref, sibling_ref, own_slot_ref, sibling_slot_ref, *out_refs):
    capacity = out_refs[0].shape[1]
    slots = len(out_refs) * capacity
    for source, (ref, slot_ref) in enumerate(
        ((own_ref, own_slot_ref), (sibling_ref, sibling_slot_ref))
    ):
        place = lax.broadcasted_iota(jnp.int32, (slots, ref.shape[0]), 0)
        chooser = (place == slot_ref[...]).astype(wide).astype(low)
        packed = dot(chooser, ref[...]).astype(low)
        for k, out_ref in enumerate(out_refs):
            out_ref[source] = packed[k * capacity : (k + 1) * capacity]


def straight_pack_kernel(values_ref, slot_ref, out_ref):
    place = lax.broadcasted_iota(jnp.int32, (out_ref.shape[0], values_ref.shape[0]), 0)
    chooser = (place == slot_ref[...]).astype(wide).astype(low)
    out_ref[...] = dot(chooser, values_ref[...]).astype(low)


def expert_kernel(first, count, chunk, place_ref, in_ref, out_ref, grads_ref, more_grads_ref, *refs):
    pieces, more_pieces = refs[:count], refs[count : 2 * count]
    x_ref, ct_ref, active_ref, slope_ref, keep_ref, give_ref = refs[-6:]
    step = pl.program_id(0)
    place = place_ref[0]
    capacity = pieces[0].shape[1]
    rows = 2 * capacity
    for k in range(count):

        @pl.when(step == k)
        def _(k=k):
            for c in range(2):
                x_ref[0, c * capacity : (c + 1) * capacity] = pieces[k][c]
                x_ref[0, rows + c * capacity : rows + (c + 1) * capacity] = more_pieces[k][c]

    source = place ^ (2 * (first + step))
    for c in range(2):
        ct_ref[0, c * capacity : (c + 1) * capacity] = grads_ref[source ^ c]
        ct_ref[0, rows + c * capacity : rows + (c + 1) * capacity] = more_grads_ref[source ^ c]
    x = x_ref[0]
    ct = ct_ref[0]
    total = None
    for start in range(0, in_ref.shape[1], chunk):
        stop = start + chunk
        pre = dot(x, in_ref[:, start:stop])
        gains = dot(ct, out_ref[start:stop], NT)
        active, slope = gelu_both(pre)
        active_ref[0, :, start:stop] = active.astype(low)
        grad_pre = (gains * slope).astype(low)
        slope_ref[0, :, start:stop] = grad_pre
        term = dot(grad_pre, in_ref[:, start:stop], NT)
        total = term if total is None else total + term
    keep_ref[0] = total[:rows]
    give_ref[0] = total[rows:].astype(low)


def expert_group(
    place, weight_in, weight_out, grads, more_grads, pieces, more_pieces, buffers, span, chips, earlier
):
    first, stop = span
    count = stop - first
    capacity, width = pieces[0].shape[1:]
    hidden = weight_in.shape[1]
    rows = 4 * capacity
    operands = [place, weight_in, weight_out, grads, more_grads, *pieces, *more_pieces]
    specs = [spec_of(place)] + [
        pl.BlockSpec(x.shape, lambda i, n=x.ndim: (0,) * n) for x in operands[1:]
    ]
    aliases = {}
    if buffers is not None:
        aliases = {len(operands) + n: n for n in range(4)}
        operands += buffers
        specs += [pl.BlockSpec(memory_space=pl.ANY)] * 4

    def block(height, size, offset):
        return pl.BlockSpec((1, height, size), lambda i: (offset + i, 0, 0))

    res = run(
        functools.partial(expert_kernel, first, count, min(512, hidden)),
        operands,
        [
            kept((chips, rows, width), low),
            kept((chips, rows, width), low),
            kept((chips, rows, hidden), low),
            kept((chips, rows, hidden), low),
            array((count, rows // 2, width), wide),
            array((count, rows // 2, width), low),
        ],
        flops=6 * count * rows * width * hidden,
        grid=(count,),
        in_specs=specs,
        out_specs=[
            block(rows, width, first),
            block(rows, width, first),
            block(rows, hidden, first),
            block(rows, hidden, first),
            block(rows // 2, width, 0),
            block(rows // 2, width, 0),
        ],
        input_output_aliases=aliases,
        first=earlier,
    )
    return res[:4], res[4], res[5]


def pieces_kernel(keep_ref, more_ref, *out_refs):
    capacity = out_refs[0].shape[1]
    for k, out_ref in enumerate(out_refs):
        total = (keep_ref[k] + more_ref[k].astype(wide)).astype(low)
        for c in range(2):
            out_ref[c] = total[c * capacity : (c + 1) * capacity]


def unpack_kernel(own_slot_ref, sibling_slot_ref, *refs):
    pieces, (own_ref, sibling_ref) = refs[:-2], refs[-2:]
    capacity = pieces[0].shape[1]
    slots = len(pieces) * capacity
    for source, (slot_ref, out_ref) in enumerate(
        ((own_slot_ref, own_ref), (sibling_slot_ref, sibling_ref))
    ):
        place = lax.broadcasted_iota(jnp.int32, (slots, out_ref.shape[0]), 0)
        chooser = (place == slot_ref[...]).astype(wide).astype(low)
        values = jnp.concatenate([piece[source] for piece in pieces], axis=0)
        out_ref[...] = dot(chooser, values, TN).astype(low)


def ffn_kernel(active_ref, weight_ref, keep_ref, give_ref):
    values = dot(active_ref[0], weight_ref[...])
    rows = keep_ref.shape[1]
    keep_ref[0] = values[:rows]
    give_ref[0] = values[rows:].astype(low)


def product_kernel(left_ref, right_ref, out_ref):
    left, right = left_ref[...], right_ref[...]
    out_ref[...] = dot(
        left.reshape(-1, left.shape[-1]), right.reshape(-1, right.shape[-1]), TN
    )


def ffn_sum_kernel(place_ref, keep_ref, more_ref, out_ref):
    place = place_ref[0]
    capacity = out_ref.shape[1]
    for k in range(keep_ref.shape[0]):
        total = (keep_ref[k] + more_ref[k].astype(wide)).astype(low)
        for c in range(2):
            out_ref[place ^ (2 * k + c)] = total[c * capacity : (c + 1) * capacity]


def out_kernel(slot_ref, values_ref, middle_ref, out_ref):
    place = lax.broadcasted_iota(jnp.int32, (values_ref.shape[0], out_ref.shape[0]), 0)
    chooser = (place == slot_ref[...]).astype(wide).astype(low)
    out_ref[...] = (middle_ref[...] + dot(chooser, values_ref[...], TN)).astype(low)


def middle_back_kernel(
    chips, place_ref, own_ref, more_ref, middle_ref, ct_ref, scale_ref, weight_ref, other_ref, keep_ref, attended_ref,
    grad_ref, mine_ref, give_ref, sums_ref, output_ref, output_give_ref, parts,
):
    grad_second = own_ref[...].astype(wide) + more_ref[...].astype(wide)
    hat, inverse = normalize(middle_ref[...])
    sums_ref[0:1] = jnp.sum(grad_second * hat, axis=0, keepdims=True)
    sums_ref[1:2] = jnp.sum(grad_second, axis=0, keepdims=True)
    grad_middle = ct_ref[...].astype(wide) + norm_back(grad_second, hat, inverse, scale_ref[2:3])
    grad_ref[...] = grad_middle
    branch = grad_middle.astype(low)
    give_ref[...] = dot(branch, other_ref[...]).astype(low)
    mine_ref[...] = dot(branch, weight_ref[...]).astype(low)

    place = place_ref[0]
    turned = branch.astype(wide).T.astype(low)
    parts[0] = dot(turned, keep_ref[...])
    parts[1] = dot(turned, attended_ref[...])
    if chips:
        rows = output_ref.shape[2]
        for k in range(chips):
            block = pl.ds(pl.multiple_of((place ^ (2 * k)) * rows, rows), rows)
            output_ref[:, k] = parts[:, block]
            block = pl.ds(pl.multiple_of((place ^ (2 * k + 1)) * rows, rows), rows)
            output_give_ref[:, k] = parts[:, block].astype(low)
    else:
        output_ref[...] = parts[0]
        output_give_ref[...] = parts[1].astype(low)


def output_sum_kernel(own_ref, more_ref, keep_ref, give_ref):
    keep_ref[...] = own_ref[0] + more_ref[0].astype(wide)
    give_ref[...] = (own_ref[1] + more_ref[1].astype(wide)).astype(low)


def first_kernel(place_ref, grads_ref, full_ref, give_ref, own_ref):
    half = own_ref.shape[0]
    side = place_ref[1]
    for out_ref, first in ((give_ref, 1 - side), (own_ref, side)):
        rows = pl.ds(pl.multiple_of(first * half, half), half)
        total = None
        for n in range(3):
            term = dot(grads_ref[n, rows], full_ref[n], NT)
            total = term if total is None else total + term
        out_ref[...] = total.astype(out_ref.dtype)


def spread(sums):
    half = sums.shape[1] // 2
    rows = []
    rest = sums
    for _ in range(3):
        term = rest.astype(low).astype(wide)
        rest = rest - term
        rows += [term[:, :half], term[:, half:]]
    rows.append(jnp.zeros((8, half), wide))
    return jnp.concatenate(rows, axis=0).astype(low)


def gathered(rows):
    rows = rows.astype(wide)
    terms = [
        jnp.concatenate([rows[8 * n : 8 * n + 4], rows[8 * n + 4 : 8 * n + 8]], axis=1)
        for n in range(3)
    ]
    return (terms[0] + terms[1]) + terms[2]


def halves_kernel(
    keep_ref, more_ref, output_ref, more_output_ref, sums_ref, core_ref, across_ref, both_ref,
    near_ref, far_ref, out_sums_ref,
):
    count, size = near_ref.shape
    pieces = keep_ref.shape[1]
    height = count // pieces
    sums = (sums_ref[...] + core_ref[...]) + (across_ref[...] + both_ref[...])
    out_sums_ref[...] = sums
    far_ref[count:] = spread(sums)
    for side, ref in ((0, near_ref), (1, far_ref)):
        for k in range(pieces):
            total = keep_ref[side, k].astype(wide) + more_ref[side, k].astype(wide)
            total = total.reshape(-1, size).astype(low)
            ref[k * height : k * height + total.shape[0]] = total
            rest = output_ref[2 * k + side] + more_output_ref[2 * k + side].astype(wide)
            ref[k * height + total.shape[0] : (k + 1) * height] = rest.astype(low)


def quarters_kernel(near_ref, more_ref, sums_ref, own_ref, out_sums_ref, *out_refs):
    rows = own_ref.shape[0]
    sums = sums_ref[...] + gathered(more_ref[near_ref.shape[0] :])
    out_sums_ref[...] = sums
    packed = spread(sums)
    for n, ref in enumerate((own_ref, *out_refs)):
        block = slice(n * rows, (n + 1) * rows)
        total = near_ref[block].astype(wide) + more_ref[block].astype(wide)
        ref[:rows] = total.astype(ref.dtype)
        if n:
            ref[rows:] = packed


def total_kernel(own_ref, sums_ref, *refs):
    aways, (in_ref, out_ref), sums_refs = refs[:-6], refs[-6:-4], refs[-4:]
    rows = out_ref.shape[0]
    sums = [sums_ref[...]]
    total = own_ref[...]
    for ref in aways:
        total = total + ref[: own_ref.shape[0]].astype(wide)
        sums.append(gathered(ref[own_ref.shape[0] :]))
    while len(sums) > 1:
        sums = [x + y for x, y in zip(sums[0::2], sums[1::2])]
    for n, ref in enumerate(sums_refs):
        ref[...] = sums[0][n : n + 1].reshape(ref.shape)
    for n in range(3):
        in_ref[n] = total[n * rows : (n + 1) * rows]
    out_ref[...] = total[3 * rows :]


def input_grad_kernel(grad_ref, own_ref, more_ref, input_ref, scale_ref, out_ref):
    hat, inverse = normalize(input_ref[...].astype(wide))
    upstream = own_ref[...] + more_ref[...].astype(wide)
    out_ref[...] = grad_ref[...] + norm_back(upstream, hat, inverse, scale_ref[0:1])


def across(values):
    return lax.ppermute(values, "tp", [(0, 1), (1, 0)])


def swapped(values, offset):
    if offset == 0:
        return values
    count = lax.axis_size("fsdp")
    return lax.ppermute(values, "fsdp", [(i, i ^ offset) for i in range(count)])


def reduce_blocks(blocks, index, count):
    bit = 0
    part = blocks
    while count > 1:
        mine = (index >> bit) & 1
        split = part.reshape(count // 2, 2, *blocks.shape[1:])
        keep = lax.dynamic_index_in_dim(split, mine, 1, keepdims=False)
        give = lax.dynamic_index_in_dim(split, 1 - mine, 1, keepdims=False)
        got = swapped(give.astype(low), 1 << bit)
        part = keep.astype(wide) + got.astype(wide)
        if count > 2:
            part = part.astype(low)
        count //= 2
        bit += 1
    return part[0]


def tree_masks(lengths, parents, tree_size):
    segment_count = lengths.shape[0]
    number = jnp.arange(segment_count, dtype=jnp.int32)
    segment_end = jnp.sum(jnp.where(number[None, :] <= number[:, None], lengths[None, :], 0), axis=1)
    starts = segment_end - lengths
    position = jnp.arange(tree_size, dtype=jnp.int32)
    member = (
        (position[:, None] >= starts[None, :]) & (position[:, None] < segment_end[None, :])
    ).astype(wide)
    closure = jnp.maximum(
        jnp.eye(segment_count, dtype=wide), (parents[:, None] == number[None, :]).astype(wide)
    )
    steps = 1
    while steps < segment_count:
        closure = jnp.minimum(jnp.dot(closure, closure), 1.0)
        steps *= 2
    unreached = (1.0 - jnp.dot(member, closure)) * masked_score
    padding = ((0, 0), (0, LANES - segment_count))
    return jnp.pad(unreached, padding).astype(low), jnp.pad(member, padding).astype(low)


def shards(
    inputs,
    token_ids,
    hash_table,
    segment_lengths,
    segment_parents,
    first_gain,
    first_bias,
    input_weight,
    output_weight,
    second_gain,
    second_bias,
    expert_in,
    expert_out,
    cotangent,
):
    own_count, width = inputs.shape
    experts_in_all = lax.axis_size("fsdp")
    tree_size = token_ids.shape[0]
    capacity = 2 * own_count // experts_in_all
    local_width = input_weight.shape[2]
    chips = experts_in_all // 2
    shard_rows = input_weight.shape[1]
    hidden = expert_in.shape[2]
    index = lax.axis_index("fsdp")
    side = lax.axis_index("tp")
    place = jnp.stack([index, side]).astype(jnp.int32)
    in_kernel = shard_rows % 16 == 0
    scales = [first_gain, first_bias, second_gain, second_bias]

    other_inputs = across(inputs)
    shard = jnp.concatenate([input_weight, output_weight.T[None]])
    pieces = {0: shard}
    for k in range(2, chips, 2):
        pieces[k] = swapped(shard, 2 * k)
    for k in range(1, chips, 2):
        pieces[k] = swapped(pieces[k - 1], 2)
    mine = jnp.stack([pieces[k] for k in range(chips)])
    sibling = swapped(mine, 1)

    own_ids = lax.dynamic_slice_in_dim(token_ids, side * own_count, own_count, 0)
    table = hash_table.reshape(-1, LANES).astype(low)
    row_hot = (own_ids[:, None] // LANES == jnp.arange(table.shape[0])[None, :]).astype(low)
    lane_hot = own_ids[:, None] % LANES == jnp.arange(LANES)[None, :]
    experts = jnp.sum(jnp.where(lane_hot, dot(row_hot, table), 0.0), axis=1).astype(jnp.int32)
    hot = (experts[:, None] == jnp.arange(experts_in_all)[None, :]).astype(low)
    earlier = (jnp.arange(own_count)[:, None] > jnp.arange(own_count)[None, :]).astype(low)
    rank = jnp.sum(dot(earlier, hot) * hot.astype(wide), axis=1).astype(jnp.int32)
    own_slot = experts * capacity + rank
    sibling_slot = swapped(own_slot, 1)

    def chip_slot(slot):
        offset = (slot // capacity) ^ index
        return jnp.where(offset & 1 == 0, (offset >> 1) * capacity + slot % capacity, -1)

    own_place, sibling_place = chip_slot(own_slot), chip_slot(sibling_slot)

    slot_count = experts_in_all * capacity
    packed_grads = run(
        straight_pack_kernel,
        (cotangent, own_slot[None]),
        kept((slot_count, width), low),
        flops=2 * slot_count * own_count * width,
        first=(mine, other_inputs),
    )
    slot_grads = lax.all_to_all(
        packed_grads.reshape(experts_in_all, capacity, width), "fsdp", 0, 0, tiled=True
    )
    more_slot_grads = across(slot_grads)

    if in_kernel:
        weights = (mine, sibling)
    else:
        both = jnp.stack([mine, sibling], 1)
        both = both.reshape(experts_in_all, 4, shard_rows, local_width)
        full = jnp.concatenate(
            [lax.dynamic_index_in_dim(both, index ^ n, 0, False) for n in range(experts_in_all)], axis=1
        )
        weights = (full, full[:1, :16])
    full_weight, out_weight, projected, scales = run(
        functools.partial(project_kernel, chips if in_kernel else 0),
        (place, inputs, other_inputs, *scales, *weights),
        [
            kept((3, width, local_width), low),
            array((width, local_width), low),
            kept((tree_size, 3 * local_width), low),
            array((4, width), wide),
        ],
        flops=2 * tree_size * width * 3 * local_width,
    )
    other_out_weight = across(out_weight)
    unreached, member = tree_masks(segment_lengths[0], segment_parents[0], tree_size)
    attended, totals, attended_keep, attended_give = attend(place, projected, unreached, member)
    attended_more = across(attended_give)
    middle, second_normed = run(
        branch_kernel,
        (attended_keep, attended_more, out_weight, other_out_weight, inputs, scales),
        [kept((own_count, width), wide), array((own_count, width), low)],
        flops=2 * own_count * width * width,
    )

    sibling_normed = swapped(second_normed, 1)
    piece = array((2, capacity, width), low)
    packed = run(
        pack_kernel,
        (second_normed, sibling_normed, own_place[None], sibling_place[None]),
        [piece] * chips,
        first=(slot_grads,),
        flops=4 * own_count * own_count * width,
    )
    quarter = chips // 4
    near, next_near, far, next_far = [(n * quarter, (n + 1) * quarter) for n in range(4)]
    arrived = {}
    for span in (far, near, next_near):
        for k in range(*span):
            arrived[k] = swapped(packed[k], 2 * k)
    for k in range(*next_far):
        arrived[k] = swapped(packed[k], 2 * k)
    spans = (near, far, next_far, next_near)
    more_arrived = {k: across(arrived[k]) for span in spans for k in range(*span)}

    turned, turned_done = run(
        turned_kernel,
        (place, Far(inputs), Far(other_inputs), scales),
        kept((width, tree_size), low),
        mark=True,
        first=(packed[0],),
    )

    weight_in, weight_out = expert_in[0], expert_out[0]
    buffers = None
    returned = {}
    done = []
    back = []
    for turn, span in enumerate(spans):
        own_pieces = [arrived[k] for k in range(*span)]
        buffers, keep, give = expert_group(
            place, weight_in, weight_out, slot_grads, more_slot_grads,
            own_pieces, [more_arrived[k] for k in range(*span)], buffers, span, chips,
            [turned_done] + [arrived[k] for k in range(1, chips)] if turn == 0 else [],
        )
        *sums, token = run(pieces_kernel, (keep, across(give)), [piece] * quarter, mark=True)
        done.append(token)
        for k in range(*span):
            returned[k] = swapped(sums[k - span[0]], 2 * k)
        back.append([returned[k] for k in range(*span)])
    slot_rows, grad_rows, actives, grad_pres = buffers
    rows = 4 * capacity
    ffn_keep, ffn_give, ffn_done = run(
        ffn_kernel,
        (in_hbm(actives), weight_out),
        [array((chips, rows // 2, width), wide), array((chips, rows // 2, width), low)],
        flops=2 * chips * rows * width * hidden,
        first=done[2:3],
        mark=True,
        light=True,
        grid=(chips,),
        in_specs=[
            pl.BlockSpec((1, rows, hidden), lambda i: (i, 0, 0)),
            pl.BlockSpec((hidden, width), lambda i: (0, 0)),
        ],
        out_specs=[pl.BlockSpec((1, rows // 2, width), lambda i: (i, 0, 0))] * 2,
    )
    ffn_more = across(ffn_give)
    tile = min(512, hidden)
    stripe = pl.BlockSpec((chips, rows, tile), lambda i: (0, 0, i))
    fixed = pl.BlockSpec((chips, rows, width), lambda i: (0, 0, 0))
    expert_out_grad, out_done = run(
        product_kernel,
        (in_hbm(actives), in_hbm(grad_rows)),
        array((hidden, width), wide),
        flops=2 * chips * rows * width * hidden,
        first=(ffn_done, done[3], *back[0], *back[1]),
        mark=True,
        grid=(hidden // tile,),
        in_specs=[stripe, fixed],
        out_specs=[pl.BlockSpec((tile, width), lambda i: (i, 0))],
    )
    own_part, sibling_part = run(
        unpack_kernel,
        (own_place[None], sibling_place[None], *[returned[k] for k in range(chips)]),
        [array((own_count, width), low)] * 2,
        first=(out_done, *back[2]),
        flops=4 * own_count * own_count * width,
    )
    sibling_part = swapped(sibling_part, 1)
    if in_kernel:
        blocks = (2, chips, shard_rows, local_width)
        output_outs = [array(blocks, wide), array(blocks, low)]
    else:
        output_outs = [array((width, local_width), wide), array((width, local_width), low)]
    grad_middle, grad_mine, grad_give, second_sums, output_own, output_give, middle_done = run(
        functools.partial(middle_back_kernel, chips if in_kernel else 0),
        (
            place, own_part, sibling_part, Far(middle), Far(cotangent), scales,
            Far(out_weight), Far(other_out_weight), Far(attended_keep), Far(attended_more),
        ),
        [
            kept((own_count, width), wide),
            array((own_count, local_width), low),
            array((own_count, local_width), low),
            array((2, width), wide),
            *output_outs,
        ],
        first=(ffn_more,),
        mark=True,
        scratch_shapes=[pltpu.VMEM((2, width, local_width), wide)],
        flops=4 * own_count * width * width,
    )
    grad_more = across(grad_give)
    ffn_sums, sums_done = run(
        ffn_sum_kernel,
        (place, ffn_keep, ffn_more),
        kept((experts_in_all, capacity, width), low),
        mark=True,
        first=(middle_done,),
    )
    ffn_back = lax.all_to_all(ffn_sums, "fsdp", 0, 0, tiled=True)

    if in_kernel:
        output_own, output_give, output_done = run(
            output_sum_kernel,
            (output_own, swapped(output_give, 1)),
            [array(blocks[1:], wide), array(blocks[1:], low)],
            mark=True,
        )
    else:
        output_done = middle_done
    output_more = across(output_give)
    grad_projected, part_keep, part_give, norm_sums = attend_back(
        place, projected, unreached, member, attended, totals, grad_mine, grad_more,
        turned, full_weight, scales, second_sums,
        chips if in_kernel else 0, first=(sums_done, output_done),
    )

    if in_kernel:
        part_more = swapped(part_give, 1)
        rows = 4 * shard_rows
        near_sum, far_sum, norm_sums, half_done = run(
            halves_kernel,
            (
                part_keep, part_more, output_own, output_more,
                norm_sums, swapped(norm_sums, 1), across(norm_sums),
                lax.ppermute(norm_sums, ("fsdp", "tp"), [(i, i ^ 3) for i in range(2 * experts_in_all)]),
            ),
            [
                kept((chips // 2 * rows, local_width), low),
                kept((chips // 2 * rows + 32, local_width), low),
                array((4, width), wide),
            ],
            mark=True,
        )
    else:
        half_done = norm_sums
    first_give, first_own, give_done = run(
        first_kernel,
        (place, Far(grad_projected), Far(full_weight)),
        [array((own_count, width), low), array((own_count, width), wide)],
        mark=True,
        first=(half_done,),
        light=True,
        flops=2 * tree_size * width * 3 * local_width,
    )
    first_more = across(first_give)
    expert_in_grad, in_done = run(
        product_kernel,
        (in_hbm(slot_rows), in_hbm(grad_pres)),
        array((width, hidden), wide),
        flops=2 * chips * capacity * 4 * width * hidden,
        first=(give_done,),
        mark=True,
        light=True,
        grid=(hidden // tile,),
        in_specs=[fixed, stripe],
        out_specs=[pl.BlockSpec((width, tile), lambda i: (0, i))],
    )
    if in_kernel:
        own_sum, norm_sums, *away = run(
            quarters_kernel,
            (Far(near_sum), Far(swapped(far_sum, 2)), norm_sums),
            [array((rows, local_width), wide), array((4, width), wide)]
            + [array((rows + 32, local_width), low)] * (chips // 2 - 1),
            first=(in_done, ffn_back),
        )
        away = [swapped(away[k - 1], 4 * k) for k in range(1, chips // 2)]
    else:
        output_part = (output_own + output_more.astype(wide)).astype(low)
        blocks = jnp.concatenate([part_keep, output_part[None]])
        blocks = blocks.reshape(4, experts_in_all, shard_rows, local_width).transpose(1, 0, 2, 3)
        summed = reduce_blocks(blocks, index, experts_in_all)
        bit = 1
        while bit < experts_in_all:
            norm_sums = norm_sums + swapped(norm_sums, bit)
            bit *= 2
        norm_sums = norm_sums + across(norm_sums)
    input_grad, input_done = run(
        input_grad_kernel,
        (Far(grad_middle), first_own, first_more, Far(inputs), scales),
        array((own_count, width), wide),
        mark=True,
        light=True,
    )
    out_block, out_done = run(
        out_kernel,
        (own_slot[None], ffn_back.reshape(slot_count, width), Far(middle)),
        array((own_count, width), low),
        mark=True,
        light=True,
        flops=2 * own_count * slot_count * width,
    )
    if in_kernel:
        input_weight_grad, output_weight_grad, *norm_sums = run(
            total_kernel,
            (own_sum, norm_sums, *away),
            [
                array((3, shard_rows, local_width), wide),
                array((shard_rows, local_width), wide),
                *[array((width,), wide)] * 4,
            ],
            first=(input_done, out_done),
        )
    else:
        input_weight_grad, output_weight_grad = summed[:3], summed[3]
    output_weight_grad = output_weight_grad.T
    return (
        out_block,
        input_grad,
        norm_sums[0],
        norm_sums[1],
        input_weight_grad,
        output_weight_grad,
        norm_sums[2],
        norm_sums[3],
        expert_in_grad[None],
        expert_out_grad[None],
    )


def solution(mesh):
    return jax.shard_map(
        shards,
        mesh=mesh,
        in_specs=(
            P(("fsdp", "tp"), None),
            P("fsdp"),
            P(),
            P("fsdp", None),
            P("fsdp", None),
            P(),
            P(),
            P(None, "fsdp", "tp"),
            P("tp", "fsdp"),
            P(),
            P(),
            P("fsdp", None, "tp"),
            P("fsdp", "tp", None),
            P(("fsdp", "tp"), None),
        ),
        out_specs=(
            P(("fsdp", "tp"), None),
            P(("fsdp", "tp"), None),
            P(),
            P(),
            P(None, "fsdp", "tp"),
            P("tp", "fsdp"),
            P(),
            P(),
            P("fsdp", None, "tp"),
            P("fsdp", "tp", None),
        ),
        check_vma=False,
    )
```

```python
import functools
import math

import jax
import jax.numpy as jnp
from jax import lax
from jax.experimental import pallas as pl
from jax.experimental.pallas import tpu as pltpu
from jax.sharding import PartitionSpec as P

HD = 64
LANES = 128

norm_eps = 1e-05
masked_score = -1e30
gelu_root = 0.7978845608028654
gelu_cubic = 0.044715
low = jnp.bfloat16
wide = jnp.float32

NN = (((1,), (0,)), ((), ()))
NT = (((1,), (1,)), ((), ()))
TN = (((0,), (0,)), ((), ()))


def dot(left, right, dims=NN):
    return lax.dot_general(left, right, dims, preferred_element_type=wide)


def gelu_both(values):
    squared = values * values
    tangent = jnp.tanh(values * (gelu_root + gelu_root * gelu_cubic * squared))
    half_up = 0.5 + 0.5 * tangent
    active = values * half_up
    slope = half_up + active * (1.0 - half_up) * (
        2.0 * gelu_root + 6.0 * gelu_root * gelu_cubic * squared
    )
    return active, slope


def normalize(values):
    average = jnp.mean(values, axis=-1, keepdims=True)
    centred = values - average
    inverse = lax.rsqrt(jnp.mean(centred * centred, axis=-1, keepdims=True) + norm_eps)
    return (centred * inverse, inverse)


def norm_back(upstream, normed, inverse, gain):
    scaled = upstream * gain
    centred_grad = (
        scaled
        - jnp.mean(scaled, axis=-1, keepdims=True)
        - normed * jnp.mean(scaled * normed, axis=-1, keepdims=True)
    )
    return inverse * centred_grad


def array(shape, kind):
    return jax.ShapeDtypeStruct(shape, kind)


def kept(shape, kind):
    return pltpu.HBM(shape, kind)


def size_of(x):
    return math.prod(x.shape) * jnp.dtype(x.dtype).itemsize


def run(kernel, operands, outs, flops=0, limit=32, first=(), mark=False, light=False, **more):
    if "in_specs" not in more:
        more["in_specs"] = [spec_of(x) for x in operands]
    operands = [in_hbm(x.values) if isinstance(x, Far) else x for x in operands]
    alone = not isinstance(outs, list)
    outs = [outs] if alone else list(outs)
    count, results = len(operands), len(outs)
    moved = sum(map(size_of, operands)) + sum(map(size_of, outs))
    if light:
        flops = moved = 0
    first = tuple(first)
    more["in_specs"] = list(more["in_specs"]) + [pl.BlockSpec(memory_space=pl.ANY)] * len(first)
    if mark:
        outs.append(array((8, LANES), wide))
    if "out_specs" in more:
        more["out_specs"] = list(more["out_specs"])
        if mark:
            more["out_specs"].append(pl.BlockSpec((8, LANES), lambda *i: (0, 0)))

    def whole(*refs):
        end = count + len(first) + results
        if mark:
            refs[end][...] = jnp.zeros((8, LANES), wide)
        kernel(*refs[:count], *refs[count + len(first) : end], *refs[end + mark :])

    res = pl.pallas_call(
        whole,
        out_shape=outs,
        compiler_params=pltpu.CompilerParams(vmem_limit_bytes=limit << 20),
        cost_estimate=pl.CostEstimate(flops=int(flops), bytes_accessed=int(moved), transcendentals=0),
        **more,
    )(*operands, *first)
    return res[0] if alone and not mark else res


def in_hbm(x):
    return pltpu.with_memory_space_constraint(x, pltpu.HBM)


class Far:
    def __init__(self, values):
        self.values = values


def spec_of(x):
    if isinstance(x, Far):
        shape = x.values.shape
        return pl.BlockSpec(shape, lambda *i: (0,) * len(shape))
    scalar = x.ndim == 1 and x.dtype == jnp.int32
    return pl.BlockSpec(memory_space=pltpu.SMEM if scalar else pltpu.VMEM)


def project_kernel(
    chips, place_ref, own_ref, other_ref, gain_ref, bias_ref, gain2_ref, bias2_ref, mine_ref, sibling_ref,
    full_ref, last_ref, out_ref, scale_ref
):
    place, side = place_ref[0], place_ref[1]
    for n, ref in enumerate((gain_ref, bias_ref, gain2_ref, bias2_ref)):
        scale_ref[n : n + 1] = ref[...].reshape(1, ref.shape[0])
    if chips:
        rows = mine_ref.shape[2]
        for k in range(chips):
            for ref, source in ((mine_ref, place ^ (2 * k)), (sibling_ref, place ^ (2 * k + 1))):
                block = pl.ds(pl.multiple_of(source * rows, rows), rows)
                full_ref[:, block, :] = ref[k, :3]
                last_ref[block, :] = ref[k, 3]
    else:
        full_ref[...] = mine_ref[:3]
        last_ref[...] = mine_ref[3]
    count, width = own_ref.shape[0], mine_ref.shape[-1]
    for ref, first in ((own_ref, side * count), (other_ref, (1 - side) * count)):
        hat, _ = normalize(ref[...].astype(wide))
        normed = (hat * scale_ref[0:1] + scale_ref[1:2]).astype(low)
        for n in range(3):
            out_ref[pl.ds(pl.multiple_of(first, count), count), n * width : (n + 1) * width] = dot(
                normed, full_ref[n]
            ).astype(low)


def turned_kernel(place_ref, own_ref, other_ref, scale_ref, out_ref):
    side = place_ref[1]
    count = own_ref.shape[0]
    for ref, first in ((own_ref, side * count), (other_ref, (1 - side) * count)):
        hat, _ = normalize(ref[...].astype(wide))
        normed = (hat * scale_ref[0:1] + scale_ref[1:2]).T
        out_ref[:, pl.ds(pl.multiple_of(first, count), count)] = normed.astype(low)


def attend_kernel(block, place_ref, q_ref, k_ref, v_ref, unreached_ref, member_ref, out_ref, total_ref, keep_ref, give_ref):
    side = place_ref[1]
    rows = q_ref.shape[0]
    lane = lax.broadcasted_iota(jnp.int32, (1, LANES), 1)
    first_head = lane < HD
    ones = jnp.ones((rows, LANES), low)
    keys = jnp.concatenate([k_ref[...], member_ref[...]], axis=1)
    values = jnp.concatenate([v_ref[...], ones], axis=1)
    row = lax.rem(lax.broadcasted_iota(jnp.int32, (2 * block, block), 0), block)
    causal = lax.broadcasted_iota(jnp.int32, (2 * block, block), 1) <= row
    for start in range(0, rows, block):
        stop = start + block
        query = q_ref[start:stop] * HD**-0.5
        zero = jnp.zeros_like(query)
        unreached = unreached_ref[start:stop]
        left = jnp.concatenate(
            [
                jnp.concatenate([jnp.where(first_head, query, zero), unreached], axis=1),
                jnp.concatenate([jnp.where(first_head, zero, query), unreached], axis=1),
            ]
        ).astype(low)
        scores = dot(left, keys[:stop], NT)
        near = jnp.where(causal, scores[:, start:], masked_score)
        top = jnp.max(near, axis=1, keepdims=True)
        if start:
            far = scores[:, :start]
            top = jnp.maximum(top, jnp.max(far, axis=1, keepdims=True))
            weights = jnp.concatenate(
                [jnp.exp(far - top).astype(low), jnp.exp(near - top).astype(low)], axis=1
            )
        else:
            weights = jnp.exp(near - top).astype(low)
        sums = dot(weights, values[:stop], NN)
        total = sums[:, LANES:]
        attended = sums[:, :LANES] / total
        total = top + jnp.log(total)
        out_ref[start:stop] = jnp.where(first_head, attended[:block], attended[block:]).astype(low)
        total_ref[start:stop] = jnp.where(first_head, total[:block], total[block:])
    half = rows // 2
    keep_ref[...] = out_ref[pl.ds(pl.multiple_of(side * half, half), half)]
    give_ref[...] = out_ref[pl.ds(pl.multiple_of((1 - side) * half, half), half)]


def attend(place, projected, unreached, member, block=256):
    rows, width = projected.shape
    pairs = width // (3 * LANES)

    def part(n, height=rows):
        return pl.BlockSpec((height, LANES), lambda p: (0, n * pairs + p))

    fixed = pl.BlockSpec((rows, LANES), lambda p: (0, 0))
    return run(
        functools.partial(attend_kernel, block),
        (place, in_hbm(projected), in_hbm(projected), in_hbm(projected), unreached, member),
        [
            kept((rows, width // 3), low),
            kept((rows, width // 3), wide),
            array((rows // 2, width // 3), low),
            array((rows // 2, width // 3), low),
        ],
        flops=12e9,
        grid=(pairs,),
        in_specs=[spec_of(place), part(0), part(1), part(2), fixed, fixed],
        out_specs=[part(0), part(0), part(0, rows // 2), part(0, rows // 2)],
    )


def attend_back_kernel(
    chips, block, place_ref, q_ref, k_ref, v_ref, unreached_ref, member_ref, out_ref, total_ref, mine_ref, more_ref,
    turned_ref, weight_ref, scale_ref, second_ref,
    res_ref, keep_ref, give_ref, sums_ref, dk, dv, grads, parts, products, columns,
):
    place, side = place_ref[0], place_ref[1]
    step = pl.program_id(0)
    rows = q_ref.shape[0]
    half = rows // 2
    grads[pl.ds(pl.multiple_of(side * half, half), half)] = mine_ref[...]
    grads[pl.ds(pl.multiple_of((1 - side) * half, half), half)] = more_ref[...]
    lane = lax.broadcasted_iota(jnp.int32, (1, LANES), 1)
    first_head = lane < HD
    keys = jnp.concatenate([k_ref[...], member_ref[...]], axis=1)
    causal = lax.broadcasted_iota(jnp.int32, (block, block), 1) <= lax.broadcasted_iota(
        jnp.int32, (block, block), 0
    )
    for start in range(rows - block, -1, -block):
        stop = start + block
        query = q_ref[start:stop] * HD**-0.5
        unreached = unreached_ref[start:stop]
        grad = grads[start:stop]
        both = grad.astype(wide) * out_ref[start:stop].astype(wide)
        query_halves = []
        key_terms = []
        value_terms = []
        for head, own in enumerate((first_head, ~first_head)):
            q_own = jnp.where(own, query, 0).astype(low)
            g_own = jnp.where(own, grad, 0).astype(low)
            scores = dot(jnp.concatenate([q_own, unreached], axis=1), keys[:stop], NT)
            total = total_ref[start:stop, HD * head : HD * head + 1]
            centre = jnp.sum(jnp.where(own, both, 0.0), axis=1, keepdims=True)
            near = jnp.exp(jnp.where(causal, scores[:, start:], masked_score) - total)
            if start:
                weights = jnp.concatenate([jnp.exp(scores[:, :start] - total), near], axis=1)
            else:
                weights = near
            gains = dot(g_own, v_ref[:stop], NT)
            slopes = (weights * (gains - centre)).astype(low)
            query_halves.append(dot(slopes, k_ref[:stop], NN))
            key_terms.append(dot(slopes, q_own, TN))
            value_terms.append(dot(weights.astype(low), g_own, TN))
        res_ref[0, start:stop] = (
            jnp.where(first_head, query_halves[0], query_halves[1]) * HD**-0.5
        ).astype(low)
        if stop == rows:
            dk[...] = key_terms[0] + key_terms[1]
            dv[...] = value_terms[0] + value_terms[1]
        else:
            dk[:stop] += key_terms[0] + key_terms[1]
            dv[:stop] += value_terms[0] + value_terms[1]
    res_ref[1] = dk[...].astype(low)
    res_ref[2] = dv[...].astype(low)

    pair = dot(turned_ref[...], jnp.concatenate([res_ref[0], res_ref[1]], axis=1))
    grads_in = (pair[:, :LANES], pair[:, LANES:], dot(turned_ref[...], res_ref[2]))
    product = column = None
    for n, grad_in in enumerate(grads_in):
        weight = weight_ref[n].astype(wide)
        total = jnp.sum(res_ref[n].astype(wide), axis=0, keepdims=True)
        terms = weight * grad_in, weight * total
        product = terms[0] if n == 0 else product + terms[0]
        column = terms[1] if n == 0 else column + terms[1]
        parts[n] = grad_in.astype(low)

    @pl.when(step == 0)
    def _():
        products[...] = product
        columns[...] = column

    @pl.when(step > 0)
    def _():
        products[...] += product
        columns[...] += column

    lanes = pl.ds(pl.multiple_of(step * LANES, LANES), LANES)
    if chips:
        height = keep_ref.shape[3]
        for k in range(chips):
            for ref, target in ((keep_ref, place ^ (2 * k)), (give_ref, place ^ (2 * k + 1))):
                ref[k % 2, k // 2, :, :, lanes] = parts[
                    :, pl.ds(pl.multiple_of(target * height, height), height)
                ]
    else:
        keep_ref[:, :, lanes] = parts[...]
        give_ref[...] = jnp.zeros(give_ref.shape, low)

    @pl.when(step == pl.num_programs(0) - 1)
    def _():
        bias_grad = jnp.sum(columns[...].T, axis=0, keepdims=True)
        whole = jnp.sum(products[...].T, axis=0, keepdims=True)
        sums_ref[0:1] = (whole - scale_ref[1:2] * bias_grad) / scale_ref[0:1]
        sums_ref[1:2] = bias_grad
        sums_ref[2:4] = second_ref[...]


def attend_back(
    place, projected, unreached, member, out, total, mine, more, turned, weight, scales, second,
    chips, block=256, first=(),
):
    rows, width = projected.shape
    pairs = width // (3 * LANES)
    features = turned.shape[0]

    def part(n, height=rows):
        return pl.BlockSpec((height, LANES), lambda p: (0, n * pairs + p))

    def fixed(shape):
        return pl.BlockSpec(shape, lambda p: (0,) * len(shape))

    if chips:
        shape = (2, chips // 2, 3, features // (2 * chips), width // 3)
        shapes = [shape, shape]
    else:
        shapes = [(3, features, width // 3), (8, LANES)]
    triple = pl.BlockSpec((3, rows, LANES), lambda p: (0, 0, p))
    return run(
        functools.partial(attend_back_kernel, chips, block),
        (
            place, in_hbm(projected), in_hbm(projected), in_hbm(projected), unreached, member,
            in_hbm(out), in_hbm(total), mine, more, in_hbm(turned), in_hbm(weight), scales, second,
        ),
        [kept((3, rows, width // 3), low), *[array(x, low) for x in shapes], array((4, features), wide)],
        flops=30e9,
        limit=44,
        first=first,
        grid=(pairs,),
        in_specs=[spec_of(place), part(0), part(1), part(2), fixed(unreached.shape), fixed(member.shape)]
        + [part(0), part(0), part(0, rows // 2), part(0, rows // 2), fixed(turned.shape)]
        + [pl.BlockSpec((3, features, LANES), lambda p: (0, 0, p)), fixed(scales.shape)]
        + [fixed(second.shape)],
        out_specs=[triple, fixed(shapes[0]), fixed(shapes[1]), fixed((4, features))],
        scratch_shapes=[pltpu.VMEM((rows, LANES), wide)] * 2
        + [pltpu.VMEM((rows, LANES), low), pltpu.VMEM((3, features, LANES), low)]
        + [pltpu.VMEM((features, LANES), wide)] * 2,
    )


def branch_kernel(keep_ref, more_ref, weight_ref, other_ref, residual_ref, scale_ref, middle_ref, normed_ref):
    branch = dot(keep_ref[...], weight_ref[...], NT) + dot(more_ref[...], other_ref[...], NT)
    middle = residual_ref[...].astype(wide) + branch
    middle_ref[...] = middle
    hat, _ = normalize(middle)
    normed_ref[...] = (hat * scale_ref[2:3] + scale_ref[3:4]).astype(low)


def pack_kernel(own_ref, sibling_ref, own_slot_ref, sibling_slot_ref, *out_refs):
    capacity = out_refs[0].shape[1]
    slots = len(out_refs) * capacity
    for source, (ref, slot_ref) in enumerate(
        ((own_ref, own_slot_ref), (sibling_ref, sibling_slot_ref))
    ):
        place = lax.broadcasted_iota(jnp.int32, (slots, ref.shape[0]), 0)
        chooser = (place == slot_ref[...]).astype(wide).astype(low)
        packed = dot(chooser, ref[...]).astype(low)
        for k, out_ref in enumerate(out_refs):
            out_ref[source] = packed[k * capacity : (k + 1) * capacity]


def straight_pack_kernel(values_ref, slot_ref, out_ref):
    place = lax.broadcasted_iota(jnp.int32, (out_ref.shape[0], values_ref.shape[0]), 0)
    chooser = (place == slot_ref[...]).astype(wide).astype(low)
    out_ref[...] = dot(chooser, values_ref[...]).astype(low)


def expert_kernel(first, count, chunk, place_ref, in_ref, out_ref, grads_ref, more_grads_ref, *refs):
    pieces, more_pieces = refs[:count], refs[count : 2 * count]
    x_ref, ct_ref, active_ref, slope_ref, ffn_keep_ref, ffn_give_ref, keep_ref, give_ref = refs[-8:]
    step = pl.program_id(0)
    place = place_ref[0]
    capacity = pieces[0].shape[1]
    rows = 2 * capacity
    for k in range(count):

        @pl.when(step == k)
        def _(k=k):
            for c in range(2):
                x_ref[0, c * capacity : (c + 1) * capacity] = pieces[k][c]
                x_ref[0, rows + c * capacity : rows + (c + 1) * capacity] = more_pieces[k][c]

    source = place ^ (2 * (first + step))
    for c in range(2):
        ct_ref[0, c * capacity : (c + 1) * capacity] = grads_ref[source ^ c]
        ct_ref[0, rows + c * capacity : rows + (c + 1) * capacity] = more_grads_ref[source ^ c]
    x = x_ref[0]
    ct = ct_ref[0]
    total = ffn = None
    for start in range(0, in_ref.shape[1], chunk):
        stop = start + chunk
        pre = dot(x, in_ref[:, start:stop])
        gains = dot(ct, out_ref[start:stop], NT)
        active, slope = gelu_both(pre)
        active = active.astype(low)
        active_ref[0, :, start:stop] = active
        more = dot(active, out_ref[start:stop])
        ffn = more if ffn is None else ffn + more
        grad_pre = (gains * slope).astype(low)
        slope_ref[0, :, start:stop] = grad_pre
        term = dot(grad_pre, in_ref[:, start:stop], NT)
        total = term if total is None else total + term
    keep_ref[0] = total[:rows]
    give_ref[0] = total[rows:].astype(low)
    ffn_keep_ref[0] = ffn[:rows]
    ffn_give_ref[0] = ffn[rows:].astype(low)


def expert_group(
    place, weight_in, weight_out, grads, more_grads, pieces, more_pieces, buffers, span, chips, earlier
):
    first, stop = span
    count = stop - first
    capacity, width = pieces[0].shape[1:]
    hidden = weight_in.shape[1]
    rows = 4 * capacity
    operands = [place, weight_in, weight_out, grads, more_grads, *pieces, *more_pieces]
    specs = [spec_of(place)] + [
        pl.BlockSpec(x.shape, lambda i, n=x.ndim: (0,) * n) for x in operands[1:]
    ]
    aliases = {}
    if buffers is not None:
        aliases = {len(operands) + n: n for n in range(6)}
        operands += buffers
        specs += [pl.BlockSpec(memory_space=pl.ANY)] * 6

    def block(height, size, offset):
        return pl.BlockSpec((1, height, size), lambda i: (offset + i, 0, 0))

    res = run(
        functools.partial(expert_kernel, first, count, min(512, hidden)),
        operands,
        [
            kept((chips, rows, width), low),
            kept((chips, rows, width), low),
            kept((chips, rows, hidden), low),
            kept((chips, rows, hidden), low),
            kept((chips, rows // 2, width), wide),
            kept((chips, rows // 2, width), low),
            array((count, rows // 2, width), wide),
            array((count, rows // 2, width), low),
        ],
        flops=8 * count * rows * width * hidden,
        grid=(count,),
        in_specs=specs,
        out_specs=[
            block(rows, width, first),
            block(rows, width, first),
            block(rows, hidden, first),
            block(rows, hidden, first),
            block(rows // 2, width, first),
            block(rows // 2, width, first),
            block(rows // 2, width, 0),
            block(rows // 2, width, 0),
        ],
        input_output_aliases=aliases,
        first=earlier,
    )
    return res[:6], res[6], res[7]


def pieces_kernel(keep_ref, more_ref, *out_refs):
    capacity = out_refs[0].shape[1]
    for k, out_ref in enumerate(out_refs):
        total = (keep_ref[k] + more_ref[k].astype(wide)).astype(low)
        for c in range(2):
            out_ref[c] = total[c * capacity : (c + 1) * capacity]


def unpack_kernel(own_slot_ref, sibling_slot_ref, *refs):
    pieces, (own_ref, sibling_ref) = refs[:-2], refs[-2:]
    capacity = pieces[0].shape[1]
    slots = len(pieces) * capacity
    for source, (slot_ref, out_ref) in enumerate(
        ((own_slot_ref, own_ref), (sibling_slot_ref, sibling_ref))
    ):
        place = lax.broadcasted_iota(jnp.int32, (slots, out_ref.shape[0]), 0)
        chooser = (place == slot_ref[...]).astype(wide).astype(low)
        values = jnp.concatenate([piece[source] for piece in pieces], axis=0)
        out_ref[...] = dot(chooser, values, TN).astype(low)


def last_pieces_kernel(keep_ref, more_ref, ffn_ref, *refs):
    pieces_kernel(keep_ref, more_ref, *refs[:-1])
    refs[-1][...] = ffn_ref[...]


def product_kernel(left_ref, right_ref, out_ref):
    left, right = left_ref[...], right_ref[...]
    out_ref[...] = dot(
        left.reshape(-1, left.shape[-1]), right.reshape(-1, right.shape[-1]), TN
    )


def ffn_sum_kernel(place_ref, keep_ref, more_ref, out_ref):
    place = place_ref[0]
    capacity = out_ref.shape[1]
    for k in range(keep_ref.shape[0]):
        total = (keep_ref[k] + more_ref[k].astype(wide)).astype(low)
        for c in range(2):
            out_ref[place ^ (2 * k + c)] = total[c * capacity : (c + 1) * capacity]


def out_kernel(slot_ref, values_ref, middle_ref, out_ref):
    place = lax.broadcasted_iota(jnp.int32, (values_ref.shape[0], out_ref.shape[0]), 0)
    chooser = (place == slot_ref[...]).astype(wide).astype(low)
    out_ref[...] = (middle_ref[...] + dot(chooser, values_ref[...], TN)).astype(low)


def middle_back_kernel(
    chips, place_ref, own_ref, more_ref, middle_ref, ct_ref, scale_ref, weight_ref, other_ref, keep_ref, attended_ref,
    grad_ref, mine_ref, give_ref, sums_ref, output_ref, output_give_ref, parts,
):
    grad_second = own_ref[...].astype(wide) + more_ref[...].astype(wide)
    hat, inverse = normalize(middle_ref[...])
    sums_ref[0:1] = jnp.sum(grad_second * hat, axis=0, keepdims=True)
    sums_ref[1:2] = jnp.sum(grad_second, axis=0, keepdims=True)
    grad_middle = ct_ref[...].astype(wide) + norm_back(grad_second, hat, inverse, scale_ref[2:3])
    grad_ref[...] = grad_middle
    branch = grad_middle.astype(low)
    give_ref[...] = dot(branch, other_ref[...]).astype(low)
    mine_ref[...] = dot(branch, weight_ref[...]).astype(low)

    place = place_ref[0]
    turned = branch.astype(wide).T.astype(low)
    parts[0] = dot(turned, keep_ref[...])
    parts[1] = dot(turned, attended_ref[...])
    if chips:
        rows = output_ref.shape[2]
        for k in range(chips):
            block = pl.ds(pl.multiple_of((place ^ (2 * k)) * rows, rows), rows)
            output_ref[:, k] = parts[:, block]
            block = pl.ds(pl.multiple_of((place ^ (2 * k + 1)) * rows, rows), rows)
            output_give_ref[:, k] = parts[:, block].astype(low)
    else:
        output_ref[...] = parts[0]
        output_give_ref[...] = parts[1].astype(low)


def output_sum_kernel(own_ref, more_ref, keep_ref, give_ref):
    keep_ref[...] = own_ref[0] + more_ref[0].astype(wide)
    give_ref[...] = (own_ref[1] + more_ref[1].astype(wide)).astype(low)


def first_kernel(place_ref, grads_ref, full_ref, give_ref, own_ref):
    half = own_ref.shape[0]
    side = place_ref[1]
    for out_ref, first in ((give_ref, 1 - side), (own_ref, side)):
        rows = pl.ds(pl.multiple_of(first * half, half), half)
        total = None
        for n in range(3):
            term = dot(grads_ref[n, rows], full_ref[n], NT)
            total = term if total is None else total + term
        out_ref[...] = total.astype(out_ref.dtype)


def spread(sums):
    half = sums.shape[1] // 2
    rows = []
    rest = sums
    for _ in range(3):
        term = rest.astype(low).astype(wide)
        rest = rest - term
        rows += [term[:, :half], term[:, half:]]
    rows.append(jnp.zeros((8, half), wide))
    return jnp.concatenate(rows, axis=0).astype(low)


def gathered(rows):
    rows = rows.astype(wide)
    terms = [
        jnp.concatenate([rows[8 * n : 8 * n + 4], rows[8 * n + 4 : 8 * n + 8]], axis=1)
        for n in range(3)
    ]
    return (terms[0] + terms[1]) + terms[2]


def halves_kernel(
    keep_ref, more_ref, output_ref, more_output_ref, sums_ref, core_ref, across_ref, both_ref,
    near_ref, far_ref, out_sums_ref,
):
    count, size = near_ref.shape
    pieces = keep_ref.shape[1]
    height = count // pieces
    sums = (sums_ref[...] + core_ref[...]) + (across_ref[...] + both_ref[...])
    out_sums_ref[...] = sums
    far_ref[count:] = spread(sums)
    for side, ref in ((0, near_ref), (1, far_ref)):
        for k in range(pieces):
            total = keep_ref[side, k].astype(wide) + more_ref[side, k].astype(wide)
            total = total.reshape(-1, size).astype(low)
            ref[k * height : k * height + total.shape[0]] = total
            rest = output_ref[2 * k + side] + more_output_ref[2 * k + side].astype(wide)
            ref[k * height + total.shape[0] : (k + 1) * height] = rest.astype(low)


def quarters_kernel(near_ref, more_ref, sums_ref, own_ref, out_sums_ref, *out_refs):
    rows = own_ref.shape[0]
    sums = sums_ref[...] + gathered(more_ref[near_ref.shape[0] :])
    out_sums_ref[...] = sums
    packed = spread(sums)
    for n, ref in enumerate((own_ref, *out_refs)):
        block = slice(n * rows, (n + 1) * rows)
        total = near_ref[block].astype(wide) + more_ref[block].astype(wide)
        ref[:rows] = total.astype(ref.dtype)
        if n:
            ref[rows:] = packed


def total_kernel(own_ref, sums_ref, *refs):
    aways, (in_ref, out_ref), sums_refs = refs[:-6], refs[-6:-4], refs[-4:]
    rows = out_ref.shape[0]
    sums = [sums_ref[...]]
    total = own_ref[...]
    for ref in aways:
        total = total + ref[: own_ref.shape[0]].astype(wide)
        sums.append(gathered(ref[own_ref.shape[0] :]))
    while len(sums) > 1:
        sums = [x + y for x, y in zip(sums[0::2], sums[1::2])]
    for n, ref in enumerate(sums_refs):
        ref[...] = sums[0][n : n + 1].reshape(ref.shape)
    for n in range(3):
        in_ref[n] = total[n * rows : (n + 1) * rows]
    out_ref[...] = total[3 * rows :]


def input_grad_kernel(grad_ref, own_ref, more_ref, input_ref, scale_ref, out_ref):
    hat, inverse = normalize(input_ref[...].astype(wide))
    upstream = own_ref[...] + more_ref[...].astype(wide)
    out_ref[...] = grad_ref[...] + norm_back(upstream, hat, inverse, scale_ref[0:1])


def across(values):
    return lax.ppermute(values, "tp", [(0, 1), (1, 0)])


def swapped(values, offset):
    if offset == 0:
        return values
    count = lax.axis_size("fsdp")
    return lax.ppermute(values, "fsdp", [(i, i ^ offset) for i in range(count)])


def reduce_blocks(blocks, index, count):
    bit = 0
    part = blocks
    while count > 1:
        mine = (index >> bit) & 1
        split = part.reshape(count // 2, 2, *blocks.shape[1:])
        keep = lax.dynamic_index_in_dim(split, mine, 1, keepdims=False)
        give = lax.dynamic_index_in_dim(split, 1 - mine, 1, keepdims=False)
        got = swapped(give.astype(low), 1 << bit)
        part = keep.astype(wide) + got.astype(wide)
        if count > 2:
            part = part.astype(low)
        count //= 2
        bit += 1
    return part[0]


def tree_masks(lengths, parents, tree_size):
    segment_count = lengths.shape[0]
    number = jnp.arange(segment_count, dtype=jnp.int32)
    segment_end = jnp.sum(jnp.where(number[None, :] <= number[:, None], lengths[None, :], 0), axis=1)
    starts = segment_end - lengths
    position = jnp.arange(tree_size, dtype=jnp.int32)
    member = (
        (position[:, None] >= starts[None, :]) & (position[:, None] < segment_end[None, :])
    ).astype(wide)
    closure = jnp.maximum(
        jnp.eye(segment_count, dtype=wide), (parents[:, None] == number[None, :]).astype(wide)
    )
    steps = 1
    while steps < segment_count:
        closure = jnp.minimum(jnp.dot(closure, closure), 1.0)
        steps *= 2
    unreached = (1.0 - jnp.dot(member, closure)) * masked_score
    padding = ((0, 0), (0, LANES - segment_count))
    return jnp.pad(unreached, padding).astype(low), jnp.pad(member, padding).astype(low)


def shards(
    inputs,
    token_ids,
    hash_table,
    segment_lengths,
    segment_parents,
    first_gain,
    first_bias,
    input_weight,
    output_weight,
    second_gain,
    second_bias,
    expert_in,
    expert_out,
    cotangent,
):
    own_count, width = inputs.shape
    experts_in_all = lax.axis_size("fsdp")
    tree_size = token_ids.shape[0]
    capacity = 2 * own_count // experts_in_all
    local_width = input_weight.shape[2]
    chips = experts_in_all // 2
    shard_rows = input_weight.shape[1]
    hidden = expert_in.shape[2]
    index = lax.axis_index("fsdp")
    side = lax.axis_index("tp")
    place = jnp.stack([index, side]).astype(jnp.int32)
    in_kernel = shard_rows % 16 == 0
    scales = [first_gain, first_bias, second_gain, second_bias]

    other_inputs = across(inputs)
    shard = jnp.concatenate([input_weight, output_weight.T[None]])
    pieces = {0: shard}
    for k in range(2, chips, 2):
        pieces[k] = swapped(shard, 2 * k)
    for k in range(1, chips, 2):
        pieces[k] = swapped(pieces[k - 1], 2)
    mine = jnp.stack([pieces[k] for k in range(chips)])
    sibling = swapped(mine, 1)

    own_ids = lax.dynamic_slice_in_dim(token_ids, side * own_count, own_count, 0)
    table = hash_table.reshape(-1, LANES).astype(low)
    row_hot = (own_ids[:, None] // LANES == jnp.arange(table.shape[0])[None, :]).astype(low)
    lane_hot = own_ids[:, None] % LANES == jnp.arange(LANES)[None, :]
    experts = jnp.sum(jnp.where(lane_hot, dot(row_hot, table), 0.0), axis=1).astype(jnp.int32)
    hot = (experts[:, None] == jnp.arange(experts_in_all)[None, :]).astype(low)
    earlier = (jnp.arange(own_count)[:, None] > jnp.arange(own_count)[None, :]).astype(low)
    rank = jnp.sum(dot(earlier, hot) * hot.astype(wide), axis=1).astype(jnp.int32)
    own_slot = experts * capacity + rank
    sibling_slot = swapped(own_slot, 1)

    def chip_slot(slot):
        offset = (slot // capacity) ^ index
        return jnp.where(offset & 1 == 0, (offset >> 1) * capacity + slot % capacity, -1)

    own_place, sibling_place = chip_slot(own_slot), chip_slot(sibling_slot)

    slot_count = experts_in_all * capacity
    packed_grads = run(
        straight_pack_kernel,
        (cotangent, own_slot[None]),
        kept((slot_count, width), low),
        flops=2 * slot_count * own_count * width,
        first=(mine, other_inputs),
    )
    slot_grads = lax.all_to_all(
        packed_grads.reshape(experts_in_all, capacity, width), "fsdp", 0, 0, tiled=True
    )
    more_slot_grads = across(slot_grads)

    if in_kernel:
        weights = (mine, sibling)
    else:
        both = jnp.stack([mine, sibling], 1)
        both = both.reshape(experts_in_all, 4, shard_rows, local_width)
        full = jnp.concatenate(
            [lax.dynamic_index_in_dim(both, index ^ n, 0, False) for n in range(experts_in_all)], axis=1
        )
        weights = (full, full[:1, :16])
    full_weight, out_weight, projected, scales = run(
        functools.partial(project_kernel, chips if in_kernel else 0),
        (place, inputs, other_inputs, *scales, *weights),
        [
            kept((3, width, local_width), low),
            array((width, local_width), low),
            kept((tree_size, 3 * local_width), low),
            array((4, width), wide),
        ],
        flops=2 * tree_size * width * 3 * local_width,
    )
    other_out_weight = across(out_weight)
    unreached, member = tree_masks(segment_lengths[0], segment_parents[0], tree_size)
    attended, totals, attended_keep, attended_give = attend(place, projected, unreached, member)
    attended_more = across(attended_give)
    middle, second_normed = run(
        branch_kernel,
        (attended_keep, attended_more, out_weight, other_out_weight, inputs, scales),
        [kept((own_count, width), wide), array((own_count, width), low)],
        flops=2 * own_count * width * width,
    )

    sibling_normed = swapped(second_normed, 1)
    piece = array((2, capacity, width), low)
    packed = run(
        pack_kernel,
        (second_normed, sibling_normed, own_place[None], sibling_place[None]),
        [piece] * chips,
        first=(slot_grads,),
        flops=4 * own_count * own_count * width,
    )
    quarter = chips // 4
    near, next_near, far, next_far = [(n * quarter, (n + 1) * quarter) for n in range(4)]
    arrived = {}
    for span in (far, near, next_near):
        for k in range(*span):
            arrived[k] = swapped(packed[k], 2 * k)
    for k in range(*next_far):
        arrived[k] = swapped(packed[k], 2 * k)
    spans = (near, far, next_far, next_near)
    more_arrived = {k: across(arrived[k]) for span in spans for k in range(*span)}

    turned, turned_done = run(
        turned_kernel,
        (place, Far(inputs), Far(other_inputs), scales),
        kept((width, tree_size), low),
        mark=True,
        first=(packed[0],),
    )

    weight_in, weight_out = expert_in[0], expert_out[0]
    buffers = None
    returned = {}
    sent = []
    done = []
    back = []
    for turn, span in enumerate(spans):
        own_pieces = [arrived[k] for k in range(*span)]
        buffers, keep, give = expert_group(
            place, weight_in, weight_out, slot_grads, more_slot_grads,
            own_pieces, [more_arrived[k] for k in range(*span)], buffers, span, chips,
            [turned_done] + [arrived[k] for k in range(1, chips)] if turn == 0 else [],
        )
        sent.append((span, keep, across(give)))
    slot_rows, grad_rows, actives, grad_pres, ffn_keep, ffn_give = buffers
    rows = 4 * capacity
    for turn, (span, keep, more) in enumerate(sent):
        if turn == 2:
            *sums, ffn_give, token = run(
                last_pieces_kernel,
                (keep, more, Far(ffn_give)),
                [piece] * quarter + [array(ffn_give.shape, low)],
                mark=True,
            )
        else:
            *sums, token = run(pieces_kernel, (keep, more), [piece] * quarter, mark=True)
        done.append(token)
        for k in range(*span):
            returned[k] = swapped(sums[k - span[0]], 2 * k)
        back.append([returned[k] for k in range(*span)])
    ffn_done = done[2]
    ffn_more = across(ffn_give)
    tile = min(512, hidden)
    stripe = pl.BlockSpec((chips, rows, tile), lambda i: (0, 0, i))
    fixed = pl.BlockSpec((chips, rows, width), lambda i: (0, 0, 0))
    expert_out_grad, out_done = run(
        product_kernel,
        (in_hbm(actives), in_hbm(grad_rows)),
        array((hidden, width), wide),
        flops=2 * chips * rows * width * hidden,
        first=(ffn_done, done[3], *back[0], *back[1]),
        mark=True,
        grid=(hidden // tile,),
        in_specs=[stripe, fixed],
        out_specs=[pl.BlockSpec((tile, width), lambda i: (i, 0))],
    )
    own_part, sibling_part = run(
        unpack_kernel,
        (own_place[None], sibling_place[None], *[returned[k] for k in range(chips)]),
        [array((own_count, width), low)] * 2,
        first=(out_done, *back[2]),
        flops=4 * own_count * own_count * width,
    )
    sibling_part = swapped(sibling_part, 1)
    if in_kernel:
        blocks = (2, chips, shard_rows, local_width)
        output_outs = [array(blocks, wide), array(blocks, low)]
    else:
        output_outs = [array((width, local_width), wide), array((width, local_width), low)]
    grad_middle, grad_mine, grad_give, second_sums, output_own, output_give, middle_done = run(
        functools.partial(middle_back_kernel, chips if in_kernel else 0),
        (
            place, own_part, sibling_part, Far(middle), Far(cotangent), scales,
            Far(out_weight), Far(other_out_weight), Far(attended_keep), Far(attended_more),
        ),
        [
            kept((own_count, width), wide),
            array((own_count, local_width), low),
            array((own_count, local_width), low),
            array((2, width), wide),
            *output_outs,
        ],
        first=(ffn_more,),
        mark=True,
        scratch_shapes=[pltpu.VMEM((2, width, local_width), wide)],
        flops=4 * own_count * width * width,
    )
    grad_more = across(grad_give)
    ffn_sums, sums_done = run(
        ffn_sum_kernel,
        (place, Far(ffn_keep), ffn_more),
        kept((experts_in_all, capacity, width), low),
        mark=True,
        first=(middle_done,),
    )
    ffn_back = lax.all_to_all(ffn_sums, "fsdp", 0, 0, tiled=True)

    if in_kernel:
        output_own, output_give, output_done = run(
            output_sum_kernel,
            (output_own, swapped(output_give, 1)),
            [array(blocks[1:], wide), array(blocks[1:], low)],
            mark=True,
        )
    else:
        output_done = middle_done
    output_more = across(output_give)
    grad_projected, part_keep, part_give, norm_sums = attend_back(
        place, projected, unreached, member, attended, totals, grad_mine, grad_more,
        turned, full_weight, scales, second_sums,
        chips if in_kernel else 0, first=(sums_done, output_done),
    )

    if in_kernel:
        part_more = swapped(part_give, 1)
        rows = 4 * shard_rows
        near_sum, far_sum, norm_sums, half_done = run(
            halves_kernel,
            (
                part_keep, part_more, output_own, output_more,
                norm_sums, swapped(norm_sums, 1), across(norm_sums),
                lax.ppermute(norm_sums, ("fsdp", "tp"), [(i, i ^ 3) for i in range(2 * experts_in_all)]),
            ),
            [
                kept((chips // 2 * rows, local_width), low),
                kept((chips // 2 * rows + 32, local_width), low),
                array((4, width), wide),
            ],
            mark=True,
        )
    else:
        half_done = norm_sums
    first_give, first_own, give_done = run(
        first_kernel,
        (place, Far(grad_projected), Far(full_weight)),
        [array((own_count, width), low), array((own_count, width), wide)],
        mark=True,
        first=(half_done,),
        light=True,
        flops=2 * tree_size * width * 3 * local_width,
    )
    first_more = across(first_give)
    expert_in_grad, in_done = run(
        product_kernel,
        (in_hbm(slot_rows), in_hbm(grad_pres)),
        array((width, hidden), wide),
        flops=2 * chips * capacity * 4 * width * hidden,
        first=(give_done,),
        mark=True,
        light=True,
        grid=(hidden // tile,),
        in_specs=[fixed, stripe],
        out_specs=[pl.BlockSpec((width, tile), lambda i: (0, i))],
    )
    if in_kernel:
        own_sum, norm_sums, *away = run(
            quarters_kernel,
            (Far(near_sum), Far(swapped(far_sum, 2)), norm_sums),
            [array((rows, local_width), wide), array((4, width), wide)]
            + [array((rows + 32, local_width), low)] * (chips // 2 - 1),
            first=(in_done, ffn_back),
        )
        away = [swapped(away[k - 1], 4 * k) for k in range(1, chips // 2)]
    else:
        output_part = (output_own + output_more.astype(wide)).astype(low)
        blocks = jnp.concatenate([part_keep, output_part[None]])
        blocks = blocks.reshape(4, experts_in_all, shard_rows, local_width).transpose(1, 0, 2, 3)
        summed = reduce_blocks(blocks, index, experts_in_all)
        bit = 1
        while bit < experts_in_all:
            norm_sums = norm_sums + swapped(norm_sums, bit)
            bit *= 2
        norm_sums = norm_sums + across(norm_sums)
    input_grad, input_done = run(
        input_grad_kernel,
        (Far(grad_middle), first_own, first_more, Far(inputs), scales),
        array((own_count, width), wide),
        mark=True,
        light=True,
    )
    out_block, out_done = run(
        out_kernel,
        (own_slot[None], ffn_back.reshape(slot_count, width), Far(middle)),
        array((own_count, width), low),
        mark=True,
        light=True,
        flops=2 * own_count * slot_count * width,
    )
    if in_kernel:
        input_weight_grad, output_weight_grad, *norm_sums = run(
            total_kernel,
            (own_sum, norm_sums, *away),
            [
                array((3, shard_rows, local_width), wide),
                array((shard_rows, local_width), wide),
                *[array((width,), wide)] * 4,
            ],
            first=(input_done, out_done),
        )
    else:
        input_weight_grad, output_weight_grad = summed[:3], summed[3]
    output_weight_grad = output_weight_grad.T
    return (
        out_block,
        input_grad,
        norm_sums[0],
        norm_sums[1],
        input_weight_grad,
        output_weight_grad,
        norm_sums[2],
        norm_sums[3],
        expert_in_grad[None],
        expert_out_grad[None],
    )


def solution(mesh):
    return jax.shard_map(
        shards,
        mesh=mesh,
        in_specs=(
            P(("fsdp", "tp"), None),
            P("fsdp"),
            P(),
            P("fsdp", None),
            P("fsdp", None),
            P(),
            P(),
            P(None, "fsdp", "tp"),
            P("tp", "fsdp"),
            P(),
            P(),
            P("fsdp", None, "tp"),
            P("fsdp", "tp", None),
            P(("fsdp", "tp"), None),
        ),
        out_specs=(
            P(("fsdp", "tp"), None),
            P(("fsdp", "tp"), None),
            P(),
            P(),
            P(None, "fsdp", "tp"),
            P("tp", "fsdp"),
            P(),
            P(),
            P("fsdp", None, "tp"),
            P("fsdp", "tp", None),
        ),
        check_vma=False,
    )
```

```python
import functools
import math

import jax
import jax.numpy as jnp
from jax import lax
from jax.experimental import pallas as pl
from jax.experimental.pallas import tpu as pltpu
from jax.sharding import PartitionSpec as P

HD = 64
LANES = 128

norm_eps = 1e-05
masked_score = -1e30
gelu_root = 0.7978845608028654
gelu_cubic = 0.044715
low = jnp.bfloat16
wide = jnp.float32

NN = (((1,), (0,)), ((), ()))
NT = (((1,), (1,)), ((), ()))
TN = (((0,), (0,)), ((), ()))


def dot(left, right, dims=NN):
    return lax.dot_general(left, right, dims, preferred_element_type=wide)


def gelu_both(values):
    squared = values * values
    tangent = jnp.tanh(values * (gelu_root + gelu_root * gelu_cubic * squared))
    half_up = 0.5 + 0.5 * tangent
    active = values * half_up
    slope = half_up + active * (1.0 - half_up) * (
        2.0 * gelu_root + 6.0 * gelu_root * gelu_cubic * squared
    )
    return active, slope


def normalize(values):
    average = jnp.mean(values, axis=-1, keepdims=True)
    centred = values - average
    inverse = lax.rsqrt(jnp.mean(centred * centred, axis=-1, keepdims=True) + norm_eps)
    return (centred * inverse, inverse)


def norm_back(upstream, normed, inverse, gain):
    scaled = upstream * gain
    centred_grad = (
        scaled
        - jnp.mean(scaled, axis=-1, keepdims=True)
        - normed * jnp.mean(scaled * normed, axis=-1, keepdims=True)
    )
    return inverse * centred_grad


def array(shape, kind):
    return jax.ShapeDtypeStruct(shape, kind)


def kept(shape, kind):
    return pltpu.HBM(shape, kind)


def size_of(x):
    return math.prod(x.shape) * jnp.dtype(x.dtype).itemsize


def run(kernel, operands, outs, flops=0, limit=32, first=(), mark=False, light=False, **more):
    if "in_specs" not in more:
        more["in_specs"] = [spec_of(x) for x in operands]
    operands = [in_hbm(x.values) if isinstance(x, Far) else x for x in operands]
    alone = not isinstance(outs, list)
    outs = [outs] if alone else list(outs)
    count, results = len(operands), len(outs)
    moved = sum(map(size_of, operands)) + sum(map(size_of, outs))
    if light:
        flops = moved = 0
    first = tuple(first)
    more["in_specs"] = list(more["in_specs"]) + [pl.BlockSpec(memory_space=pl.ANY)] * len(first)
    if mark:
        outs.append(array((8, LANES), wide))
    if "out_specs" in more:
        more["out_specs"] = list(more["out_specs"])
        if mark:
            more["out_specs"].append(pl.BlockSpec((8, LANES), lambda *i: (0, 0)))

    def whole(*refs):
        end = count + len(first) + results
        if mark:
            refs[end][...] = jnp.zeros((8, LANES), wide)
        kernel(*refs[:count], *refs[count + len(first) : end], *refs[end + mark :])

    res = pl.pallas_call(
        whole,
        out_shape=outs,
        compiler_params=pltpu.CompilerParams(vmem_limit_bytes=limit << 20),
        cost_estimate=pl.CostEstimate(flops=int(flops), bytes_accessed=int(moved), transcendentals=0),
        **more,
    )(*operands, *first)
    return res[0] if alone and not mark else res


def in_hbm(x):
    return pltpu.with_memory_space_constraint(x, pltpu.HBM)


class Far:
    def __init__(self, values):
        self.values = values


def spec_of(x):
    if isinstance(x, Far):
        shape = x.values.shape
        return pl.BlockSpec(shape, lambda *i: (0,) * len(shape))
    scalar = x.ndim == 1 and x.dtype == jnp.int32
    return pl.BlockSpec(memory_space=pltpu.SMEM if scalar else pltpu.VMEM)


def project_kernel(
    chips, place_ref, own_ref, other_ref, gain_ref, bias_ref, gain2_ref, bias2_ref, mine_ref, sibling_ref,
    full_ref, last_ref, out_ref, scale_ref
):
    place, side = place_ref[0], place_ref[1]
    for n, ref in enumerate((gain_ref, bias_ref, gain2_ref, bias2_ref)):
        scale_ref[n : n + 1] = ref[...].reshape(1, ref.shape[0])
    if chips:
        rows = mine_ref.shape[2]
        for k in range(chips):
            for ref, source in ((mine_ref, place ^ (2 * k)), (sibling_ref, place ^ (2 * k + 1))):
                block = pl.ds(pl.multiple_of(source * rows, rows), rows)
                full_ref[:, block, :] = ref[k, :3]
                last_ref[block, :] = ref[k, 3]
    else:
        full_ref[...] = mine_ref[:3]
        last_ref[...] = mine_ref[3]
    count, width = own_ref.shape[0], mine_ref.shape[-1]
    for ref, first in ((own_ref, side * count), (other_ref, (1 - side) * count)):
        hat, _ = normalize(ref[...].astype(wide))
        normed = (hat * scale_ref[0:1] + scale_ref[1:2]).astype(low)
        for n in range(3):
            out_ref[pl.ds(pl.multiple_of(first, count), count), n * width : (n + 1) * width] = dot(
                normed, full_ref[n]
            ).astype(low)


def turned_kernel(place_ref, own_ref, other_ref, scale_ref, out_ref):
    side = place_ref[1]
    count = own_ref.shape[0]
    for ref, first in ((own_ref, side * count), (other_ref, (1 - side) * count)):
        hat, _ = normalize(ref[...].astype(wide))
        normed = (hat * scale_ref[0:1] + scale_ref[1:2]).T
        out_ref[:, pl.ds(pl.multiple_of(first, count), count)] = normed.astype(low)


def attend_kernel(block, place_ref, q_ref, k_ref, v_ref, unreached_ref, member_ref, out_ref, total_ref, keep_ref, give_ref):
    side = place_ref[1]
    rows = q_ref.shape[0]
    lane = lax.broadcasted_iota(jnp.int32, (1, LANES), 1)
    first_head = lane < HD
    ones = jnp.ones((rows, LANES), low)
    keys = jnp.concatenate([k_ref[...], member_ref[...]], axis=1)
    values = jnp.concatenate([v_ref[...], ones], axis=1)
    row = lax.rem(lax.broadcasted_iota(jnp.int32, (2 * block, block), 0), block)
    causal = lax.broadcasted_iota(jnp.int32, (2 * block, block), 1) <= row
    for start in range(0, rows, block):
        stop = start + block
        query = q_ref[start:stop] * HD**-0.5
        zero = jnp.zeros_like(query)
        unreached = unreached_ref[start:stop]
        left = jnp.concatenate(
            [
                jnp.concatenate([jnp.where(first_head, query, zero), unreached], axis=1),
                jnp.concatenate([jnp.where(first_head, zero, query), unreached], axis=1),
            ]
        ).astype(low)
        scores = dot(left, keys[:stop], NT)
        near = jnp.where(causal, scores[:, start:], masked_score)
        top = jnp.max(near, axis=1, keepdims=True)
        if start:
            far = scores[:, :start]
            top = jnp.maximum(top, jnp.max(far, axis=1, keepdims=True))
            weights = jnp.concatenate(
                [jnp.exp(far - top).astype(low), jnp.exp(near - top).astype(low)], axis=1
            )
        else:
            weights = jnp.exp(near - top).astype(low)
        sums = dot(weights, values[:stop], NN)
        total = sums[:, LANES:]
        attended = sums[:, :LANES] / total
        total = top + jnp.log(total)
        out_ref[start:stop] = jnp.where(first_head, attended[:block], attended[block:]).astype(low)
        total_ref[start:stop] = jnp.where(first_head, total[:block], total[block:])
    half = rows // 2
    keep_ref[...] = out_ref[pl.ds(pl.multiple_of(side * half, half), half)]
    give_ref[...] = out_ref[pl.ds(pl.multiple_of((1 - side) * half, half), half)]


def attend(place, projected, unreached, member, block=256):
    rows, width = projected.shape
    pairs = width // (3 * LANES)

    def part(n, height=rows):
        return pl.BlockSpec((height, LANES), lambda p: (0, n * pairs + p))

    fixed = pl.BlockSpec((rows, LANES), lambda p: (0, 0))
    return run(
        functools.partial(attend_kernel, block),
        (place, in_hbm(projected), in_hbm(projected), in_hbm(projected), unreached, member),
        [
            kept((rows, width // 3), low),
            kept((rows, width // 3), wide),
            array((rows // 2, width // 3), low),
            array((rows // 2, width // 3), low),
        ],
        flops=12e9,
        grid=(pairs,),
        in_specs=[spec_of(place), part(0), part(1), part(2), fixed, fixed],
        out_specs=[part(0), part(0), part(0, rows // 2), part(0, rows // 2)],
    )


def attend_back_kernel(
    chips, block, place_ref, q_ref, k_ref, v_ref, unreached_ref, member_ref, out_ref, total_ref, mine_ref, more_ref,
    turned_ref, weight_ref, scale_ref, second_ref,
    res_ref, keep_ref, give_ref, sums_ref, dk, dv, grads, parts, products, columns,
):
    place, side = place_ref[0], place_ref[1]
    step = pl.program_id(0)
    rows = q_ref.shape[0]
    half = rows // 2
    grads[pl.ds(pl.multiple_of(side * half, half), half)] = mine_ref[...]
    grads[pl.ds(pl.multiple_of((1 - side) * half, half), half)] = more_ref[...]
    lane = lax.broadcasted_iota(jnp.int32, (1, LANES), 1)
    first_head = lane < HD
    keys = jnp.concatenate([k_ref[...], member_ref[...]], axis=1)
    causal = lax.broadcasted_iota(jnp.int32, (block, block), 1) <= lax.broadcasted_iota(
        jnp.int32, (block, block), 0
    )
    for start in range(rows - block, -1, -block):
        stop = start + block
        query = q_ref[start:stop] * HD**-0.5
        unreached = unreached_ref[start:stop]
        grad = grads[start:stop]
        both = grad.astype(wide) * out_ref[start:stop].astype(wide)
        query_halves = []
        key_terms = []
        value_terms = []
        for head, own in enumerate((first_head, ~first_head)):
            q_own = jnp.where(own, query, 0).astype(low)
            g_own = jnp.where(own, grad, 0).astype(low)
            scores = dot(jnp.concatenate([q_own, unreached], axis=1), keys[:stop], NT)
            total = total_ref[start:stop, HD * head : HD * head + 1]
            centre = jnp.sum(jnp.where(own, both, 0.0), axis=1, keepdims=True)
            near = jnp.exp(jnp.where(causal, scores[:, start:], masked_score) - total)
            if start:
                weights = jnp.concatenate([jnp.exp(scores[:, :start] - total), near], axis=1)
            else:
                weights = near
            gains = dot(g_own, v_ref[:stop], NT)
            slopes = (weights * (gains - centre)).astype(low)
            query_halves.append(dot(slopes, k_ref[:stop], NN))
            key_terms.append(dot(slopes, q_own, TN))
            value_terms.append(dot(weights.astype(low), g_own, TN))
        res_ref[0, start:stop] = (
            jnp.where(first_head, query_halves[0], query_halves[1]) * HD**-0.5
        ).astype(low)
        if stop == rows:
            dk[...] = key_terms[0] + key_terms[1]
            dv[...] = value_terms[0] + value_terms[1]
        else:
            dk[:stop] += key_terms[0] + key_terms[1]
            dv[:stop] += value_terms[0] + value_terms[1]
    res_ref[1] = dk[...].astype(low)
    res_ref[2] = dv[...].astype(low)

    pair = dot(turned_ref[...], jnp.concatenate([res_ref[0], res_ref[1]], axis=1))
    grads_in = (pair[:, :LANES], pair[:, LANES:], dot(turned_ref[...], res_ref[2]))
    product = column = None
    for n, grad_in in enumerate(grads_in):
        weight = weight_ref[n].astype(wide)
        total = jnp.sum(res_ref[n].astype(wide), axis=0, keepdims=True)
        terms = weight * grad_in, weight * total
        product = terms[0] if n == 0 else product + terms[0]
        column = terms[1] if n == 0 else column + terms[1]
        parts[n] = grad_in.astype(low)

    @pl.when(step == 0)
    def _():
        products[...] = product
        columns[...] = column

    @pl.when(step > 0)
    def _():
        products[...] += product
        columns[...] += column

    lanes = pl.ds(pl.multiple_of(step * LANES, LANES), LANES)
    if chips:
        height = keep_ref.shape[3]
        for k in range(chips):
            for ref, target in ((keep_ref, place ^ (2 * k)), (give_ref, place ^ (2 * k + 1))):
                ref[k % 2, k // 2, :, :, lanes] = parts[
                    :, pl.ds(pl.multiple_of(target * height, height), height)
                ]
    else:
        keep_ref[:, :, lanes] = parts[...]
        give_ref[...] = jnp.zeros(give_ref.shape, low)

    @pl.when(step == pl.num_programs(0) - 1)
    def _():
        bias_grad = jnp.sum(columns[...].T, axis=0, keepdims=True)
        whole = jnp.sum(products[...].T, axis=0, keepdims=True)
        sums_ref[0:1] = (whole - scale_ref[1:2] * bias_grad) / scale_ref[0:1]
        sums_ref[1:2] = bias_grad
        sums_ref[2:4] = second_ref[...]


def attend_back(
    place, projected, unreached, member, out, total, mine, more, turned, weight, scales, second,
    chips, block=256, first=(),
):
    rows, width = projected.shape
    pairs = width // (3 * LANES)
    features = turned.shape[0]

    def part(n, height=rows):
        return pl.BlockSpec((height, LANES), lambda p: (0, n * pairs + p))

    def fixed(shape):
        return pl.BlockSpec(shape, lambda p: (0,) * len(shape))

    if chips:
        shape = (2, chips // 2, 3, features // (2 * chips), width // 3)
        shapes = [shape, shape]
    else:
        shapes = [(3, features, width // 3), (8, LANES)]
    triple = pl.BlockSpec((3, rows, LANES), lambda p: (0, 0, p))
    return run(
        functools.partial(attend_back_kernel, chips, block),
        (
            place, in_hbm(projected), in_hbm(projected), in_hbm(projected), unreached, member,
            in_hbm(out), in_hbm(total), mine, more, in_hbm(turned), in_hbm(weight), scales, second,
        ),
        [kept((3, rows, width // 3), low), *[array(x, low) for x in shapes], array((4, features), wide)],
        flops=30e9,
        limit=44,
        first=first,
        grid=(pairs,),
        in_specs=[spec_of(place), part(0), part(1), part(2), fixed(unreached.shape), fixed(member.shape)]
        + [part(0), part(0), part(0, rows // 2), part(0, rows // 2), fixed(turned.shape)]
        + [pl.BlockSpec((3, features, LANES), lambda p: (0, 0, p)), fixed(scales.shape)]
        + [fixed(second.shape)],
        out_specs=[triple, fixed(shapes[0]), fixed(shapes[1]), fixed((4, features))],
        scratch_shapes=[pltpu.VMEM((rows, LANES), wide)] * 2
        + [pltpu.VMEM((rows, LANES), low), pltpu.VMEM((3, features, LANES), low)]
        + [pltpu.VMEM((features, LANES), wide)] * 2,
    )


def branch_kernel(keep_ref, more_ref, weight_ref, other_ref, residual_ref, scale_ref, middle_ref, normed_ref):
    branch = dot(keep_ref[...], weight_ref[...], NT) + dot(more_ref[...], other_ref[...], NT)
    middle = residual_ref[...].astype(wide) + branch
    middle_ref[...] = middle
    hat, _ = normalize(middle)
    normed_ref[...] = (hat * scale_ref[2:3] + scale_ref[3:4]).astype(low)


def pack_kernel(own_ref, sibling_ref, own_slot_ref, sibling_slot_ref, *out_refs):
    capacity = out_refs[0].shape[1]
    slots = len(out_refs) * capacity
    for source, (ref, slot_ref) in enumerate(
        ((own_ref, own_slot_ref), (sibling_ref, sibling_slot_ref))
    ):
        place = lax.broadcasted_iota(jnp.int32, (slots, ref.shape[0]), 0)
        chooser = (place == slot_ref[...]).astype(wide).astype(low)
        packed = dot(chooser, ref[...]).astype(low)
        for k, out_ref in enumerate(out_refs):
            out_ref[source] = packed[k * capacity : (k + 1) * capacity]


def straight_pack_kernel(values_ref, slot_ref, out_ref):
    place = lax.broadcasted_iota(jnp.int32, (out_ref.shape[0], values_ref.shape[0]), 0)
    chooser = (place == slot_ref[...]).astype(wide).astype(low)
    out_ref[...] = dot(chooser, values_ref[...]).astype(low)


def expert_kernel(first, count, chunk, place_ref, in_ref, out_ref, grads_ref, more_grads_ref, *refs):
    pieces, more_pieces = refs[:count], refs[count : 2 * count]
    x_ref, ct_ref, active_ref, slope_ref, ffn_keep_ref, ffn_give_ref, keep_ref, give_ref = refs[-8:]
    step = pl.program_id(0)
    place = place_ref[0]
    capacity = pieces[0].shape[1]
    rows = 2 * capacity
    for k in range(count):

        @pl.when(step == k)
        def _(k=k):
            for c in range(2):
                x_ref[0, c * capacity : (c + 1) * capacity] = pieces[k][c]
                x_ref[0, rows + c * capacity : rows + (c + 1) * capacity] = more_pieces[k][c]

    source = place ^ (2 * (first + step))
    for c in range(2):
        ct_ref[0, c * capacity : (c + 1) * capacity] = grads_ref[source ^ c]
        ct_ref[0, rows + c * capacity : rows + (c + 1) * capacity] = more_grads_ref[source ^ c]
    x = x_ref[0]
    ct = ct_ref[0]
    total = ffn = None
    for start in range(0, in_ref.shape[1], chunk):
        stop = start + chunk
        pre = dot(x, in_ref[:, start:stop])
        gains = dot(ct, out_ref[start:stop], NT)
        active, slope = gelu_both(pre)
        active = active.astype(low)
        active_ref[0, :, start:stop] = active
        more = dot(active, out_ref[start:stop])
        ffn = more if ffn is None else ffn + more
        grad_pre = (gains * slope).astype(low)
        slope_ref[0, :, start:stop] = grad_pre
        term = dot(grad_pre, in_ref[:, start:stop], NT)
        total = term if total is None else total + term
    keep_ref[0] = total[:rows]
    give_ref[0] = total[rows:].astype(low)
    ffn_keep_ref[0] = ffn[:rows]
    ffn_give_ref[0] = ffn[rows:].astype(low)


def expert_group(
    place, weight_in, weight_out, grads, more_grads, pieces, more_pieces, buffers, span, chips, earlier
):
    first, stop = span
    count = stop - first
    capacity, width = pieces[0].shape[1:]
    hidden = weight_in.shape[1]
    rows = 4 * capacity
    operands = [place, weight_in, weight_out, grads, more_grads, *pieces, *more_pieces]
    specs = [spec_of(place)] + [
        pl.BlockSpec(x.shape, lambda i, n=x.ndim: (0,) * n) for x in operands[1:]
    ]
    aliases = {}
    if buffers is not None:
        aliases = {len(operands) + n: n for n in range(6)}
        operands += buffers
        specs += [pl.BlockSpec(memory_space=pl.ANY)] * 6

    def block(height, size, offset):
        return pl.BlockSpec((1, height, size), lambda i: (offset + i, 0, 0))

    res = run(
        functools.partial(expert_kernel, first, count, min(512, hidden)),
        operands,
        [
            kept((chips, rows, width), low),
            kept((chips, rows, width), low),
            kept((chips, rows, hidden), low),
            kept((chips, rows, hidden), low),
            kept((chips, rows // 2, width), wide),
            kept((chips, rows // 2, width), low),
            array((count, rows // 2, width), wide),
            array((count, rows // 2, width), low),
        ],
        flops=8 * count * rows * width * hidden,
        grid=(count,),
        in_specs=specs,
        out_specs=[
            block(rows, width, first),
            block(rows, width, first),
            block(rows, hidden, first),
            block(rows, hidden, first),
            block(rows // 2, width, first),
            block(rows // 2, width, first),
            block(rows // 2, width, 0),
            block(rows // 2, width, 0),
        ],
        input_output_aliases=aliases,
        first=earlier,
    )
    return res[:6], res[6], res[7]


def pieces_kernel(keep_ref, more_ref, *out_refs):
    capacity = out_refs[0].shape[1]
    for k, out_ref in enumerate(out_refs):
        total = (keep_ref[k] + more_ref[k].astype(wide)).astype(low)
        for c in range(2):
            out_ref[c] = total[c * capacity : (c + 1) * capacity]


def unpack_kernel(own_slot_ref, sibling_slot_ref, *refs):
    pieces, (own_ref, sibling_ref) = refs[:-2], refs[-2:]
    capacity = pieces[0].shape[1]
    slots = len(pieces) * capacity
    for source, (slot_ref, out_ref) in enumerate(
        ((own_slot_ref, own_ref), (sibling_slot_ref, sibling_ref))
    ):
        place = lax.broadcasted_iota(jnp.int32, (slots, out_ref.shape[0]), 0)
        chooser = (place == slot_ref[...]).astype(wide).astype(low)
        values = jnp.concatenate([piece[source] for piece in pieces], axis=0)
        out_ref[...] = dot(chooser, values, TN).astype(low)


def last_pieces_kernel(keep_ref, more_ref, ffn_ref, *refs):
    pieces_kernel(keep_ref, more_ref, *refs[:-1])
    refs[-1][...] = ffn_ref[...]


def product_kernel(left_ref, right_ref, out_ref):
    left, right = left_ref[...], right_ref[...]
    out_ref[...] = dot(
        left.reshape(-1, left.shape[-1]), right.reshape(-1, right.shape[-1]), TN
    )


def ffn_sum_kernel(place_ref, keep_ref, more_ref, out_ref):
    place = place_ref[0]
    capacity = out_ref.shape[1]
    for k in range(keep_ref.shape[0]):
        total = (keep_ref[k] + more_ref[k].astype(wide)).astype(low)
        for c in range(2):
            out_ref[place ^ (2 * k + c)] = total[c * capacity : (c + 1) * capacity]


def out_kernel(slot_ref, values_ref, middle_ref, out_ref):
    place = lax.broadcasted_iota(jnp.int32, (values_ref.shape[0], out_ref.shape[0]), 0)
    chooser = (place == slot_ref[...]).astype(wide).astype(low)
    out_ref[...] = (middle_ref[...] + dot(chooser, values_ref[...], TN)).astype(low)


def middle_back_kernel(
    chips, place_ref, own_ref, more_ref, middle_ref, ct_ref, scale_ref, weight_ref, other_ref, keep_ref, attended_ref,
    grad_ref, mine_ref, give_ref, sums_ref, output_ref, output_give_ref, parts,
):
    grad_second = own_ref[...].astype(wide) + more_ref[...].astype(wide)
    hat, inverse = normalize(middle_ref[...])
    sums_ref[0:1] = jnp.sum(grad_second * hat, axis=0, keepdims=True)
    sums_ref[1:2] = jnp.sum(grad_second, axis=0, keepdims=True)
    grad_middle = ct_ref[...].astype(wide) + norm_back(grad_second, hat, inverse, scale_ref[2:3])
    grad_ref[...] = grad_middle
    branch = grad_middle.astype(low)
    give_ref[...] = dot(branch, other_ref[...]).astype(low)
    mine_ref[...] = dot(branch, weight_ref[...]).astype(low)

    place = place_ref[0]
    turned = branch.astype(wide).T.astype(low)
    parts[0] = dot(turned, keep_ref[...])
    parts[1] = dot(turned, attended_ref[...])
    if chips:
        rows = output_ref.shape[2]
        for k in range(chips):
            block = pl.ds(pl.multiple_of((place ^ (2 * k)) * rows, rows), rows)
            output_ref[:, k] = parts[:, block]
            block = pl.ds(pl.multiple_of((place ^ (2 * k + 1)) * rows, rows), rows)
            output_give_ref[:, k] = parts[:, block].astype(low)
    else:
        output_ref[...] = parts[0]
        output_give_ref[...] = parts[1].astype(low)


def output_sum_kernel(own_ref, more_ref, keep_ref, give_ref):
    keep_ref[...] = own_ref[0] + more_ref[0].astype(wide)
    give_ref[...] = (own_ref[1] + more_ref[1].astype(wide)).astype(low)


def first_kernel(place_ref, grads_ref, full_ref, give_ref, own_ref):
    half = own_ref.shape[0]
    side = place_ref[1]
    for out_ref, first in ((give_ref, 1 - side), (own_ref, side)):
        rows = pl.ds(pl.multiple_of(first * half, half), half)
        total = None
        for n in range(3):
            term = dot(grads_ref[n, rows], full_ref[n], NT)
            total = term if total is None else total + term
        out_ref[...] = total.astype(out_ref.dtype)


def spread(sums):
    half = sums.shape[1] // 2
    rows = []
    rest = sums
    for _ in range(3):
        term = rest.astype(low).astype(wide)
        rest = rest - term
        rows += [term[:, :half], term[:, half:]]
    rows.append(jnp.zeros((8, half), wide))
    return jnp.concatenate(rows, axis=0).astype(low)


def gathered(rows):
    rows = rows.astype(wide)
    terms = [
        jnp.concatenate([rows[8 * n : 8 * n + 4], rows[8 * n + 4 : 8 * n + 8]], axis=1)
        for n in range(3)
    ]
    return (terms[0] + terms[1]) + terms[2]


def halves_kernel(
    keep_ref, more_ref, output_ref, more_output_ref, sums_ref, core_ref, across_ref, both_ref,
    near_ref, far_ref, out_sums_ref,
):
    count, size = near_ref.shape
    pieces = keep_ref.shape[1]
    height = count // pieces
    sums = (sums_ref[...] + core_ref[...]) + (across_ref[...] + both_ref[...])
    out_sums_ref[...] = sums
    far_ref[count:] = spread(sums)
    for side, ref in ((0, near_ref), (1, far_ref)):
        for k in range(pieces):
            total = keep_ref[side, k].astype(wide) + more_ref[side, k].astype(wide)
            total = total.reshape(-1, size).astype(low)
            ref[k * height : k * height + total.shape[0]] = total
            rest = output_ref[2 * k + side] + more_output_ref[2 * k + side].astype(wide)
            ref[k * height + total.shape[0] : (k + 1) * height] = rest.astype(low)


def quarters_kernel(near_ref, more_ref, sums_ref, own_ref, out_sums_ref, *out_refs):
    rows = own_ref.shape[0]
    sums = sums_ref[...] + gathered(more_ref[near_ref.shape[0] :])
    out_sums_ref[...] = sums
    packed = spread(sums)
    for n, ref in enumerate((own_ref, *out_refs)):
        block = slice(n * rows, (n + 1) * rows)
        total = near_ref[block].astype(wide) + more_ref[block].astype(wide)
        ref[:rows] = total.astype(ref.dtype)
        if n:
            ref[rows:] = packed


def total_kernel(own_ref, sums_ref, *refs):
    aways, (in_ref, out_ref), sums_refs = refs[:-6], refs[-6:-4], refs[-4:]
    rows = out_ref.shape[0]
    sums = [sums_ref[...]]
    total = own_ref[...]
    for ref in aways:
        total = total + ref[: own_ref.shape[0]].astype(wide)
        sums.append(gathered(ref[own_ref.shape[0] :]))
    while len(sums) > 1:
        sums = [x + y for x, y in zip(sums[0::2], sums[1::2])]
    for n, ref in enumerate(sums_refs):
        ref[...] = sums[0][n : n + 1].reshape(ref.shape)
    for n in range(3):
        in_ref[n] = total[n * rows : (n + 1) * rows]
    out_ref[...] = total[3 * rows :]


def input_grad_kernel(grad_ref, own_ref, more_ref, input_ref, scale_ref, out_ref):
    hat, inverse = normalize(input_ref[...].astype(wide))
    upstream = own_ref[...] + more_ref[...].astype(wide)
    out_ref[...] = grad_ref[...] + norm_back(upstream, hat, inverse, scale_ref[0:1])


def across(values):
    return lax.ppermute(values, "tp", [(0, 1), (1, 0)])


def swapped(values, offset):
    if offset == 0:
        return values
    count = lax.axis_size("fsdp")
    return lax.ppermute(values, "fsdp", [(i, i ^ offset) for i in range(count)])


def reduce_blocks(blocks, index, count):
    bit = 0
    part = blocks
    while count > 1:
        mine = (index >> bit) & 1
        split = part.reshape(count // 2, 2, *blocks.shape[1:])
        keep = lax.dynamic_index_in_dim(split, mine, 1, keepdims=False)
        give = lax.dynamic_index_in_dim(split, 1 - mine, 1, keepdims=False)
        got = swapped(give.astype(low), 1 << bit)
        part = keep.astype(wide) + got.astype(wide)
        if count > 2:
            part = part.astype(low)
        count //= 2
        bit += 1
    return part[0]


def tree_masks(lengths, parents, tree_size):
    segment_count = lengths.shape[0]
    number = jnp.arange(segment_count, dtype=jnp.int32)
    segment_end = jnp.sum(jnp.where(number[None, :] <= number[:, None], lengths[None, :], 0), axis=1)
    starts = segment_end - lengths
    position = jnp.arange(tree_size, dtype=jnp.int32)
    member = (
        (position[:, None] >= starts[None, :]) & (position[:, None] < segment_end[None, :])
    ).astype(wide)
    closure = jnp.maximum(
        jnp.eye(segment_count, dtype=wide), (parents[:, None] == number[None, :]).astype(wide)
    )
    steps = 1
    while steps < segment_count:
        closure = jnp.minimum(jnp.dot(closure, closure), 1.0)
        steps *= 2
    unreached = (1.0 - jnp.dot(member, closure)) * masked_score
    padding = ((0, 0), (0, LANES - segment_count))
    return jnp.pad(unreached, padding).astype(low), jnp.pad(member, padding).astype(low)


def shards(
    inputs,
    token_ids,
    hash_table,
    segment_lengths,
    segment_parents,
    first_gain,
    first_bias,
    input_weight,
    output_weight,
    second_gain,
    second_bias,
    expert_in,
    expert_out,
    cotangent,
):
    own_count, width = inputs.shape
    experts_in_all = lax.axis_size("fsdp")
    tree_size = token_ids.shape[0]
    capacity = 2 * own_count // experts_in_all
    local_width = input_weight.shape[2]
    chips = experts_in_all // 2
    shard_rows = input_weight.shape[1]
    hidden = expert_in.shape[2]
    index = lax.axis_index("fsdp")
    side = lax.axis_index("tp")
    place = jnp.stack([index, side]).astype(jnp.int32)
    in_kernel = shard_rows % 16 == 0
    scales = [first_gain, first_bias, second_gain, second_bias]

    other_inputs = across(inputs)
    shard = jnp.concatenate([input_weight, output_weight.T[None]])
    pieces = {0: shard}
    for k in range(2, chips, 2):
        pieces[k] = swapped(shard, 2 * k)
    for k in range(1, chips, 2):
        pieces[k] = swapped(pieces[k - 1], 2)
    mine = jnp.stack([pieces[k] for k in range(chips)])
    sibling = swapped(mine, 1)

    own_ids = lax.dynamic_slice_in_dim(token_ids, side * own_count, own_count, 0)
    table = hash_table.reshape(-1, LANES).astype(low)
    row_hot = (own_ids[:, None] // LANES == jnp.arange(table.shape[0])[None, :]).astype(low)
    lane_hot = own_ids[:, None] % LANES == jnp.arange(LANES)[None, :]
    experts = jnp.sum(jnp.where(lane_hot, dot(row_hot, table), 0.0), axis=1).astype(jnp.int32)
    hot = (experts[:, None] == jnp.arange(experts_in_all)[None, :]).astype(low)
    earlier = (jnp.arange(own_count)[:, None] > jnp.arange(own_count)[None, :]).astype(low)
    rank = jnp.sum(dot(earlier, hot) * hot.astype(wide), axis=1).astype(jnp.int32)
    own_slot = experts * capacity + rank
    sibling_slot = swapped(own_slot, 1)

    def chip_slot(slot):
        offset = (slot // capacity) ^ index
        return jnp.where(offset & 1 == 0, (offset >> 1) * capacity + slot % capacity, -1)

    own_place, sibling_place = chip_slot(own_slot), chip_slot(sibling_slot)

    slot_count = experts_in_all * capacity
    packed_grads = run(
        straight_pack_kernel,
        (cotangent, own_slot[None]),
        kept((slot_count, width), low),
        flops=2 * slot_count * own_count * width,
        first=(mine, other_inputs),
    )
    slot_grads = lax.all_to_all(
        packed_grads.reshape(experts_in_all, capacity, width), "fsdp", 0, 0, tiled=True
    )
    more_slot_grads = across(slot_grads)

    if in_kernel:
        weights = (mine, sibling)
    else:
        both = jnp.stack([mine, sibling], 1)
        both = both.reshape(experts_in_all, 4, shard_rows, local_width)
        full = jnp.concatenate(
            [lax.dynamic_index_in_dim(both, index ^ n, 0, False) for n in range(experts_in_all)], axis=1
        )
        weights = (full, full[:1, :16])
    full_weight, out_weight, projected, scales = run(
        functools.partial(project_kernel, chips if in_kernel else 0),
        (place, inputs, other_inputs, *scales, *weights),
        [
            kept((3, width, local_width), low),
            array((width, local_width), low),
            kept((tree_size, 3 * local_width), low),
            array((4, width), wide),
        ],
        flops=2 * tree_size * width * 3 * local_width,
    )
    other_out_weight = across(out_weight)
    unreached, member = tree_masks(segment_lengths[0], segment_parents[0], tree_size)
    attended, totals, attended_keep, attended_give = attend(place, projected, unreached, member)
    attended_more = across(attended_give)
    middle, second_normed = run(
        branch_kernel,
        (attended_keep, attended_more, out_weight, other_out_weight, inputs, scales),
        [kept((own_count, width), wide), array((own_count, width), low)],
        flops=2 * own_count * width * width,
    )

    sibling_normed = swapped(second_normed, 1)
    piece = array((2, capacity, width), low)
    packed = run(
        pack_kernel,
        (second_normed, sibling_normed, own_place[None], sibling_place[None]),
        [piece] * chips,
        first=(slot_grads,),
        flops=4 * own_count * own_count * width,
    )
    quarter = chips // 4
    near, next_near, far, next_far = [(n * quarter, (n + 1) * quarter) for n in range(4)]
    arrived = {}
    for span in (far, near, next_near):
        for k in range(*span):
            arrived[k] = swapped(packed[k], 2 * k)
    for k in range(*next_far):
        arrived[k] = swapped(packed[k], 2 * k)
    spans = (near, far, next_far, next_near)
    more_arrived = {k: across(arrived[k]) for span in spans for k in range(*span)}

    turned, turned_done = run(
        turned_kernel,
        (place, Far(inputs), Far(other_inputs), scales),
        kept((width, tree_size), low),
        mark=True,
        first=(packed[0],),
    )

    weight_in, weight_out = expert_in[0], expert_out[0]
    buffers = None
    returned = {}
    sent = []
    done = []
    back = []
    for turn, span in enumerate(spans):
        own_pieces = [arrived[k] for k in range(*span)]
        buffers, keep, give = expert_group(
            place, weight_in, weight_out, slot_grads, more_slot_grads,
            own_pieces, [more_arrived[k] for k in range(*span)], buffers, span, chips,
            [turned_done] + [arrived[k] for k in range(1, chips)] if turn == 0 else [],
        )
        sent.append((span, keep, across(give)))
    slot_rows, grad_rows, actives, grad_pres, ffn_keep, ffn_give = buffers
    rows = 4 * capacity
    for turn, (span, keep, more) in enumerate(sent):
        if turn == 2:
            *sums, ffn_give, token = run(
                last_pieces_kernel,
                (keep, more, Far(ffn_give)),
                [piece] * quarter + [array(ffn_give.shape, low)],
                mark=True,
            )
        else:
            *sums, token = run(pieces_kernel, (keep, more), [piece] * quarter, mark=True)
        done.append(token)
        for k in range(*span):
            returned[k] = swapped(sums[k - span[0]], 2 * k)
        back.append([returned[k] for k in range(*span)])
    ffn_done = done[2]
    ffn_more = across(ffn_give)
    tile = min(512, hidden)
    stripe = pl.BlockSpec((chips, rows, tile), lambda i: (0, 0, i))
    fixed = pl.BlockSpec((chips, rows, width), lambda i: (0, 0, 0))
    expert_out_grad, out_done = run(
        product_kernel,
        (in_hbm(actives), in_hbm(grad_rows)),
        array((hidden, width), wide),
        flops=2 * chips * rows * width * hidden,
        first=(ffn_done, done[3], *back[1]),
        mark=True,
        grid=(hidden // tile,),
        in_specs=[stripe, fixed],
        out_specs=[pl.BlockSpec((tile, width), lambda i: (i, 0))],
    )
    own_part, sibling_part = run(
        unpack_kernel,
        (own_place[None], sibling_place[None], *[returned[k] for k in range(chips)]),
        [array((own_count, width), low)] * 2,
        first=(out_done, *back[2]),
        flops=4 * own_count * own_count * width,
    )
    sibling_part = swapped(sibling_part, 1)
    if in_kernel:
        blocks = (2, chips, shard_rows, local_width)
        output_outs = [array(blocks, wide), array(blocks, low)]
    else:
        output_outs = [array((width, local_width), wide), array((width, local_width), low)]
    grad_middle, grad_mine, grad_give, second_sums, output_own, output_give, middle_done = run(
        functools.partial(middle_back_kernel, chips if in_kernel else 0),
        (
            place, own_part, sibling_part, Far(middle), Far(cotangent), scales,
            Far(out_weight), Far(other_out_weight), Far(attended_keep), Far(attended_more),
        ),
        [
            kept((own_count, width), wide),
            array((own_count, local_width), low),
            array((own_count, local_width), low),
            array((2, width), wide),
            *output_outs,
        ],
        first=(ffn_more,),
        mark=True,
        scratch_shapes=[pltpu.VMEM((2, width, local_width), wide)],
        flops=4 * own_count * width * width,
    )
    grad_more = across(grad_give)
    ffn_sums, sums_done = run(
        ffn_sum_kernel,
        (place, Far(ffn_keep), ffn_more),
        kept((experts_in_all, capacity, width), low),
        mark=True,
        first=(middle_done,),
    )
    ffn_back = lax.all_to_all(ffn_sums, "fsdp", 0, 0, tiled=True)

    if in_kernel:
        output_own, output_give, output_done = run(
            output_sum_kernel,
            (output_own, swapped(output_give, 1)),
            [array(blocks[1:], wide), array(blocks[1:], low)],
            mark=True,
        )
    else:
        output_done = middle_done
    output_more = across(output_give)
    grad_projected, part_keep, part_give, norm_sums = attend_back(
        place, projected, unreached, member, attended, totals, grad_mine, grad_more,
        turned, full_weight, scales, second_sums,
        chips if in_kernel else 0, first=(sums_done, output_done),
    )

    if in_kernel:
        part_more = swapped(part_give, 1)
        rows = 4 * shard_rows
        near_sum, far_sum, norm_sums, half_done = run(
            halves_kernel,
            (
                part_keep, part_more, output_own, output_more,
                norm_sums, swapped(norm_sums, 1), across(norm_sums),
                lax.ppermute(norm_sums, ("fsdp", "tp"), [(i, i ^ 3) for i in range(2 * experts_in_all)]),
            ),
            [
                kept((chips // 2 * rows, local_width), low),
                kept((chips // 2 * rows + 32, local_width), low),
                array((4, width), wide),
            ],
            mark=True,
        )
    else:
        half_done = norm_sums
    first_give, first_own, give_done = run(
        first_kernel,
        (place, Far(grad_projected), Far(full_weight)),
        [array((own_count, width), low), array((own_count, width), wide)],
        mark=True,
        first=(half_done,),
        light=True,
        flops=2 * tree_size * width * 3 * local_width,
    )
    first_more = across(first_give)
    expert_in_grad, in_done = run(
        product_kernel,
        (in_hbm(slot_rows), in_hbm(grad_pres)),
        array((width, hidden), wide),
        flops=2 * chips * capacity * 4 * width * hidden,
        first=(give_done,),
        mark=True,
        light=True,
        grid=(hidden // tile,),
        in_specs=[fixed, stripe],
        out_specs=[pl.BlockSpec((width, tile), lambda i: (0, i))],
    )
    if in_kernel:
        own_sum, norm_sums, *away = run(
            quarters_kernel,
            (Far(near_sum), Far(swapped(far_sum, 2)), norm_sums),
            [array((rows, local_width), wide), array((4, width), wide)]
            + [array((rows + 32, local_width), low)] * (chips // 2 - 1),
            first=(in_done, ffn_back),
        )
        away = [swapped(away[k - 1], 4 * k) for k in range(1, chips // 2)]
    else:
        output_part = (output_own + output_more.astype(wide)).astype(low)
        blocks = jnp.concatenate([part_keep, output_part[None]])
        blocks = blocks.reshape(4, experts_in_all, shard_rows, local_width).transpose(1, 0, 2, 3)
        summed = reduce_blocks(blocks, index, experts_in_all)
        bit = 1
        while bit < experts_in_all:
            norm_sums = norm_sums + swapped(norm_sums, bit)
            bit *= 2
        norm_sums = norm_sums + across(norm_sums)
    input_grad, input_done = run(
        input_grad_kernel,
        (Far(grad_middle), first_own, first_more, Far(inputs), scales),
        array((own_count, width), wide),
        mark=True,
        light=True,
    )
    out_block, out_done = run(
        out_kernel,
        (own_slot[None], ffn_back.reshape(slot_count, width), Far(middle)),
        array((own_count, width), low),
        mark=True,
        light=True,
        flops=2 * own_count * slot_count * width,
    )
    if in_kernel:
        input_weight_grad, output_weight_grad, *norm_sums = run(
            total_kernel,
            (own_sum, norm_sums, *away),
            [
                array((3, shard_rows, local_width), wide),
                array((shard_rows, local_width), wide),
                *[array((width,), wide)] * 4,
            ],
            first=(input_done, out_done),
        )
    else:
        input_weight_grad, output_weight_grad = summed[:3], summed[3]
    output_weight_grad = output_weight_grad.T
    return (
        out_block,
        input_grad,
        norm_sums[0],
        norm_sums[1],
        input_weight_grad,
        output_weight_grad,
        norm_sums[2],
        norm_sums[3],
        expert_in_grad[None],
        expert_out_grad[None],
    )


def solution(mesh):
    return jax.shard_map(
        shards,
        mesh=mesh,
        in_specs=(
            P(("fsdp", "tp"), None),
            P("fsdp"),
            P(),
            P("fsdp", None),
            P("fsdp", None),
            P(),
            P(),
            P(None, "fsdp", "tp"),
            P("tp", "fsdp"),
            P(),
            P(),
            P("fsdp", None, "tp"),
            P("fsdp", "tp", None),
            P(("fsdp", "tp"), None),
        ),
        out_specs=(
            P(("fsdp", "tp"), None),
            P(("fsdp", "tp"), None),
            P(),
            P(),
            P(None, "fsdp", "tp"),
            P("tp", "fsdp"),
            P(),
            P(),
            P("fsdp", None, "tp"),
            P("fsdp", "tp", None),
        ),
        check_vma=False,
    )
```
